32 devices in a mesh: expert: 8 (over z, y), tensor: 4 (over x, core).
Axes of the slice: x: 2, y: 2, z: 4, core: 2. Of those that a mesh axis runs over, the one named last changes fastest.
Arguments:
- tokens: bfloat16 [256, 1536], P('expert')
- attn_gain: bfloat16 [1536], replicated, may hold values from 0.099609375 to 1.8984375
- query_weight: bfloat16 [1536, 1536], P(None, 'tensor'), may hold values from -0.15625 to 0.15625
- key_value_weight: bfloat16 [4, 1536, 128], P('tensor'), may hold values from -0.15625 to 0.15625
- paired_cache: bfloat16 [8, 4, 768, 128], P('expert', 'tensor')
- prompt_length: int32 [8, 3], P('expert'), may hold values from 1 to 256, 640 in all within a row
- group_index: int32 [256], P('expert'), may hold values from 0 to 2
- offsets: int32 [256], P('expert'), may hold values from 0 to 127
- sink_logit: float32 [12], P('tensor'), may hold values from -2 to 4
- out_weight: bfloat16 [1536, 1536], P('tensor'), may hold values from -0.15625 to 0.15625
- mixer_gain: bfloat16 [1536], replicated, may hold values from 0.099609375 to 1.8984375
- routes: int32 [256, 4], P('expert'), may hold values from 0 to 31, all different within a row; in each aligned block of 32 rows (0 to 31, 32 to 63, ...) at most 8 rows name the same one
- route_weight: float32 [256, 4], P('expert'), may hold values from 0.05 to 1
- copy_slot: int32 [32], replicated, may hold values from 0 to 31, as said below
- gate_weight: bfloat16 [32, 1536, 768], P('expert', None, 'tensor'), as said below
- up_weight: bfloat16 [32, 1536, 768], P('expert', None, 'tensor'), as said below
- down_weight: bfloat16 [32, 768, 1536], P('expert', 'tensor'), as said below
- final_gain: bfloat16 [1536], P('tensor'), may hold values from 0.099609375 to 1.8984375
Outputs:
- normed: bfloat16 [256, 1536], P('expert', 'tensor')
The draws below stay inside these ranges and needn't reach their ends.
Inputs may be any that keep to these rules, and one draw needn't show every extreme that they name: `routes`: in each aligned block of 32 rows no expert is named by more than 8 rows, and in some block one is named by exactly 8. `copy_slot`: a permutation: every slot appears once; slot s lies on expert-axis index s // 4 as its local copy s % 4. `prompt_length`: on every expert-axis index one prompt fills all 256 slots. `gate_weight`: all 1 replicas of an expert hold equal weights. `up_weight`: all 1 replicas of an expert hold equal weights. `down_weight`: all 1 replicas of an expert hold equal weights.
All inputs are finite; a program needn't handle non-finite values.
Results may differ from the reference program's by a relative error of at most 0.013.
Values may be sent and summed in bfloat16 or wider, within the bound.
No kernel may reach another device: no remote copies, remote signals or barrier semaphores. Data moves between devices by JAX's collectives and lax.ppermute only.
A program may use at most 64 MiB of HBM per device.

```python
import math
import jax
import jax.numpy as jnp
import numpy as np
from jax import lax

MODEL_WIDTH = 1536
QUERY_HEADS = 12
KEY_VALUE_HEADS = 2
HEAD_SIZE = 128
EXPERTS = 32
FF = 768
TOP = 4
TOK_DEV = 32
PROMPTS_DEV = 3
PROMPT_CAP = 256
GEN = 128
WINDOW = 192
TOKENS = 256
CACHE_PER_SLICE = 768
COPIES = 32
REPL = 1
MOST = 8
N_EXPERT = 8
N_TENSOR = 4


def draw_tokens(key, part):
    first_key, second_key = jax.random.split(key)
    columns = 10.0 ** (jnp.arange(MODEL_WIDTH, dtype=jnp.float32) / MODEL_WIDTH)
    row_scale = 10.0 ** jax.random.uniform(second_key, (TOKENS, 1), jnp.float32)
    drawn_draw = jax.random.normal(first_key, (TOKENS, MODEL_WIDTH), jnp.float32)
    return (drawn_draw * columns[None, :] * row_scale / 8.0).astype(jnp.bfloat16)


def draw_paired_cache(key, part):
    first_key = jax.random.fold_in(key, 0)
    cache_layout = (N_EXPERT, 2 * KEY_VALUE_HEADS, CACHE_PER_SLICE, HEAD_SIZE)
    return jax.random.normal(first_key, cache_layout, jnp.float32).astype(jnp.bfloat16)


def slot_order(key):
    return jax.random.permutation(jax.random.fold_in(key, 7), COPIES).astype(jnp.int32)


def expert_of_slot(key):
    return (jnp.argsort(slot_order(key)) // REPL).astype(jnp.int32)


def draw_copy_slot(key, part):
    return slot_order(key)


def draw_gate_weight(key, part):
    drawn_draw = jax.random.normal(jax.random.fold_in(key, 11), (EXPERTS, MODEL_WIDTH, FF), jnp.float32) * MODEL_WIDTH ** (-0.5)
    return drawn_draw[expert_of_slot(key)].astype(jnp.bfloat16)


def draw_up_weight(key, part):
    drawn_draw = jax.random.normal(jax.random.fold_in(key, 13), (EXPERTS, MODEL_WIDTH, FF), jnp.float32) * MODEL_WIDTH ** (-0.5)
    return drawn_draw[expert_of_slot(key)].astype(jnp.bfloat16)


def draw_down_weight(key, part):
    drawn_draw = jax.random.normal(jax.random.fold_in(key, 17), (EXPERTS, FF, MODEL_WIDTH), jnp.float32) * FF ** (-0.5)
    return drawn_draw[expert_of_slot(key)].astype(jnp.bfloat16)


def set_ends(values, own_key, smallest, largest):
    shape = values.shape
    spot = [jax.random.randint(jax.random.fold_in(own_key, axis), (), 0, shape[axis]) for axis in range(len(shape))]
    values = values.at[tuple(spot)].set(smallest)
    longest = shape.index(max(shape))
    spot[longest] = (spot[longest] + 1) % shape[longest]
    return values.at[tuple(spot)].set(largest)


def levels(own_key, shape, cuts, least, largest):
    factor_of = 1.0
    for axis_at, blocks in cuts:
        draws = jax.random.uniform(jax.random.fold_in(jax.random.fold_in(own_key, 6), axis_at), (blocks,), jnp.float32, least / len(cuts), largest / len(cuts))
        factor_of = factor_of * jnp.repeat(jnp.exp(draws), shape[axis_at] // blocks).reshape((-1,) + (1,) * (len(shape) - 1 - axis_at))
    return factor_of


def profile(amount, total, limit, lean):
    loads = [(1 << 20) // math.isqrt(grade ** lean) + 1 for grade in range(2, amount + 1)]
    surplus, counts = total - limit - (amount - 1), [1] * (amount - 1)
    while surplus > 0:
        free = [i for i in range(amount - 1) if counts[i] < limit]
        whole, left = sum([loads[i] for i in free]), surplus
        for i in free:
            more = min(limit - counts[i], max(1, left * loads[i] // whole), surplus)
            counts[i] = counts[i] + more
            surplus = surplus - more
    return np.array([limit] + counts)


def ragged_sizes(stream_key, number_of, total, limit, skew):
    if number_of == 2:
        one = jax.random.randint(stream_key, (), max(1, total - limit), min(limit, total - 1) + 1)
        return jnp.stack([one, total - one])
    sizes = jnp.asarray(profile(number_of, total, limit, skew), jnp.int32)
    couples = (number_of - 1) // 2
    giver, sink = sizes[1:1 + 2 * couples:2], sizes[2:2 + 2 * couples:2]
    slack = jnp.minimum(giver - 1, limit - sink)
    shifted = jax.random.randint(jax.random.fold_in(stream_key, 1), (couples,), 0, 1 << 20) % (slack + 1)
    sizes = sizes.at[1:1 + 2 * couples:2].set(giver - shifted).at[2:2 + 2 * couples:2].set(sink + shifted)
    return sizes[jax.random.permutation(jax.random.fold_in(stream_key, 2), number_of)]


def routed_block(stream_key, own, number, rows, count, top, most, slope):
    order = jax.random.permutation(stream_key, count)
    packed, common = load_shares(count, rows * top, most, slope, True), load_shares(count, rows * top, most, slope, False)
    places = jnp.arange(count)

    def named(sizes, turn):
        used = int((sizes > 0).sum())
        fixed = max(1, used // 4)
        shifted = fixed + (places - fixed + turn * (used - fixed)) % max(1, count - fixed)
        return jnp.zeros((count,), jnp.int32).at[order[jnp.where(places < fixed, places, shifted)]].set(jnp.asarray(sizes, jnp.int32))

    sizes = jnp.where(number % 4 == 0, named(packed, number // 4), named(common, number - number // 4 - 1))
    mixed = jax.random.permutation(jax.random.fold_in(own, 3), count)
    giver, receiver = mixed[0:count // 2 * 2:2], mixed[1:count // 2 * 2:2]
    margin = jnp.minimum(sizes[giver] - 1, most - sizes[receiver]) // 2
    margin = jnp.where((giver == order[0]) | (receiver == order[0]) | (sizes[receiver] == 0), 0, jnp.maximum(margin, 0))
    shifted = jax.random.randint(jax.random.fold_in(own, 4), (count // 2,), 0, 1 << 20) % (margin + 1)
    sizes = sizes.at[giver].add(-shifted).at[receiver].add(shifted)
    items = jnp.searchsorted(jnp.cumsum(sizes), jnp.arange(rows * top), side="right").astype(jnp.int32)
    table = items.reshape(top, rows).T
    table = table[jax.random.permutation(jax.random.fold_in(own, 1), rows)]
    turn = jax.random.randint(jax.random.fold_in(own, 2), (rows, 1), 0, top)
    return jnp.take_along_axis(table, (jnp.arange(top)[None, :] + turn) % top, axis=1)


def load_shares(amount, total, limit, skew, full):
    weights = [(1 << 20) // math.isqrt(grade ** skew) + 1 for grade in range(1, amount + 1)]
    largest = limit if full else min(limit, max(-(-total // amount), total * weights[0] // sum(weights)))
    least = 1 if total - largest >= amount - 1 else 0
    holding, spare = [largest] + [least] * (amount - 1), total - largest - least * (amount - 1)
    while spare > 0:
        candidates = [i for i in range(1, amount) if holding[i] < largest] or [i for i in range(1, amount) if holding[i] < limit]
        whole, remaining = sum([weights[i] for i in candidates]), spare
        for i in candidates:
            extra = min(limit - holding[i], max(1, remaining * weights[i] // whole), spare)
            holding[i] = holding[i] + extra
            spare = spare - extra
    return np.array(holding)


def normal_values(own_key, extent, scale, bound, cuts=(), kind=jnp.bfloat16):
    level = levels(own_key, extent, cuts, -0.22, 0.18) if cuts else 1.0
    result = jax.random.normal(own_key, extent, jnp.float32) * scale * level
    return jnp.minimum(jnp.maximum(result, -bound), bound).astype(kind)


def setup_inputs(seed: int = 0) -> dict:
    arg_keys = jax.random.split(jax.random.key(seed), 19)
    tokens = draw_tokens(jax.random.fold_in(arg_keys[18], 71), 0)
    attn_gain = jnp.clip(1.0 + 0.18 * jax.random.normal(arg_keys[1], (MODEL_WIDTH,), jnp.float32), 0.099609375, 1.8984375).astype(jnp.bfloat16)
    query_weight = normal_values(arg_keys[2], (MODEL_WIDTH, QUERY_HEADS * HEAD_SIZE), MODEL_WIDTH ** -0.5, 0.15625, ((1, 4),))
    key_value_weight = normal_values(arg_keys[3], (2 * KEY_VALUE_HEADS, MODEL_WIDTH, HEAD_SIZE), MODEL_WIDTH ** -0.5, 0.15625, ((0, 4),))
    paired_cache = draw_paired_cache(jax.random.fold_in(arg_keys[18], 71), 0)
    prompt_length = jax.vmap(lambda own: ragged_sizes(own, PROMPTS_DEV, PROMPTS_DEV * PROMPT_CAP * 5 // 6, PROMPT_CAP, 1))(jax.random.split(arg_keys[5], N_EXPERT)).reshape((N_EXPERT, PROMPTS_DEV)).astype(jnp.int32)
    group_index = set_ends(jax.random.randint(arg_keys[6], (TOKENS,), 0, PROMPTS_DEV), jax.random.fold_in(arg_keys[6], 1), 0, PROMPTS_DEV - 1).astype(jnp.int32)
    offsets = set_ends(jax.random.randint(arg_keys[7], (TOKENS,), 0, GEN), jax.random.fold_in(arg_keys[7], 1), 0, GEN - 1).astype(jnp.int32)
    sink_logit = jnp.clip(-2.0 + 6.0 * jax.random.uniform(arg_keys[8], (QUERY_HEADS,), jnp.float32) ** levels(arg_keys[8], (QUERY_HEADS,), ((0, 4),), -0.2, 0.2), -2.0, 4.0)
    out_weight = normal_values(arg_keys[9], (QUERY_HEADS * HEAD_SIZE, MODEL_WIDTH), (QUERY_HEADS * HEAD_SIZE) ** -0.5, 0.15625, ((0, 4),))
    mixer_gain = jnp.clip(1.0 + 0.18 * jax.random.normal(arg_keys[10], (MODEL_WIDTH,), jnp.float32), 0.099609375, 1.8984375).astype(jnp.bfloat16)
    routes_keys = jax.random.split(jax.random.fold_in(arg_keys[11], 1), TOKENS // (TOK_DEV // REPL))
    routes_turns = jax.random.permutation(jax.random.fold_in(arg_keys[11], 3), TOKENS // (TOK_DEV // REPL))
    routes = jax.vmap(lambda own, number: routed_block(jax.random.fold_in(arg_keys[11], 2), own, number, TOK_DEV // REPL, EXPERTS, TOP, MOST, 2))(routes_keys, routes_turns).reshape((TOKENS, TOP))
    route_weight = jnp.clip(jnp.exp(math.log(1.0) - 2.9957323 * jax.random.uniform(arg_keys[12], (TOKENS, TOP), jnp.float32) ** levels(arg_keys[12], (TOKENS, TOP), ((0, 8),), -0.2, 0.2)), 0.05, 1.0)
    copy_slot = draw_copy_slot(jax.random.fold_in(arg_keys[18], 71), 0)
    gate_weight = draw_gate_weight(jax.random.fold_in(arg_keys[18], 71), 0)
    up_weight = draw_up_weight(jax.random.fold_in(arg_keys[18], 71), 0)
    down_weight = draw_down_weight(jax.random.fold_in(arg_keys[18], 71), 0)
    final_gain = jnp.clip(1.0 + 0.18 * jax.random.normal(arg_keys[17], (MODEL_WIDTH,), jnp.float32), 0.099609375, 1.8984375).astype(jnp.bfloat16)
    return {"tokens": tokens, "attn_gain": attn_gain, "query_weight": query_weight, "key_value_weight": key_value_weight, "paired_cache": paired_cache, "prompt_length": prompt_length, "group_index": group_index, "offsets": offsets, "sink_logit": sink_logit, "out_weight": out_weight, "mixer_gain": mixer_gain, "routes": routes, "route_weight": route_weight, "copy_slot": copy_slot, "gate_weight": gate_weight, "up_weight": up_weight, "down_weight": down_weight, "final_gain": final_gain}


EPSILON = 1e-06

def rms_scale(values, gain_row):
    mean_square = lax.optimization_barrier(jnp.mean(values * values, axis=-1, keepdims=True))
    return values * lax.rsqrt(mean_square + EPSILON) * gain_row.astype(jnp.float32)

def rotate(values, position):
    half_dim = values.shape[-1] // 2
    frequency = 10000.0 ** (-jnp.arange(half_dim, dtype=jnp.float32) / half_dim)
    angles = position.astype(jnp.float32)[:, None] * frequency[None, :]
    if values.ndim == 3:
        angles = angles[:, None, :]
    cosine_part = jnp.cos(angles)
    sine_part = jnp.sin(angles)
    front_half = values[..., :half_dim]
    back_half = values[..., half_dim:]
    return jnp.concatenate([front_half * cosine_part - back_half * sine_part, front_half * sine_part + back_half * cosine_part], axis=-1)

def slot_places(routes, copy_slot, replicas):
    row_count = routes.shape[0]
    flat_routes = routes.reshape(-1)
    slot_count = flat_routes.shape[0]
    block_of = jnp.arange(slot_count, dtype=jnp.int32) // TOP // (row_count // replicas)
    onehot = (flat_routes[:, None] == jnp.arange(EXPERTS, dtype=jnp.int32)[None, :]).astype(jnp.int32)
    grouped = onehot.reshape(replicas, slot_count // replicas, EXPERTS)
    earlier = jnp.cumsum(grouped, axis=1) - grouped
    slot_rank = lax.optimization_barrier(jnp.sum(earlier * grouped, axis=-1)).reshape(slot_count)
    holder = copy_slot[flat_routes * replicas + block_of]
    return (holder, slot_rank)

def reference(tokens, attn_gain, query_weight, key_value_weight, paired_cache, prompt_length, group_index, offsets, sink_logit, out_weight, mixer_gain, routes, route_weight, copy_slot, gate_weight, up_weight, down_weight, final_gain):
    score_scale = 1.0 / HEAD_SIZE ** 0.5
    group_width = QUERY_HEADS // KEY_VALUE_HEADS

    def attend(inputs):
        rows_in, cache_block, lengths, groups, offset_rows = inputs
        normed_in = rms_scale(rows_in.astype(jnp.float32), attn_gain).astype(jnp.bfloat16)
        row_length = lengths[groups]
        position = row_length + offset_rows
        queries = jnp.dot(normed_in, query_weight, preferred_element_type=jnp.float32).reshape(-1, QUERY_HEADS, HEAD_SIZE)
        queries = rotate(queries, position).astype(jnp.bfloat16)
        projected = jnp.einsum('td,kde->tke', normed_in.astype(jnp.float32), key_value_weight.astype(jnp.float32))
        new_keys = rotate(projected[:, 0::2], position).astype(jnp.bfloat16)
        new_values = projected[:, 1::2].astype(jnp.bfloat16)
        new_keys = jnp.repeat(new_keys, group_width, axis=1)
        new_values = jnp.repeat(new_values, group_width, axis=1)
        cache_keys = jnp.repeat(cache_block[0::2], group_width, axis=0)
        cache_values = jnp.repeat(cache_block[1::2], group_width, axis=0)
        scores = jnp.einsum('thd,hcd->thc', queries.astype(jnp.float32), cache_keys.astype(jnp.float32)) * score_scale
        self_score = lax.optimization_barrier(jnp.sum(queries.astype(jnp.float32) * new_keys.astype(jnp.float32), axis=-1)) * score_scale
        slot_index = jnp.arange(CACHE_PER_SLICE, dtype=jnp.int32)
        slot_group = slot_index // PROMPT_CAP
        slot_pos = slot_index % PROMPT_CAP
        visible = (slot_group[None, :] == groups[:, None]) & (slot_pos[None, :] < row_length[:, None]) & (slot_pos[None, :] > position[:, None] - WINDOW)
        visible = visible[:, None, :]
        masked = jnp.where(visible, scores, -jnp.inf)
        ceiling = jnp.maximum(jnp.maximum(lax.optimization_barrier(jnp.max(masked, axis=-1)), self_score), sink_logit[None, :])
        weights = jnp.where(visible, jnp.exp(scores - ceiling[..., None]), 0.0)
        own_weight = jnp.exp(self_score - ceiling)
        denominator = lax.optimization_barrier(jnp.sum(weights, axis=-1)) + own_weight + jnp.exp(sink_logit[None, :] - ceiling)
        probabilities = (weights / denominator[..., None]).astype(jnp.bfloat16)
        own_prob = (own_weight / denominator).astype(jnp.bfloat16)
        context = jnp.einsum('thc,hcd->thd', probabilities.astype(jnp.float32), cache_values.astype(jnp.float32))
        context = context + own_prob.astype(jnp.float32)[..., None] * new_values.astype(jnp.float32)
        context = context.astype(jnp.bfloat16).reshape(-1, QUERY_HEADS * HEAD_SIZE)
        attended = jnp.dot(context, out_weight, preferred_element_type=jnp.float32)
        return (rows_in.astype(jnp.float32) + attended).astype(jnp.bfloat16)
    residual = lax.map(attend, (tokens.reshape(N_EXPERT, TOK_DEV, MODEL_WIDTH), paired_cache, prompt_length, group_index.reshape(N_EXPERT, TOK_DEV), offsets.reshape(N_EXPERT, TOK_DEV)))
    residual = residual.reshape(TOKENS, MODEL_WIDTH)
    mixed_in = rms_scale(residual.astype(jnp.float32), mixer_gain).astype(jnp.bfloat16)
    replicas = COPIES // EXPERTS

    def place_device(device_routes):
        return slot_places(device_routes, copy_slot, replicas)
    holders, slot_ranks = jax.vmap(place_device)(routes.reshape(N_EXPERT, TOK_DEV, TOP))
    copy_rows = N_EXPERT * MOST
    source = jnp.arange(N_EXPERT, dtype=jnp.int32)[:, None]
    places = (holders * copy_rows + source * MOST + slot_ranks).reshape(-1)
    slot_ids = jnp.arange(TOKENS * TOP, dtype=jnp.int32)
    slot_table = jnp.zeros((COPIES * copy_rows,), jnp.int32).at[places].set(slot_ids).reshape(COPIES, copy_rows)
    block_units = FF // N_TENSOR

    def expert_rows(inputs):
        slot_picks, gate_part, up_part, down_part = inputs
        gathered = mixed_in[slot_picks // TOP]
        gate_val = jnp.dot(gathered, gate_part, preferred_element_type=jnp.float32)
        up_val = jnp.dot(gathered, up_part, preferred_element_type=jnp.float32)
        hidden = (jnp.maximum(gate_val, 0.0) * up_val).astype(jnp.bfloat16)
        partial_sums = jnp.einsum('rbf,bfd->brd', hidden.reshape(copy_rows, N_TENSOR, block_units).astype(jnp.float32), down_part.reshape(N_TENSOR, block_units, MODEL_WIDTH).astype(jnp.float32))
        rounded = lax.optimization_barrier(partial_sums.astype(jnp.bfloat16)).astype(jnp.float32)
        return lax.optimization_barrier(jnp.sum(rounded, axis=0)).astype(jnp.bfloat16)
    expert_out = lax.map(expert_rows, (slot_table, gate_weight, up_weight, down_weight)).reshape(COPIES * copy_rows, MODEL_WIDTH)
    per_slot = expert_out[places].astype(jnp.float32).reshape(TOKENS, TOP, MODEL_WIDTH)
    mixture = lax.optimization_barrier(jnp.sum(route_weight[..., None] * per_slot, axis=1))
    combined = residual.astype(jnp.float32) + mixture
    return rms_scale(combined, final_gain).astype(jnp.bfloat16)
```

```python
import functools
import math

import jax
import jax.numpy as jnp
from jax import lax
from jax.experimental import pallas as pl
from jax.experimental.pallas import tpu as pltpu
from jax.sharding import PartitionSpec as P

EXPERTS = 32
TOP = 4
PROMPT_CAP = 256
WINDOW = 192
EPSILON = 1e-06
LANES = 128
HIDE = -1e30
F32 = jnp.float32
BF16 = jnp.bfloat16
I32 = jnp.int32


def swap(block, axis, bits):
    count = lax.axis_size(axis)
    return lax.ppermute(block, axis, [(i, i ^ bits) for i in range(count)])


def swap_both(block, expert_bits, tensor_bits):
    lanes = lax.axis_size("tensor")
    count = lax.axis_size("expert") * lanes
    bits = expert_bits * lanes + tensor_bits
    return lax.ppermute(block, ("expert", "tensor"), [(i, i ^ bits) for i in range(count)])


def iota(shape, dim):
    return lax.broadcasted_iota(I32, shape, dim)


def dot(a, b):
    return jnp.dot(a, b, preferred_element_type=F32)


def dot_t(a, b):
    return lax.dot_general(a, b, (((1,), (1,)), ((), ())), preferred_element_type=F32)


def call(body, outs, args, smem=(), vmem=None, cost=None, name=None):
    in_specs = [
        pl.BlockSpec(memory_space=pltpu.SMEM) if i in smem else pl.BlockSpec(memory_space=pltpu.VMEM)
        for i in range(len(args))
    ]
    single = not isinstance(outs, (list, tuple))
    listed = [outs] if single else list(outs)
    out_specs = [pl.BlockSpec(memory_space=pltpu.VMEM) for _ in listed]
    flops, nbytes = cost or (0, 0)
    result = pl.pallas_call(
        body,
        out_shape=listed,
        in_specs=in_specs,
        out_specs=out_specs,
        compiler_params=pltpu.CompilerParams(vmem_limit_bytes=vmem or 16 << 20),
        cost_estimate=pl.CostEstimate(flops=flops, bytes_accessed=nbytes, transcendentals=0),
        name=name,
    )(*args)
    return result[0] if single else result


def shape(dims, dtype):
    return jax.ShapeDtypeStruct(tuple(dims), dtype)


def spread(rows, values):
    index = iota((rows, LANES), 0)
    total = jnp.full((rows, LANES), values[0], I32)
    for i in range(1, rows):
        total = jnp.where(index == i, values[i], total)
    return total


def row_places(rows, length_ref, group_ref, offset_ref):
    groups = [group_ref[i] for i in range(rows)]
    lengths = [length_ref[0, g] for g in groups]
    row_length = spread(rows, lengths)
    position = spread(rows, [lengths[i] + offset_ref[i] for i in range(rows)])
    return spread(rows, groups), row_length, position


def project_body(member_ref, length_ref, group_ref, offset_ref, tok_ref, gain_ref, qw_ref, kvw_ref, q_ref, own_ref):
    rows, width = tok_ref.shape
    dim = kvw_ref.shape[2]
    heads = qw_ref.shape[1] // dim
    half = dim // 2
    tok = tok_ref[...].astype(F32)
    mean = jnp.sum(tok * tok, axis=1, keepdims=True) / width
    normed = (tok * lax.rsqrt(mean + EPSILON) * gain_ref[...].astype(F32)).astype(BF16)
    _, _, position = row_places(rows, length_ref, group_ref, offset_ref)
    lane = iota((rows, dim), 1)
    step = jnp.where(lane >= half, lane - half, lane).astype(F32)
    angle = position.astype(F32) * jnp.exp(step * (-math.log(10000.0) / half))
    cosine = jnp.cos(angle)
    sine = jnp.sin(angle)
    sine = jnp.where(lane < half, -sine, sine)
    own = dot(normed, kvw_ref[0])
    keyed = member_ref[0] % 2 == 0
    turned = own * cosine + pltpu.roll(own, half, 1) * sine
    own_ref[...] = jnp.where(keyed, turned, own).astype(BF16)
    q = dot(normed, qw_ref[...])
    for h in range(heads):
        part = q[:, h * dim : (h + 1) * dim]
        q_ref[h * rows : (h + 1) * rows, :] = (part * cosine + pltpu.roll(part, half, 1) * sine).astype(BF16)


def cached_body(
    member_ref, length_ref, group_ref, offset_ref, sink_ref, q_ref, mine_ref, theirs_ref,
    routes_ref, weight_ref, slot_ref, sums_ref, tops_ref, parts_ref, extra_ref,
):
    rows = routes_ref.shape[0]
    dim = q_ref.shape[1]
    heads = q_ref.shape[0] // rows
    slots = mine_ref.shape[0]
    scale = 1.0 / dim**0.5
    keyed = member_ref[0] % 2 == 0
    mine, theirs = mine_ref[...], theirs_ref[...]
    keys = jnp.where(keyed, mine, theirs)
    values = jnp.where(keyed, theirs, mine)
    group, row_length, position = row_places(rows, length_ref, group_ref, offset_ref)
    lane = iota((rows, LANES), 1)
    seen = []
    for start in range(0, slots, LANES):
        place = lane + start % PROMPT_CAP
        seen.append((group == start // PROMPT_CAP) & (place < row_length) & (place > position - WINDOW))
    scores = dot_t(q_ref[...], keys)
    probs = []
    for h in range(heads):
        span = slice(h * rows, (h + 1) * rows)
        masked = [
            jnp.where(seen[k], scores[span, k * LANES : (k + 1) * LANES] * scale, HIDE) for k in range(len(seen))
        ]
        top = functools.reduce(jnp.maximum, masked)
        top = jnp.maximum(jnp.max(top, axis=1, keepdims=True), sink_ref[h])
        part = [jnp.exp(m - top) for m in masked]
        total = jnp.sum(functools.reduce(jnp.add, part), axis=1, keepdims=True) + jnp.exp(sink_ref[h] - top)
        probs.append(jnp.concatenate([p.astype(BF16) for p in part], axis=1))
        tops_ref[span, :] = jnp.broadcast_to(top, (rows, LANES))
        parts_ref[span, :] = jnp.broadcast_to(total, (rows, LANES))
    sums_ref[...] = dot(jnp.concatenate(probs, axis=0), values)
    copies = slot_ref.shape[1]
    replicas = copies // EXPERTS
    block = iota((rows, copies), 0) // (rows // replicas)
    place = iota((rows, copies), 1)
    chosen = jnp.zeros((rows, copies), F32)
    for k in range(TOP):
        named = routes_ref[:, k : k + 1] * replicas + block
        chosen = chosen + jnp.where(named == place, weight_ref[:, k : k + 1], 0.0)
    order = (iota((copies, copies), 0) == slot_ref[...]).astype(F32).astype(BF16)
    high = chosen.astype(BF16)
    low = (chosen - high.astype(F32)).astype(BF16)
    packed = [dot_t(high, order), dot_t(low, order)]
    spare = extra_ref.shape[1] - 2 * copies
    extra_ref[...] = jnp.concatenate(packed + [jnp.zeros((rows, spare), F32)], axis=1)


def attend_body(
    member_ref, q_ref, mine_ref, theirs_ref, sums_ref, tops_ref, parts_ref, out_ref, tok_ref, extra_ref,
    send_ref, keep_ref,
):
    rows, width = tok_ref.shape
    dim = q_ref.shape[1]
    heads = q_ref.shape[0] // rows
    quarter = width // 4
    scale = 1.0 / dim**0.5
    member = member_ref[0]
    keyed = member % 2 == 0
    mine, theirs = mine_ref[...].astype(F32), theirs_ref[...].astype(F32)
    key = jnp.where(keyed, mine, theirs)
    value = jnp.where(keyed, theirs, mine)
    context = []
    for h in range(heads):
        span = slice(h * rows, (h + 1) * rows)
        score = jnp.sum(q_ref[span, :].astype(F32) * key, axis=1, keepdims=True) * scale
        top = jnp.maximum(tops_ref[span, :], score)
        old = jnp.exp(tops_ref[span, :] - top)
        own = jnp.exp(score - top)
        inverse = 1.0 / (parts_ref[span, :] * old + own)
        context.append(((sums_ref[span, :] * old + own * value) * inverse).astype(BF16))
    attended = dot(jnp.concatenate(context, axis=1), out_ref[...])
    part = [attended[:, i * quarter : (i + 1) * quarter] for i in range(4)]
    token = [tok_ref[:, i * quarter : (i + 1) * quarter].astype(F32) for i in range(4)]
    first = member < 2
    for i in range(2):
        span = slice(i * quarter, (i + 1) * quarter)
        send_ref[:, span] = jnp.where(keyed, part[2 * i + 1], part[2 * i]).astype(BF16)
        kept = jnp.where(keyed, part[2 * i], part[2 * i + 1])
        added = jnp.where(keyed, token[2 * i], token[2 * i + 1])
        keep_ref[:, span] = kept + jnp.where(first, added, 0.0)
    keep_ref[:, 2 * quarter :] = jnp.where(first, extra_ref[...], 0.0)


def chip_body(keep_ref, got_ref, out_ref):
    width = got_ref.shape[1]
    out_ref[:, :width] = (keep_ref[:, :width] + got_ref[...].astype(F32)).astype(BF16)
    out_ref[:, width:] = keep_ref[:, width:].astype(BF16)


def residual_body(copies, member_ref, gain_ref, own_ref, x_ref, y_ref, xy_ref, rows_ref, keep_ref):
    rows, total = own_ref.shape
    quarter = keep_ref.shape[1]
    width = 2 * quarter
    keyed = member_ref[0] % 2 == 0
    gain = [gain_ref[:, i * quarter : (i + 1) * quarter] for i in range(4)]
    gain = [jnp.where(keyed, gain[2 * i], gain[2 * i + 1]).astype(F32) for i in range(2)]
    lane = iota((rows, total - width), 1)
    for i, (a_ref, b_ref) in enumerate(((own_ref, x_ref), (y_ref, xy_ref))):
        span = slice(i * rows, (i + 1) * rows)
        parts = []
        squares = jnp.zeros((rows, 1), F32)
        for k in range(2):
            cols = slice(k * quarter, (k + 1) * quarter)
            part = (a_ref[:, cols].astype(F32) + b_ref[:, cols].astype(F32)).astype(BF16)
            wide = part.astype(F32)
            squares = squares + jnp.sum(wide * wide, axis=1, keepdims=True)
            rows_ref[span, cols] = (wide * gain[k]).astype(BF16)
            parts.append(part)
        extra = a_ref[:, width:].astype(F32) + b_ref[:, width:].astype(F32)
        high = squares.astype(BF16).astype(F32)
        extra = jnp.where(lane == 2 * copies, high, extra)
        extra = jnp.where(lane == 2 * copies + 1, squares - high, extra)
        rows_ref[span, width:] = extra.astype(BF16)
        if i == 0:
            keep_ref[...] = jnp.where(member_ref[0] < 2, parts[0], parts[1])


def expert_body(copies, blocks, member_ref, *refs):
    own_refs, other_refs = refs[:blocks], refs[blocks : 2 * blocks]
    gate_ref, up_ref, down_ref, hidden_ref, send_ref = refs[2 * blocks :]
    hosted, width, units = gate_ref.shape
    quarter = width // 4
    keyed = member_ref[0] % 2 == 0
    own = jnp.concatenate([r[...] for r in own_refs], axis=0)
    other = jnp.concatenate([r[...] for r in other_refs], axis=0)
    parts = []
    for i in range(4):
        span = slice(i // 2 * quarter, (i // 2 + 1) * quarter)
        mine = keyed if i % 2 == 0 else jnp.logical_not(keyed)
        parts.append(jnp.where(mine, own[:, span], other[:, span]))
    rows = jnp.concatenate(parts, axis=1)
    extra = own[:, 2 * quarter :].astype(F32)
    lane = iota(extra.shape, 1)
    squares = jnp.where((lane == 2 * copies) | (lane == 2 * copies + 1), extra + other[:, 2 * quarter :].astype(F32), 0.0)
    scale = lax.rsqrt(jnp.sum(squares, axis=1, keepdims=True) / width + EPSILON)
    tall = rows.shape[0] // blocks
    for j in range(hosted):
        slot = member_ref[1] * hosted + j
        weight = jnp.where((lane == slot) | (lane == slot + copies), extra, 0.0)
        weight = jnp.sum(weight, axis=1, keepdims=True)
        gate = dot(rows, gate_ref[j]) * scale
        up = dot(rows, up_ref[j]) * scale
        hidden = (jnp.maximum(gate, 0.0) * up * weight).astype(BF16)
        for b in range(blocks):
            hidden_ref[j, b] = hidden[b * tall : (b + 1) * tall]
    for k in range(2):
        start = pl.multiple_of((2 * k + 1 - member_ref[0] % 2) * quarter, LANES)
        total = None
        for j in range(hosted):
            hidden = jnp.concatenate([hidden_ref[j, b] for b in range(blocks)], axis=0)
            part = dot(hidden, down_ref[j, :, pl.ds(start, quarter)])
            total = part if total is None else total + part
        total = total.astype(BF16)
        for b in range(blocks):
            send_ref[b, :, k * quarter : (k + 1) * quarter] = total[b * tall : (b + 1) * tall]


def keep_body(blocks, member_ref, hidden_ref, down_ref, out_ref):
    hosted = down_ref.shape[0]
    quarter = down_ref.shape[2] // 4
    tall = hidden_ref.shape[2]
    for k in range(2):
        start = pl.multiple_of((2 * k + member_ref[0] % 2) * quarter, LANES)
        total = None
        for j in range(hosted):
            hidden = jnp.concatenate([hidden_ref[j, b] for b in range(blocks)], axis=0)
            part = dot(hidden, down_ref[j, :, pl.ds(start, quarter)])
            total = part if total is None else total + part
        for b in range(blocks):
            out_ref[b, :, k * quarter : (k + 1) * quarter] = total[b * tall : (b + 1) * tall]


def split_body(member_ref, keep_ref, got_ref, own_ref, x_ref, y_ref, xy_ref):
    rows, quarter = own_ref.shape[1:]
    first = member_ref[0] < 2
    near = keep_ref[:, :, :quarter] + got_ref[:, :, :quarter].astype(F32)
    far = keep_ref[:, :, quarter:] + got_ref[:, :, quarter:].astype(F32)
    mine = jnp.where(first, near, far)
    theirs = jnp.where(first, far, near)
    own_ref[...] = mine[:, :rows]
    x_ref[...] = theirs[:, :rows].astype(BF16)
    y_ref[...] = mine[:, rows:].astype(BF16)
    xy_ref[...] = theirs[:, rows:].astype(BF16)


def pass_body(terms, *refs):
    total = refs[0][...]
    for r in refs[1:terms]:
        total = total + r[...].astype(F32)
    outs = refs[terms:]
    tall = total.shape[0] // len(outs)
    for i, r in enumerate(outs):
        r[...] = total[i * tall : (i + 1) * tall].astype(r.dtype)


def combine_body(terms, *refs):
    residual_ref, combined_ref, square_ref = refs[terms:]
    total = refs[0][0]
    for r in refs[1:terms]:
        total = total + r[0].astype(F32)
    total = residual_ref[...].astype(F32) + total
    combined_ref[...] = total
    square_ref[...] = jnp.broadcast_to(jnp.sum(total * total, axis=1, keepdims=True), square_ref.shape)


def finish_body(width, combined_ref, gain_ref, a_ref, b_ref, c_ref, d_ref, out_ref):
    mean = (a_ref[...] + b_ref[...] + c_ref[...] + d_ref[...])[:, :1] / width
    out_ref[...] = (combined_ref[...] * lax.rsqrt(mean + EPSILON) * gain_ref[...].astype(F32)).astype(BF16)


def expert_calls(member, own, other, gate_weight, up_weight, down_weight, copies):
    blocks = len(own)
    tall, total = own[0].shape
    hosted, width, units = gate_weight.shape
    step = min(tall, 64)
    grid = (tall // step,)
    smem = pl.BlockSpec(memory_space=pltpu.SMEM)
    row_spec = pl.BlockSpec((step, total), lambda i: (i, 0))
    half_spec = pl.BlockSpec((blocks, step, width // 2), lambda i: (0, i, 0))
    hidden_spec = pl.BlockSpec((hosted, blocks, step, units), lambda i: (0, 0, i, 0))
    whole = pl.BlockSpec(memory_space=pltpu.VMEM)
    params = pltpu.CompilerParams(vmem_limit_bytes=40 << 20)
    flops = 2 * blocks * tall * hosted * width * units
    hidden, send = pl.pallas_call(
        functools.partial(expert_body, copies, blocks),
        grid=grid,
        out_shape=[shape((hosted, blocks, tall, units), BF16), shape((blocks, tall, width // 2), BF16)],
        in_specs=[smem] + [row_spec] * (2 * blocks) + [whole] * 3,
        out_specs=[hidden_spec, half_spec],
        compiler_params=params,
        cost_estimate=pl.CostEstimate(flops=5 * flops // 2, bytes_accessed=8 << 20, transcendentals=0),
        name="experts",
    )(member, *own, *other, gate_weight, up_weight, down_weight)
    got = swap(send, "tensor", 1)
    keep = pl.pallas_call(
        functools.partial(keep_body, blocks),
        grid=grid,
        out_shape=shape((blocks, tall, width // 2), F32),
        in_specs=[smem, hidden_spec, whole],
        out_specs=half_spec,
        compiler_params=params,
        cost_estimate=pl.CostEstimate(flops=flops // 2, bytes_accessed=4 << 20, transcendentals=0),
        name="experts_own_half",
    )(member, hidden, down_weight)
    return keep, got


def on_device(
    tokens, attn_gain, query_weight, key_value_weight, paired_cache, prompt_length, group_index, offsets,
    sink_logit, out_weight, mixer_gain, routes, route_weight, copy_slot, gate_weight, up_weight, down_weight,
    final_gain,
):
    rows, width = tokens.shape
    dim = key_value_weight.shape[2]
    heads = query_weight.shape[1] // dim
    half, quarter = width // 2, width // 4
    copies = copy_slot.shape[0]
    peers = lax.axis_size("expert")
    extra_width = -(-(2 * copies + 2) // LANES) * LANES
    member = jnp.stack([lax.axis_index("tensor"), lax.axis_index("expert")]).astype(I32)
    places = (prompt_length, group_index, offsets)

    own_cache = paired_cache[0, 0]
    other_cache = swap(own_cache, "tensor", 1)
    queries, own_new = call(
        project_body,
        [shape((heads * rows, dim), BF16), shape((rows, dim), BF16)],
        (member, *places, tokens, attn_gain[None, :], query_weight, key_value_weight),
        smem=range(4),
        name="project",
        cost=(2 * rows * width * (heads + 1) * dim, 2 << 20),
    )
    other_new = swap(own_new, "tensor", 1)
    sums, tops, parts, extra = call(
        cached_body,
        [shape((heads * rows, dim), F32)] + [shape((heads * rows, LANES), F32)] * 2 + [shape((rows, extra_width), F32)],
        (member, *places, sink_logit, queries, own_cache, other_cache, routes, route_weight, copy_slot[None, :]),
        smem=range(5),
        name="cached_attention",
        cost=(4 * heads * rows * dim * own_cache.shape[0], 1 << 20),
    )
    send, keep = call(
        attend_body,
        [shape((rows, half), BF16), shape((rows, half + extra_width), F32)],
        (member, queries, own_new, other_new, sums, tops, parts, out_weight, tokens, extra),
        smem=range(1),
        name="attention_out",
        cost=(2 * rows * heads * dim * width, 2 << 20),
    )
    own = call(
        chip_body, shape((rows, half + extra_width), BF16), (keep, swap(send, "tensor", 1)), name="chip_sum",
        cost=(rows * width, 1 << 18),
    )
    block, residual = call(
        functools.partial(residual_body, copies),
        [shape((2 * rows, half + extra_width), BF16), shape((rows, quarter), BF16)],
        (member, mixer_gain[None, :], own, swap(own, "tensor", 2), swap(own, "expert", 1), swap_both(own, 1, 2)),
        smem=range(1),
        name="residual",
        cost=(rows * width, 1 << 18),
    )

    bit, stages = 2, []
    while bit < peers:
        stages.append([bit] if 2 * bit >= peers else [bit, 2 * bit, 3 * bit])
        bit *= 4
    blocks = [block]
    for stage in stages:
        whole = blocks[0] if len(blocks) == 1 else jnp.concatenate(blocks, axis=0)
        blocks = [whole] + [swap(whole, "expert", b) for b in stage]
    others = [swap(b, "tensor", 1) for b in blocks]
    keep, got = expert_calls(member, blocks, others, gate_weight, up_weight, down_weight, copies)

    groups = peers // 2
    piece = (groups, rows, quarter)
    own, x_part, y_part, xy_part = call(
        split_body,
        [shape(piece, F32)] + [shape(piece, BF16)] * 3,
        (member, keep.reshape(groups, 2 * rows, half), got.reshape(groups, 2 * rows, half)),
        smem=range(1),
        vmem=48 << 20,
        name="split",
        cost=(groups * rows * width, 2 << 20),
    )
    terms = [own, swap(x_part, "tensor", 2), swap(y_part, "expert", 1), swap_both(xy_part, 1, 2)]
    for stage in stages[::-1]:
        count = len(stage) + 1
        groups //= count
        piece = (groups, rows, quarter)
        pieces = call(
            functools.partial(pass_body, len(terms)),
            [shape(piece, F32)] + [shape(piece, BF16)] * len(stage),
            terms,
            vmem=48 << 20,
            name="pass_on",
            cost=(groups * rows * width, 1 << 20),
        )
        terms = [pieces[0]] + [swap(p, "expert", b) for p, b in zip(pieces[1:], stage)]
    combined, squares = call(
        functools.partial(combine_body, len(terms)),
        [shape((rows, quarter), F32), shape((rows, LANES), F32)],
        (*terms, residual),
        name="combine",
        cost=(rows * width, 1 << 18),
    )
    return call(
        functools.partial(finish_body, width),
        shape((rows, quarter), BF16),
        (combined, final_gain[None, :], squares, *[swap(squares, "tensor", b) for b in (1, 2, 3)]),
        name="finish",
        cost=(rows * width, 1 << 18),
    )


def solution(mesh):
    in_specs = (
        P("expert", None),
        P(),
        P(None, "tensor"),
        P("tensor", None, None),
        P("expert", "tensor", None, None),
        P("expert", None),
        P("expert"),
        P("expert"),
        P("tensor"),
        P("tensor", None),
        P(),
        P("expert", None),
        P("expert", None),
        P(),
        P("expert", None, "tensor"),
        P("expert", None, "tensor"),
        P("expert", "tensor", None),
        P("tensor"),
    )
    out_specs = P("expert", "tensor")
    return jax.shard_map(
        on_device, mesh=mesh, in_specs=in_specs, out_specs=out_specs, check_vma=False
    )
```

```python
import functools
import math

import jax
import jax.numpy as jnp
from jax import lax
from jax.experimental import pallas as pl
from jax.experimental.pallas import tpu as pltpu
from jax.sharding import PartitionSpec as P

EXPERTS = 32
TOP = 4
PROMPT_CAP = 256
WINDOW = 192
EPSILON = 1e-06
LANES = 128
HIDE = -1e30
F32 = jnp.float32
BF16 = jnp.bfloat16
I32 = jnp.int32


def swap(block, axis, bits):
    count = lax.axis_size(axis)
    return lax.ppermute(block, axis, [(i, i ^ bits) for i in range(count)])


def swap_both(block, expert_bits, tensor_bits):
    lanes = lax.axis_size("tensor")
    count = lax.axis_size("expert") * lanes
    bits = expert_bits * lanes + tensor_bits
    return lax.ppermute(block, ("expert", "tensor"), [(i, i ^ bits) for i in range(count)])


def iota(shape, dim):
    return lax.broadcasted_iota(I32, shape, dim)


def dot(a, b):
    return jnp.dot(a, b, preferred_element_type=F32)


def dot_t(a, b):
    return lax.dot_general(a, b, (((1,), (1,)), ((), ())), preferred_element_type=F32)


def call(body, outs, args, hbm=(), scratch=(), vmem=None, cost=None, name=None):
    in_specs = [
        pl.BlockSpec(memory_space=pltpu.HBM) if i in hbm else pl.BlockSpec(memory_space=pltpu.VMEM)
        for i in range(len(args))
    ]
    single = not isinstance(outs, (list, tuple))
    listed = [outs] if single else list(outs)
    out_specs = [pl.BlockSpec(memory_space=pltpu.VMEM) for _ in listed]
    flops, nbytes = cost or (0, 0)
    result = pl.pallas_call(
        body,
        out_shape=listed,
        in_specs=in_specs,
        out_specs=out_specs,
        scratch_shapes=list(scratch),
        compiler_params=pltpu.CompilerParams(vmem_limit_bytes=vmem or 16 << 20),
        cost_estimate=pl.CostEstimate(flops=flops, bytes_accessed=nbytes, transcendentals=0),
        name=name,
    )(*args)
    return result[0] if single else result


def shape(dims, dtype):
    return jax.ShapeDtypeStruct(tuple(dims), dtype)


def spread(rows, values):
    index = iota((rows, LANES), 0)
    total = jnp.full((rows, LANES), values[0], I32)
    for i in range(1, rows):
        total = jnp.where(index == i, values[i], total)
    return total


def is_key():
    return lax.axis_index("tensor") % 2 == 0


def is_first():
    return lax.axis_index("tensor") < 2


def project_body(
    length_hbm, group_hbm, offset_hbm, tok_hbm, gain_hbm, kvw_hbm, qw_hbm, cache_hbm,
    q_ref, own_ref, cache_ref, token_ref, group_out, length_out, position_out,
    length_ref, group_ref, offset_ref, tok_ref, gain_ref, kvw_ref, qw_ref, sems,
):
    pairs = [
        (length_hbm, length_ref), (group_hbm, group_ref), (offset_hbm, offset_ref), (tok_hbm, tok_ref),
        (gain_hbm, gain_ref), (kvw_hbm.at[0], kvw_ref), (qw_hbm, qw_ref), (cache_hbm.at[0, 0], cache_ref),
    ]
    loads = [pltpu.make_async_copy(src, dst, sems.at[i]) for i, (src, dst) in enumerate(pairs)]
    for load in loads:
        load.start()
    rows, width = tok_ref.shape
    dim = kvw_ref.shape[1]
    heads = qw_ref.shape[1] // dim
    half = dim // 2
    quarter = width // 4
    for load in loads[:3]:
        load.wait()
    groups = [group_ref[i] for i in range(rows)]
    lengths = [length_ref[0, g] for g in groups]
    group_out[...] = spread(rows, groups)
    length_out[...] = spread(rows, lengths)
    position = spread(rows, [lengths[i] + offset_ref[i] for i in range(rows)])
    position_out[...] = position
    lane = iota((rows, dim), 1)
    step = jnp.where(lane >= half, lane - half, lane).astype(F32)
    angle = position.astype(F32) * jnp.exp(step * (-math.log(10000.0) / half))
    cosine = jnp.cos(angle)
    sine = jnp.sin(angle)
    sine = jnp.where(lane < half, -sine, sine)
    loads[3].wait()
    loads[4].wait()
    tok = tok_ref[...].astype(F32)
    mean = jnp.sum(tok * tok, axis=1, keepdims=True) / width
    normed = (tok * lax.rsqrt(mean + EPSILON) * gain_ref[...].astype(F32)).astype(BF16)
    for i in range(2):
        low, high = (tok[:, (2 * i + k) * quarter : (2 * i + k + 1) * quarter] for k in range(2))
        token_ref[:, i * quarter : (i + 1) * quarter] = jnp.where(
            is_first(), jnp.where(is_key(), low, high), 0.0
        )
    loads[5].wait()
    own = dot(normed, kvw_ref[...])
    turned = own * cosine + pltpu.roll(own, half, 1) * sine
    own_ref[...] = jnp.where(is_key(), turned, own).astype(BF16)
    loads[6].wait()
    q = dot(normed, qw_ref[...])
    for h in range(heads):
        part = q[:, h * dim : (h + 1) * dim]
        q_ref[h * rows : (h + 1) * rows, :] = (part * cosine + pltpu.roll(part, half, 1) * sine).astype(BF16)
    loads[7].wait()


def cached_body(
    q_ref, mine_ref, theirs_ref, group_ref, length_ref, position_ref, sink_hbm, routes_hbm, weight_hbm, slot_hbm,
    sums_ref, tops_ref, parts_ref, extra_ref, sink_ref, routes_ref, weight_ref, slot_ref, sems,
):
    pairs = [(sink_hbm, sink_ref), (routes_hbm, routes_ref), (weight_hbm, weight_ref), (slot_hbm, slot_ref)]
    loads = [pltpu.make_async_copy(src, dst, sems.at[i]) for i, (src, dst) in enumerate(pairs)]
    for load in loads:
        load.start()
    rows = group_ref.shape[0]
    dim = q_ref.shape[1]
    heads = q_ref.shape[0] // rows
    slots = mine_ref.shape[0]
    scale = 1.0 / dim**0.5
    mine, theirs = mine_ref[...], theirs_ref[...]
    keys = jnp.where(is_key(), mine, theirs)
    values = jnp.where(is_key(), theirs, mine)
    scores = dot_t(q_ref[...], keys)
    group, row_length, position = group_ref[...], length_ref[...], position_ref[...]
    lane = iota((rows, LANES), 1)
    seen = []
    for start in range(0, slots, LANES):
        place = lane + start % PROMPT_CAP
        seen.append((group == start // PROMPT_CAP) & (place < row_length) & (place > position - WINDOW))
    for load in loads:
        load.wait()
    probs = []
    for h in range(heads):
        span = slice(h * rows, (h + 1) * rows)
        masked = [
            jnp.where(seen[k], scores[span, k * LANES : (k + 1) * LANES] * scale, HIDE) for k in range(len(seen))
        ]
        top = functools.reduce(jnp.maximum, masked)
        top = jnp.maximum(jnp.max(top, axis=1, keepdims=True), sink_ref[h])
        part = [jnp.exp(m - top) for m in masked]
        total = jnp.sum(functools.reduce(jnp.add, part), axis=1, keepdims=True) + jnp.exp(sink_ref[h] - top)
        probs.append(jnp.concatenate([p.astype(BF16) for p in part], axis=1))
        tops_ref[span, :] = jnp.broadcast_to(top, (rows, LANES))
        parts_ref[span, :] = jnp.broadcast_to(total, (rows, LANES))
    sums_ref[...] = dot(jnp.concatenate(probs, axis=0), values)
    copies = slot_ref.shape[1]
    replicas = copies // EXPERTS
    block = iota((copies, rows), 1) // (rows // replicas)
    place = iota((copies, rows), 0)
    chosen = jnp.zeros((copies, rows), F32)
    for k in range(TOP):
        named = routes_ref[k : k + 1, :] * replicas + block
        chosen = chosen + jnp.where(named == place, weight_ref[k : k + 1, :], 0.0)
    order = (iota((copies, copies), 0) == slot_ref[...]).astype(F32).astype(BF16)
    high = chosen.astype(BF16)
    low = (chosen - high.astype(F32)).astype(BF16)
    extra_ref[...] = jnp.zeros(extra_ref.shape, F32)
    for i, part in enumerate((high, low)):
        moved = lax.dot_general(part, order, (((0,), (1,)), ((), ())), preferred_element_type=F32)
        extra_ref[:, i * copies : (i + 1) * copies] = jnp.where(is_first(), moved, 0.0)


def attend_body(
    q_ref, mine_ref, theirs_ref, sums_ref, tops_ref, parts_ref, out_ref, token_ref, extra_ref, send_ref, keep_ref
):
    rows, dim = mine_ref.shape
    heads = q_ref.shape[0] // rows
    quarter = send_ref.shape[1] // 2
    scale = 1.0 / dim**0.5
    mine, theirs = mine_ref[...].astype(F32), theirs_ref[...].astype(F32)
    key = jnp.where(is_key(), mine, theirs)
    value = jnp.where(is_key(), theirs, mine)
    context = []
    for h in range(heads):
        span = slice(h * rows, (h + 1) * rows)
        score = jnp.sum(q_ref[span, :].astype(F32) * key, axis=1, keepdims=True) * scale
        top = jnp.maximum(tops_ref[span, :], score)
        old = jnp.exp(tops_ref[span, :] - top)
        own = jnp.exp(score - top)
        inverse = 1.0 / (parts_ref[span, :] * old + own)
        context.append(((sums_ref[span, :] * old + own * value) * inverse).astype(BF16))
    attended = dot(jnp.concatenate(context, axis=1), out_ref[...])
    part = [attended[:, i * quarter : (i + 1) * quarter] for i in range(4)]
    for i in range(2):
        span = slice(i * quarter, (i + 1) * quarter)
        send_ref[:, span] = jnp.where(is_key(), part[2 * i + 1], part[2 * i]).astype(BF16)
        keep_ref[:, span] = jnp.where(is_key(), part[2 * i], part[2 * i + 1]) + token_ref[:, span]
    keep_ref[:, 2 * quarter :] = extra_ref[...]


def chip_body(keep_ref, got_ref, out_ref):
    width = got_ref.shape[1]
    out_ref[:, :width] = (keep_ref[:, :width] + got_ref[...].astype(F32)).astype(BF16)
    out_ref[:, width:] = keep_ref[:, width:].astype(BF16)


def residual_body(copies, gain_ref, own_ref, x_ref, y_ref, xy_ref, rows_ref, keep_ref):
    rows, total = own_ref.shape
    width = keep_ref.shape[1]
    quarter = width // 2
    gain = [gain_ref[:, i * quarter : (i + 1) * quarter] for i in range(4)]
    gain = [jnp.where(is_key(), gain[2 * i].astype(F32), gain[2 * i + 1].astype(F32)) for i in range(2)]
    lane = iota((rows, total - width), 1)
    for i, (a_ref, b_ref) in enumerate(((own_ref, x_ref), (y_ref, xy_ref))):
        span = slice(i * rows, (i + 1) * rows)
        squares = jnp.zeros((rows, 1), F32)
        for k in range(2):
            cols = slice(k * quarter, (k + 1) * quarter)
            part = (a_ref[:, cols].astype(F32) + b_ref[:, cols].astype(F32)).astype(BF16)
            wide = part.astype(F32)
            squares = squares + jnp.sum(wide * wide, axis=1, keepdims=True)
            rows_ref[span, cols] = (wide * gain[k]).astype(BF16)
            if i == 0:
                keep_ref[:, cols] = part
        extra = a_ref[:, width:].astype(F32) + b_ref[:, width:].astype(F32)
        high = squares.astype(BF16).astype(F32)
        extra = jnp.where(lane == 2 * copies, high, extra)
        extra = jnp.where(lane == 2 * copies + 1, squares - high, extra)
        rows_ref[span, width:] = extra.astype(BF16)


def expert_body(copies, blocks, *refs):
    own_refs, other_refs = refs[:blocks], refs[blocks : 2 * blocks]
    gate_ref, up_ref, down_ref, hidden_ref, send_ref = refs[2 * blocks :]
    hosted, units, width = gate_ref.shape
    quarter = width // 4
    own = jnp.concatenate([r[...] for r in own_refs], axis=0)
    other = jnp.concatenate([r[...] for r in other_refs], axis=0)
    parts = []
    for i in range(4):
        span = slice(i // 2 * quarter, (i // 2 + 1) * quarter)
        mine = is_key() if i % 2 == 0 else jnp.logical_not(is_key())
        parts.append(jnp.where(mine, own[:, span], other[:, span]))
    rows = jnp.concatenate(parts, axis=1)
    extra = own[:, 2 * quarter :].astype(F32)
    lane = iota(extra.shape, 1)
    squares = jnp.where((lane == 2 * copies) | (lane == 2 * copies + 1), extra + other[:, 2 * quarter :].astype(F32), 0.0)
    scale = lax.rsqrt(jnp.sum(squares, axis=1, keepdims=True) / width + EPSILON)
    tall = rows.shape[0] // blocks
    hiddens = []
    for j in range(hosted):
        slot = lax.axis_index("expert") * hosted + j
        weight = jnp.where((lane == slot) | (lane == slot + copies), extra, 0.0)
        weight = jnp.sum(weight, axis=1, keepdims=True)
        gate = dot_t(rows, gate_ref[j]) * scale
        up = dot_t(rows, up_ref[j]) * scale
        hidden = (jnp.maximum(gate, 0.0) * up * weight).astype(BF16)
        hiddens.append(hidden)
        for b in range(blocks):
            hidden_ref[j, b] = hidden[b * tall : (b + 1) * tall]
    for k in range(2):
        start = pl.multiple_of((2 * k + 1 - lax.axis_index("tensor") % 2) * quarter, LANES)
        total = None
        for j in range(hosted):
            part = dot(hiddens[j], down_ref[j, :, pl.ds(start, quarter)])
            total = part if total is None else total + part
        total = total.astype(BF16)
        for b in range(blocks):
            send_ref[b, :, k * quarter : (k + 1) * quarter] = total[b * tall : (b + 1) * tall]


def keep_body(blocks, hidden_ref, down_ref, out_ref):
    hosted = down_ref.shape[0]
    quarter = down_ref.shape[2] // 4
    tall = hidden_ref.shape[2]
    hiddens = [jnp.concatenate([hidden_ref[j, b] for b in range(blocks)], axis=0) for j in range(hosted)]
    for k in range(2):
        start = pl.multiple_of((2 * k + lax.axis_index("tensor") % 2) * quarter, LANES)
        total = None
        for j in range(hosted):
            part = dot(hiddens[j], down_ref[j, :, pl.ds(start, quarter)])
            total = part if total is None else total + part
        for b in range(blocks):
            out_ref[b, :, k * quarter : (k + 1) * quarter] = total[b * tall : (b + 1) * tall]


def chips_body(keep_ref, got_ref, *out_refs):
    for b, out_ref in enumerate(out_refs):
        out_ref[...] = (keep_ref[b] + got_ref[b].astype(F32)).astype(out_ref.dtype)


def pass_body(terms, *refs):
    total = refs[0][...]
    for r in refs[1:terms]:
        total = total + r[...].astype(F32)
    outs = refs[terms:]
    tall = total.shape[0] // len(outs)
    for i, r in enumerate(outs):
        r[...] = total[i * tall : (i + 1) * tall].astype(r.dtype)


def pair_body(terms, *refs):
    total = refs[0][...]
    for r in refs[1:terms]:
        total = total + r[...].astype(F32)
    own_ref, x_ref, y_ref = refs[terms:]
    rows = own_ref.shape[0]
    own_ref[...] = total[:rows]
    x_ref[...] = total[:rows].astype(BF16)
    y_ref[...] = total[rows:].astype(BF16)


def combine_body(own_ref, x_ref, y_ref, xy_ref, residual_ref, combined_ref, square_ref):
    quarter = combined_ref.shape[1]
    total = (own_ref[...] + x_ref[...].astype(F32)) + (y_ref[...].astype(F32) + xy_ref[...].astype(F32))
    total = residual_ref[...].astype(F32) + total
    combined_ref[...] = jnp.where(is_first(), total[:, :quarter], total[:, quarter:])
    square_ref[...] = jnp.broadcast_to(jnp.sum(total * total, axis=1, keepdims=True), square_ref.shape)


def finish_body(width, combined_ref, gain_ref, a_ref, b_ref, out_ref):
    mean = (a_ref[...] + b_ref[...])[:, :1] / width
    out_ref[...] = (combined_ref[...] * lax.rsqrt(mean + EPSILON) * gain_ref[...].astype(F32)).astype(BF16)


def run_experts(own, other, gate_weight, up_weight, down_weight, copies, first):
    blocks = len(own)
    tall, total = own[0].shape
    hosted, units, width = gate_weight.shape
    step = min(tall, 64)
    grid = (tall // step,) if tall > step else ()

    def spec(dims, place):
        if not grid:
            return pl.BlockSpec(memory_space=pltpu.VMEM)
        return pl.BlockSpec(dims, place)

    row_spec = spec((step, total), lambda i: (i, 0))
    half_spec = spec((blocks, step, width // 2), lambda i: (0, i, 0))
    hidden_spec = spec((hosted, blocks, step, units), lambda i: (0, 0, i, 0))
    whole = pl.BlockSpec(memory_space=pltpu.VMEM)
    params = pltpu.CompilerParams(vmem_limit_bytes=32 << 20)
    flops = 2 * blocks * tall * hosted * width * units
    hidden, send = pl.pallas_call(
        functools.partial(expert_body, copies, blocks),
        grid=grid,
        out_shape=[shape((hosted, blocks, tall, units), BF16), shape((blocks, tall, width // 2), BF16)],
        in_specs=[row_spec] * (2 * blocks) + [whole] * 3,
        out_specs=[hidden_spec, half_spec],
        compiler_params=params,
        cost_estimate=pl.CostEstimate(flops=5 * flops // 2, bytes_accessed=8 << 20, transcendentals=0),
        name="experts",
    )(*own, *other, gate_weight, up_weight, down_weight)
    got = swap(send, "tensor", 1)
    keep = pl.pallas_call(
        functools.partial(keep_body, blocks),
        grid=grid,
        out_shape=shape((blocks, tall, width // 2), F32),
        in_specs=[hidden_spec, whole],
        out_specs=half_spec,
        compiler_params=params,
        cost_estimate=pl.CostEstimate(flops=flops // 2, bytes_accessed=3 << 20, transcendentals=0),
        name="experts_own_half",
    )(hidden, down_weight)
    sums = call(
        chips_body,
        [shape((tall, width // 2), F32 if first and b == 0 else BF16) for b in range(blocks)],
        (keep, got),
        vmem=48 << 20,
        name="chip_sums",
        cost=(blocks * tall * width, 1 << 20),
    )
    return list(sums)


def on_device(
    tokens, attn_gain, query_weight, key_value_weight, paired_cache, prompt_length, group_index, offsets,
    sink_logit, out_weight, mixer_gain, routes, route_weight, copy_slot, gate_weight, up_weight, down_weight,
    final_gain,
):
    rows, width = tokens.shape
    dim = key_value_weight.shape[2]
    heads = query_weight.shape[1] // dim
    half, quarter = width // 2, width // 4
    slots = paired_cache.shape[2]
    copies = copy_slot.shape[0]
    peers = lax.axis_size("expert")
    extra_width = -(-(2 * copies + 2) // LANES) * LANES
    gate_weight = jnp.swapaxes(gate_weight, 1, 2)
    up_weight = jnp.swapaxes(up_weight, 1, 2)

    other_cache = swap(paired_cache[0, 0], "tensor", 1)
    place = shape((rows, LANES), I32)
    queries, own_new, own_cache, token_half, *places = call(
        project_body,
        [
            shape((heads * rows, dim), BF16), shape((rows, dim), BF16), shape((slots, dim), BF16),
            shape((rows, half), F32), place, place, place,
        ],
        (
            prompt_length, group_index, offsets, tokens, attn_gain[None, :], key_value_weight, query_weight,
            paired_cache,
        ),
        hbm=range(8),
        scratch=[
            pltpu.SMEM(prompt_length.shape, I32),
            pltpu.SMEM(group_index.shape, I32),
            pltpu.SMEM(offsets.shape, I32),
            pltpu.VMEM(tokens.shape, BF16),
            pltpu.VMEM((1, width), BF16),
            pltpu.VMEM(key_value_weight.shape[1:], BF16),
            pltpu.VMEM(query_weight.shape, BF16),
            pltpu.SemaphoreType.DMA((8,)),
        ],
        name="project",
        cost=(2 * rows * width * (heads + 1) * dim, 2 << 20),
    )
    other_new = swap(own_new, "tensor", 1)
    sums, tops, parts, extra = call(
        cached_body,
        [shape((heads * rows, dim), F32)] + [shape((heads * rows, LANES), F32)] * 2 + [shape((rows, extra_width), F32)],
        (
            queries, own_cache, other_cache, *places, sink_logit, routes.T, route_weight.T, copy_slot[None, :],
        ),
        hbm=range(6, 10),
        scratch=[
            pltpu.SMEM(sink_logit.shape, F32),
            pltpu.VMEM((TOP, rows), I32),
            pltpu.VMEM((TOP, rows), F32),
            pltpu.VMEM((1, copies), I32),
            pltpu.SemaphoreType.DMA((4,)),
        ],
        name="cached_attention",
        cost=(4 * heads * rows * dim * slots, 1 << 20),
    )
    send, keep = call(
        attend_body,
        [shape((rows, half), BF16), shape((rows, half + extra_width), F32)],
        (queries, own_new, other_new, sums, tops, parts, out_weight, token_half, extra),
        name="attention_out",
        cost=(2 * rows * heads * dim * width, 2 << 20),
    )
    own = call(
        chip_body, shape((rows, half + extra_width), BF16), (keep, swap(send, "tensor", 1)), name="chip_sum",
        cost=(rows * width, 1 << 18),
    )
    block, residual = call(
        functools.partial(residual_body, copies),
        [shape((2 * rows, half + extra_width), BF16), shape((rows, half), BF16)],
        (mixer_gain[None, :], own, swap(own, "tensor", 2), swap(own, "expert", 1), swap_both(own, 1, 2)),
        name="residual",
        cost=(rows * width, 1 << 18),
    )

    bit, stages = 2, []
    while bit < peers:
        stages.append([bit] if 2 * bit >= peers else [bit, 2 * bit, 3 * bit])
        bit *= 4
    blocks = [block]
    for stage in stages:
        whole = blocks[0] if len(blocks) == 1 else jnp.concatenate(blocks, axis=0)
        blocks = [whole] + [swap(whole, "expert", b) for b in stage]
    others = [swap(b, "tensor", 1) for b in blocks]
    pieces = []
    for i in range(0, len(blocks), 2):
        pieces += run_experts(
            blocks[i : i + 2], others[i : i + 2], gate_weight, up_weight, down_weight, copies, i == 0
        )
    terms = [pieces[0]] + [swap(p, "expert", b) for p, b in zip(pieces[1:], stages[-1])]
    for stage in stages[-2::-1]:
        tall = terms[0].shape[0] // (len(stage) + 1)
        pieces = call(
            functools.partial(pass_body, len(terms)),
            [shape((tall, half), F32)] + [shape((tall, half), BF16)] * len(stage),
            terms,
            vmem=48 << 20,
            name="pass_on",
            cost=(tall * width, 1 << 20),
        )
        terms = [pieces[0]] + [swap(p, "expert", b) for p, b in zip(pieces[1:], stage)]
    own, x_part, y_part = call(
        functools.partial(pair_body, len(terms)),
        [shape((rows, half), F32), shape((rows, half), BF16), shape((rows, half), BF16)],
        terms,
        name="z_sums",
        cost=(rows * width, 1 << 18),
    )
    combined, squares = call(
        combine_body,
        [shape((rows, quarter), F32), shape((rows, LANES), F32)],
        (own, swap(x_part, "tensor", 2), swap(y_part, "expert", 1), swap_both(y_part, 1, 2), residual),
        name="combine",
        cost=(rows * width, 1 << 18),
    )
    return call(
        functools.partial(finish_body, width),
        shape((rows, quarter), BF16),
        (combined, final_gain[None, :], squares, swap(squares, "tensor", 1)),
        name="finish",
        cost=(rows * width, 1 << 18),
    )


def solution(mesh):
    in_specs = (
        P("expert", None),
        P(),
        P(None, "tensor"),
        P("tensor", None, None),
        P("expert", "tensor", None, None),
        P("expert", None),
        P("expert"),
        P("expert"),
        P("tensor"),
        P("tensor", None),
        P(),
        P("expert", None),
        P("expert", None),
        P(),
        P("expert", None, "tensor"),
        P("expert", None, "tensor"),
        P("expert", "tensor", None),
        P("tensor"),
    )
    out_specs = P("expert", "tensor")
    return jax.shard_map(
        on_device, mesh=mesh, in_specs=in_specs, out_specs=out_specs, check_vma=False
    )
```

```python
import functools
import math

import jax
import jax.numpy as jnp
from jax import lax
from jax.experimental import pallas as pl
from jax.experimental.pallas import tpu as pltpu
from jax.sharding import PartitionSpec as P

EXPERTS = 32
TOP = 4
PROMPT_CAP = 256
WINDOW = 192
EPSILON = 1e-06
LANES = 128
CHUNKS = 4
HIDE = -1e30
F32 = jnp.float32
BF16 = jnp.bfloat16
I32 = jnp.int32


def swap(block, axis, bits):
    count = lax.axis_size(axis)
    return lax.ppermute(block, axis, [(i, i ^ bits) for i in range(count)])


def swap_both(block, expert_bits, tensor_bits):
    lanes = lax.axis_size("tensor")
    count = lax.axis_size("expert") * lanes
    bits = expert_bits * lanes + tensor_bits
    return lax.ppermute(block, ("expert", "tensor"), [(i, i ^ bits) for i in range(count)])


def iota(shape, dim):
    return lax.broadcasted_iota(I32, shape, dim)


def dot(a, b):
    return jnp.dot(a, b, preferred_element_type=F32)


def dot_t(a, b):
    return lax.dot_general(a, b, (((1,), (1,)), ((), ())), preferred_element_type=F32)


def call(body, outs, args, hbm=(), free=(), scratch=(), vmem=None, cost=None, name=None):
    in_specs = [
        pl.BlockSpec(memory_space=pltpu.HBM if i in hbm else pl.ANY if i in free else pltpu.VMEM)
        for i in range(len(args))
    ]
    args = [pltpu.with_memory_space_constraint(a, pltpu.HBM) if i in hbm else a for i, a in enumerate(args)]
    single = not isinstance(outs, (list, tuple))
    listed = [outs] if single else list(outs)
    out_specs = [pl.BlockSpec(memory_space=pltpu.VMEM) for _ in listed]
    flops, nbytes = cost or (0, 0)
    result = pl.pallas_call(
        body,
        out_shape=listed,
        in_specs=in_specs,
        out_specs=out_specs,
        scratch_shapes=list(scratch),
        compiler_params=pltpu.CompilerParams(vmem_limit_bytes=vmem or 16 << 20),
        cost_estimate=pl.CostEstimate(flops=flops, bytes_accessed=nbytes, transcendentals=0),
        name=name,
    )(*args)
    return result[0] if single else result


def shape(dims, dtype):
    return jax.ShapeDtypeStruct(tuple(dims), dtype)


def spread(rows, values):
    index = iota((rows, LANES), 0)
    total = jnp.full((rows, LANES), values[0], I32)
    for i in range(1, rows):
        total = jnp.where(index == i, values[i], total)
    return total


def is_key():
    return lax.axis_index("tensor") % 2 == 0


def is_first():
    return lax.axis_index("tensor") < 2


def project_body(
    length_hbm, group_hbm, offset_hbm, tok_hbm, gain_hbm, kvw_hbm, qw_hbm, cache_hbm,
    q_ref, own_ref, cache_ref, token_ref, group_out, length_out, position_out,
    length_ref, group_ref, offset_ref, tok_ref, gain_ref, kvw_ref, qw_ref, sems,
):
    rows, width = tok_ref.shape
    part = width // CHUNKS
    pairs = [
        (length_hbm, length_ref), (group_hbm, group_ref), (offset_hbm, offset_ref), (tok_hbm, tok_ref),
        (gain_hbm, gain_ref), (kvw_hbm.at[0], kvw_ref),
    ]
    pairs += [(qw_hbm.at[pl.ds(i * part, part)], qw_ref.at[pl.ds(i * part, part)]) for i in range(CHUNKS)]
    pairs += [(cache_hbm.at[0, 0], cache_ref)]
    loads = [pltpu.make_async_copy(src, dst, sems.at[i]) for i, (src, dst) in enumerate(pairs)]
    for load in loads:
        load.start()
    dim = kvw_ref.shape[1]
    heads = qw_ref.shape[1] // dim
    half = dim // 2
    quarter = width // 4
    for load in loads[:3]:
        load.wait()
    groups = [group_ref[i] for i in range(rows)]
    lengths = [length_ref[0, g] for g in groups]
    group_out[...] = spread(rows, groups)
    length_out[...] = spread(rows, lengths)
    position = spread(rows, [lengths[i] + offset_ref[i] for i in range(rows)])
    position_out[...] = position
    lane = iota((rows, dim), 1)
    step = jnp.where(lane >= half, lane - half, lane).astype(F32)
    angle = position.astype(F32) * jnp.exp(step * (-math.log(10000.0) / half))
    cosine = jnp.cos(angle)
    sine = jnp.sin(angle)
    sine = jnp.where(lane < half, -sine, sine)
    loads[3].wait()
    loads[4].wait()
    tok = tok_ref[...].astype(F32)
    mean = jnp.sum(tok * tok, axis=1, keepdims=True) / width
    normed = (tok * lax.rsqrt(mean + EPSILON) * gain_ref[...].astype(F32).reshape(1, width)).astype(BF16)
    for i in range(2):
        low, high = (tok[:, (2 * i + k) * quarter : (2 * i + k + 1) * quarter] for k in range(2))
        token_ref[:, i * quarter : (i + 1) * quarter] = jnp.where(
            is_first(), jnp.where(is_key(), low, high), 0.0
        )
    loads[5].wait()
    own = dot(normed, kvw_ref[...])
    turned = own * cosine + pltpu.roll(own, half, 1) * sine
    own_ref[...] = jnp.where(is_key(), turned, own).astype(BF16)
    q = None
    for i in range(CHUNKS):
        loads[6 + i].wait()
        part_sum = dot(normed[:, i * part : (i + 1) * part], qw_ref[i * part : (i + 1) * part, :])
        q = part_sum if q is None else q + part_sum
    for h in range(heads):
        head = q[:, h * dim : (h + 1) * dim]
        q_ref[h * rows : (h + 1) * rows, :] = (head * cosine + pltpu.roll(head, half, 1) * sine).astype(BF16)
    loads[-1].wait()


def cached_body(
    q_ref, mine_ref, theirs_ref, group_ref, length_ref, position_ref, sink_hbm, routes_hbm, weight_hbm, slot_hbm,
    sums_ref, tops_ref, parts_ref, extra_ref, sink_ref, routes_ref, weight_ref, slot_ref, sems,
):
    pairs = [(sink_hbm, sink_ref), (routes_hbm, routes_ref), (weight_hbm, weight_ref), (slot_hbm, slot_ref)]
    loads = [pltpu.make_async_copy(src, dst, sems.at[i]) for i, (src, dst) in enumerate(pairs)]
    for load in loads:
        load.start()
    rows = group_ref.shape[0]
    dim = q_ref.shape[1]
    heads = q_ref.shape[0] // rows
    slots = mine_ref.shape[0]
    scale = 1.0 / dim**0.5
    mine, theirs = mine_ref[...], theirs_ref[...]
    keys = jnp.where(is_key(), mine, theirs)
    values = jnp.where(is_key(), theirs, mine)
    scores = dot_t(q_ref[...], keys)
    group, row_length, position = group_ref[...], length_ref[...], position_ref[...]
    lane = iota((rows, LANES), 1)
    seen = []
    for start in range(0, slots, LANES):
        place = lane + start % PROMPT_CAP
        seen.append((group == start // PROMPT_CAP) & (place < row_length) & (place > position - WINDOW))
    for load in loads:
        load.wait()
    probs = []
    for h in range(heads):
        span = slice(h * rows, (h + 1) * rows)
        masked = [
            jnp.where(seen[k], scores[span, k * LANES : (k + 1) * LANES] * scale, HIDE) for k in range(len(seen))
        ]
        top = functools.reduce(jnp.maximum, masked)
        top = jnp.maximum(jnp.max(top, axis=1, keepdims=True), sink_ref[h])
        part = [jnp.exp(m - top) for m in masked]
        total = jnp.sum(functools.reduce(jnp.add, part), axis=1, keepdims=True) + jnp.exp(sink_ref[h] - top)
        probs.append(jnp.concatenate([p.astype(BF16) for p in part], axis=1))
        tops_ref[span, :] = jnp.broadcast_to(top, (rows, LANES))
        parts_ref[span, :] = jnp.broadcast_to(total, (rows, LANES))
    sums_ref[...] = dot(jnp.concatenate(probs, axis=0), values)
    copies = slot_ref.shape[1]
    replicas = copies // EXPERTS
    block = iota((copies, rows), 1) // (rows // replicas)
    place = iota((copies, rows), 0)
    chosen = jnp.zeros((copies, rows), F32)
    for k in range(TOP):
        named = routes_ref[k : k + 1, :] * replicas + block
        chosen = chosen + jnp.where(named == place, weight_ref[k : k + 1, :], 0.0)
    order = (iota((copies, copies), 0) == slot_ref[...]).astype(F32).astype(BF16)
    high = chosen.astype(BF16)
    low = (chosen - high.astype(F32)).astype(BF16)
    extra_ref[...] = jnp.zeros(extra_ref.shape, F32)
    for i, part in enumerate((high, low)):
        moved = lax.dot_general(part, order, (((0,), (1,)), ((), ())), preferred_element_type=F32)
        extra_ref[:, i * copies : (i + 1) * copies] = jnp.where(is_first(), moved, 0.0)


def attend_body(
    q_ref, mine_ref, theirs_ref, sums_ref, tops_ref, parts_ref, out_ref, token_ref, extra_ref, send_ref, keep_ref
):
    rows, dim = mine_ref.shape
    heads = q_ref.shape[0] // rows
    quarter = send_ref.shape[1] // 2
    scale = 1.0 / dim**0.5
    mine, theirs = mine_ref[...].astype(F32), theirs_ref[...].astype(F32)
    key = jnp.where(is_key(), mine, theirs)
    value = jnp.where(is_key(), theirs, mine)
    context = []
    for h in range(heads):
        span = slice(h * rows, (h + 1) * rows)
        score = jnp.sum(q_ref[span, :].astype(F32) * key, axis=1, keepdims=True) * scale
        top = jnp.maximum(tops_ref[span, :], score)
        old = jnp.exp(tops_ref[span, :] - top)
        own = jnp.exp(score - top)
        inverse = 1.0 / (parts_ref[span, :] * old + own)
        context.append(((sums_ref[span, :] * old + own * value) * inverse).astype(BF16))
    attended = dot(jnp.concatenate(context, axis=1), out_ref[...])
    part = [attended[:, i * quarter : (i + 1) * quarter] for i in range(4)]
    for i in range(2):
        span = slice(i * quarter, (i + 1) * quarter)
        send_ref[:, span] = jnp.where(is_key(), part[2 * i + 1], part[2 * i]).astype(BF16)
        keep_ref[:, span] = jnp.where(is_key(), part[2 * i], part[2 * i + 1]) + token_ref[:, span]
    keep_ref[:, 2 * quarter :] = extra_ref[...]


def chip_body(keep_ref, got_ref, out_ref):
    width = got_ref.shape[1]
    out_ref[:, :width] = (keep_ref[:, :width] + got_ref[...].astype(F32)).astype(BF16)
    out_ref[:, width:] = keep_ref[:, width:].astype(BF16)


def relay_body(count, *refs):
    for src, dst in zip(refs[:count], refs[-count:]):
        dst[...] = src[...]


def after_all(blocks, earlier):
    tall, total = blocks[0].shape
    return call(
        functools.partial(relay_body, len(blocks)),
        [shape(b.shape, b.dtype) for b in blocks],
        (*blocks, *earlier),
        free=range(len(blocks), len(blocks) + len(earlier)),
        vmem=16 << 20,
        name="relay",
        cost=(len(blocks) * tall * total, 1 << 18),
    )


def residual_body(copies, gain_ref, own_ref, x_ref, y_ref, xy_ref, loaded_ref, rows_ref, keep_ref):
    rows, total = own_ref.shape
    width = keep_ref.shape[1]
    quarter = width // 2
    gain = [gain_ref[:, i * quarter : (i + 1) * quarter] for i in range(4)]
    gain = [jnp.where(is_key(), gain[2 * i].astype(F32), gain[2 * i + 1].astype(F32)) for i in range(2)]
    lane = iota((rows, total - width), 1)
    for i, (a_ref, b_ref) in enumerate(((own_ref, x_ref), (y_ref, xy_ref))):
        span = slice(i * rows, (i + 1) * rows)
        squares = jnp.zeros((rows, 1), F32)
        for k in range(2):
            cols = slice(k * quarter, (k + 1) * quarter)
            part = (a_ref[:, cols].astype(F32) + b_ref[:, cols].astype(F32)).astype(BF16)
            wide = part.astype(F32)
            squares = squares + jnp.sum(wide * wide, axis=1, keepdims=True)
            rows_ref[span, cols] = (wide * gain[k]).astype(BF16)
            if i == 0:
                keep_ref[:, cols] = part
        extra = a_ref[:, width:].astype(F32) + b_ref[:, width:].astype(F32)
        high = squares.astype(BF16).astype(F32)
        extra = jnp.where(lane == 2 * copies, high, extra)
        extra = jnp.where(lane == 2 * copies + 1, squares - high, extra)
        rows_ref[span, width:] = extra.astype(BF16)


def load_body(*refs):
    sems = refs[-1]
    count = (len(refs) - 2) // 2
    loads = []
    for src, dst in zip(refs[1 : 1 + count], refs[1 + count : -1]):
        for j in range(src.shape[0]):
            loads.append(pltpu.make_async_copy(src.at[j], dst.at[j], sems.at[len(loads)]))
    for load in loads:
        load.start()
    for load in loads:
        load.wait()


def expert_body(copies, blocks, *refs):
    own_refs, other_refs = refs[:blocks], refs[blocks : 2 * blocks]
    gate_ref, up_ref, down_ref = refs[2 * blocks : 2 * blocks + 3]
    hidden_ref, send_ref = refs[-2:]
    hosted, units, width = gate_ref.shape
    quarter = width // 4
    own = jnp.concatenate([r[...] for r in own_refs], axis=0)
    other = jnp.concatenate([r[...] for r in other_refs], axis=0)
    parts = []
    for i in range(4):
        span = slice(i // 2 * quarter, (i // 2 + 1) * quarter)
        mine = is_key() if i % 2 == 0 else jnp.logical_not(is_key())
        parts.append(jnp.where(mine, own[:, span], other[:, span]))
    rows = jnp.concatenate(parts, axis=1)
    extra = own[:, 2 * quarter :].astype(F32)
    lane = iota(extra.shape, 1)
    squares = jnp.where((lane == 2 * copies) | (lane == 2 * copies + 1), extra + other[:, 2 * quarter :].astype(F32), 0.0)
    scale = lax.rsqrt(jnp.sum(squares, axis=1, keepdims=True) / width + EPSILON)
    tall = rows.shape[0] // blocks
    hiddens = []
    for j in range(hosted):
        slot = lax.axis_index("expert") * hosted + j
        weight = jnp.where((lane == slot) | (lane == slot + copies), extra, 0.0)
        weight = jnp.sum(weight, axis=1, keepdims=True)
        gate = dot_t(rows, gate_ref[j]) * scale
        up = dot_t(rows, up_ref[j]) * scale
        hidden = (jnp.maximum(gate, 0.0) * up * weight).astype(BF16)
        hiddens.append(hidden)
        for b in range(blocks):
            hidden_ref[j, b] = hidden[b * tall : (b + 1) * tall]
    for k in range(2):
        start = pl.multiple_of((2 * k + 1 - lax.axis_index("tensor") % 2) * quarter, LANES)
        total = None
        for j in range(hosted):
            part = dot(hiddens[j], down_ref[j, :, pl.ds(start, quarter)])
            total = part if total is None else total + part
        total = total.astype(BF16)
        for b in range(blocks):
            send_ref[b, :, k * quarter : (k + 1) * quarter] = total[b * tall : (b + 1) * tall]


def keep_body(blocks, hidden_ref, down_ref, out_ref):
    hosted = down_ref.shape[0]
    quarter = down_ref.shape[2] // 4
    tall = hidden_ref.shape[2]
    hiddens = [jnp.concatenate([hidden_ref[j, b] for b in range(blocks)], axis=0) for j in range(hosted)]
    for k in range(2):
        start = pl.multiple_of((2 * k + lax.axis_index("tensor") % 2) * quarter, LANES)
        total = None
        for j in range(hosted):
            part = dot(hiddens[j], down_ref[j, :, pl.ds(start, quarter)])
            total = part if total is None else total + part
        for b in range(blocks):
            out_ref[b, :, k * quarter : (k + 1) * quarter] = total[b * tall : (b + 1) * tall]


def chips_body(keep_ref, got_ref, *out_refs):
    for b, out_ref in enumerate(out_refs):
        out_ref[...] = (keep_ref[b] + got_ref[b].astype(F32)).astype(out_ref.dtype)


def pass_body(terms, *refs):
    total = refs[0][...]
    for r in refs[1:terms]:
        total = total + r[...].astype(F32)
    outs = refs[terms:]
    tall = total.shape[0] // len(outs)
    for i, r in enumerate(outs):
        r[...] = total[i * tall : (i + 1) * tall].astype(r.dtype)


def pair_body(terms, *refs):
    total = refs[0][...]
    for r in refs[1:terms]:
        total = total + r[...].astype(F32)
    own_ref, x_ref, y_ref = refs[terms:]
    rows = own_ref.shape[0]
    own_ref[...] = total[:rows]
    x_ref[...] = total[:rows].astype(BF16)
    y_ref[...] = total[rows:].astype(BF16)


def combine_body(own_ref, x_ref, y_ref, xy_ref, residual_ref, combined_ref, square_ref):
    quarter = combined_ref.shape[1]
    total = (own_ref[...] + x_ref[...].astype(F32)) + (y_ref[...].astype(F32) + xy_ref[...].astype(F32))
    total = residual_ref[...].astype(F32) + total
    combined_ref[...] = jnp.where(is_first(), total[:, :quarter], total[:, quarter:])
    square_ref[...] = jnp.broadcast_to(jnp.sum(total * total, axis=1, keepdims=True), square_ref.shape)


def finish_body(width, combined_ref, gain_ref, a_ref, b_ref, out_ref):
    mean = (a_ref[...] + b_ref[...])[:, :1] / width
    out_ref[...] = (combined_ref[...] * lax.rsqrt(mean + EPSILON) * gain_ref[...].astype(F32)).astype(BF16)


def run_experts(own, other, gate_weight, up_weight, down_weight, copies, first):
    blocks = len(own)
    tall, total = own[0].shape
    hosted, units, width = gate_weight.shape
    step = min(tall, 64)
    grid = (tall // step,) if tall > step else ()

    def spec(dims, place):
        if not grid:
            return pl.BlockSpec(memory_space=pltpu.VMEM)
        return pl.BlockSpec(dims, place)

    row_spec = spec((step, total), lambda i: (i, 0))
    half_spec = spec((blocks, step, width // 2), lambda i: (0, i, 0))
    hidden_spec = spec((hosted, blocks, step, units), lambda i: (0, 0, i, 0))
    whole = pl.BlockSpec(memory_space=pltpu.VMEM)
    params = pltpu.CompilerParams(vmem_limit_bytes=32 << 20)
    flops = 2 * blocks * tall * hosted * width * units
    hidden, send = pl.pallas_call(
        functools.partial(expert_body, copies, blocks),
        grid=grid,
        out_shape=[shape((hosted, blocks, tall, units), BF16), shape((blocks, tall, width // 2), BF16)],
        in_specs=[row_spec] * (2 * blocks) + [whole] * 3,
        out_specs=[hidden_spec, half_spec],
        compiler_params=params,
        cost_estimate=pl.CostEstimate(flops=1, bytes_accessed=1, transcendentals=0),
        name="experts",
    )(*own, *other, gate_weight, up_weight, down_weight)
    got = swap(send, "tensor", 1)
    keep = pl.pallas_call(
        functools.partial(keep_body, blocks),
        grid=grid,
        out_shape=shape((blocks, tall, width // 2), F32),
        in_specs=[hidden_spec, whole],
        out_specs=half_spec,
        compiler_params=params,
        cost_estimate=pl.CostEstimate(flops=1, bytes_accessed=1, transcendentals=0),
        name="experts_own_half",
    )(hidden, down_weight)
    sums = call(
        chips_body,
        [shape((tall, width // 2), F32 if first and b == 0 else BF16) for b in range(blocks)],
        (keep, got),
        vmem=48 << 20,
        name="chip_sums",
        cost=(1, 1),
    )
    return list(sums), send


def on_device(
    tokens, attn_gain, query_weight, key_value_weight, paired_cache, prompt_length, group_index, offsets,
    sink_logit, out_weight, mixer_gain, routes, route_weight, copy_slot, gate_weight, up_weight, down_weight,
    final_gain,
):
    rows, width = tokens.shape
    dim = key_value_weight.shape[2]
    heads = query_weight.shape[1] // dim
    half, quarter = width // 2, width // 4
    slots = paired_cache.shape[2]
    copies = copy_slot.shape[0]
    far = lax.axis_size("expert") // 2
    extra_width = -(-(2 * copies + 2) // LANES) * LANES
    gate_weight = jnp.swapaxes(gate_weight, 1, 2)
    up_weight = jnp.swapaxes(up_weight, 1, 2)

    other_cache = swap(paired_cache[0, 0], "tensor", 1)
    place = shape((rows, LANES), I32)
    queries, own_new, own_cache, token_half, *places = call(
        project_body,
        [
            shape((heads * rows, dim), BF16), shape((rows, dim), BF16), shape((slots, dim), BF16),
            shape((rows, half), F32), place, place, place,
        ],
        (
            prompt_length, group_index, offsets, tokens, attn_gain, key_value_weight, query_weight,
            paired_cache,
        ),
        hbm=range(8),
        scratch=[
            pltpu.SMEM(prompt_length.shape, I32),
            pltpu.SMEM(group_index.shape, I32),
            pltpu.SMEM(offsets.shape, I32),
            pltpu.VMEM(tokens.shape, BF16),
            pltpu.VMEM((width,), BF16),
            pltpu.VMEM(key_value_weight.shape[1:], BF16),
            pltpu.VMEM(query_weight.shape, BF16),
            pltpu.SemaphoreType.DMA((7 + CHUNKS,)),
        ],
        name="project",
        cost=(2 * rows * width * (heads + 1) * dim, 2 << 20),
    )
    other_new = swap(own_new, "tensor", 1)
    sums, tops, parts, extra = call(
        cached_body,
        [shape((heads * rows, dim), F32)] + [shape((heads * rows, LANES), F32)] * 2 + [shape((rows, extra_width), F32)],
        (
            queries, own_cache, other_cache, *places, sink_logit, routes.T, route_weight.T, copy_slot[None, :],
        ),
        hbm=range(6, 10),
        scratch=[
            pltpu.SMEM(sink_logit.shape, F32),
            pltpu.VMEM((TOP, rows), I32),
            pltpu.VMEM((TOP, rows), F32),
            pltpu.VMEM((1, copies), I32),
            pltpu.SemaphoreType.DMA((4,)),
        ],
        name="cached_attention",
        cost=(4 * heads * rows * dim * slots, 1 << 20),
    )
    send, keep = call(
        attend_body,
        [shape((rows, half), BF16), shape((rows, half + extra_width), F32)],
        (queries, own_new, other_new, sums, tops, parts, out_weight, token_half, extra),
        name="attention_out",
        cost=(2 * rows * heads * dim * width, 2 << 20),
    )
    own = call(
        chip_body, shape((rows, half + extra_width), BF16), (keep, swap(send, "tensor", 1)), name="chip_sum",
        cost=(rows * width, 1 << 18),
    )
    weights = (gate_weight, up_weight, down_weight)
    weights = call(
        load_body,
        [shape(w.shape, BF16) for w in weights],
        (own, *weights),
        hbm=range(1, 4),
        scratch=[pltpu.SemaphoreType.DMA((sum(w.shape[0] for w in weights),))],
        name="load_experts",
        cost=(0, 8 << 20),
    )
    block, residual = call(
        functools.partial(residual_body, copies),
        [shape((2 * rows, half + extra_width), BF16), shape((rows, half), BF16)],
        (mixer_gain[None, :], own, swap(own, "tensor", 2), swap(own, "expert", far), swap_both(own, far, 2), weights[0]),
        free=[5],
        name="residual",
        cost=(rows * width, 1 << 18),
    )

    bit, stages = 1, []
    while bit < far:
        stages.append([bit] if 2 * bit >= far else [bit, 2 * bit, 3 * bit])
        bit *= 4
    blocks = [block]
    for stage in stages:
        whole = blocks[0] if len(blocks) == 1 else jnp.concatenate(blocks, axis=0)
        blocks = [whole] + [swap(whole, "expert", b) for b in stage]
    pieces = []
    for group in (blocks[:1], blocks[1:]):
        if pieces:
            group = after_all(group, [send])
        others = [swap(b, "tensor", 1) for b in group]
        sums, send = run_experts(group, others, *weights, copies, not pieces)
        pieces += sums
    terms = [pieces[0]] + [swap(p, "expert", b) for p, b in zip(pieces[1:], stages[-1])]
    for stage in stages[-2::-1]:
        tall = terms[0].shape[0] // (len(stage) + 1)
        pieces = call(
            functools.partial(pass_body, len(terms)),
            [shape((tall, half), F32)] + [shape((tall, half), BF16)] * len(stage),
            terms,
            vmem=48 << 20,
            name="pass_on",
            cost=(tall * width, 1 << 20),
        )
        terms = [pieces[0]] + [swap(p, "expert", b) for p, b in zip(pieces[1:], stage)]
    own, x_part, far_part = call(
        functools.partial(pair_body, len(terms)),
        [shape((rows, half), F32), shape((rows, half), BF16), shape((rows, half), BF16)],
        terms,
        name="z_sums",
        cost=(rows * width, 1 << 18),
    )
    combined, squares = call(
        combine_body,
        [shape((rows, quarter), F32), shape((rows, LANES), F32)],
        (own, swap(x_part, "tensor", 2), swap(far_part, "expert", far), swap_both(far_part, far, 2), residual),
        name="combine",
        cost=(rows * width, 1 << 18),
    )
    return call(
        functools.partial(finish_body, width),
        shape((rows, quarter), BF16),
        (combined, final_gain[None, :], squares, swap(squares, "tensor", 1)),
        name="finish",
        cost=(rows * width, 1 << 18),
    )


def solution(mesh):
    in_specs = (
        P("expert", None),
        P(),
        P(None, "tensor"),
        P("tensor", None, None),
        P("expert", "tensor", None, None),
        P("expert", None),
        P("expert"),
        P("expert"),
        P("tensor"),
        P("tensor", None),
        P(),
        P("expert", None),
        P("expert", None),
        P(),
        P("expert", None, "tensor"),
        P("expert", None, "tensor"),
        P("expert", "tensor", None),
        P("tensor"),
    )
    out_specs = P("expert", "tensor")
    return jax.shard_map(
        on_device, mesh=mesh, in_specs=in_specs, out_specs=out_specs, check_vma=False
    )
```

```python
import functools
import math

import jax
import jax.numpy as jnp
from jax import lax
from jax.experimental import pallas as pl
from jax.experimental.pallas import tpu as pltpu
from jax.sharding import PartitionSpec as P

EXPERTS = 32
TOP = 4
PROMPT_CAP = 256
WINDOW = 192
EPSILON = 1e-06
LANES = 128
CHUNKS = 4
HIDE = -1e30
F32 = jnp.float32
BF16 = jnp.bfloat16
I32 = jnp.int32


def swap(block, axis, bits):
    count = lax.axis_size(axis)
    return lax.ppermute(block, axis, [(i, i ^ bits) for i in range(count)])


def swap_both(block, expert_bits, tensor_bits):
    lanes = lax.axis_size("tensor")
    count = lax.axis_size("expert") * lanes
    bits = expert_bits * lanes + tensor_bits
    return lax.ppermute(block, ("expert", "tensor"), [(i, i ^ bits) for i in range(count)])


def iota(shape, dim):
    return lax.broadcasted_iota(I32, shape, dim)


def dot(a, b):
    return jnp.dot(a, b, preferred_element_type=F32)


def dot_t(a, b):
    return lax.dot_general(a, b, (((1,), (1,)), ((), ())), preferred_element_type=F32)


def call(body, outs, args, hbm=(), free=(), scratch=(), vmem=None, cost=None, name=None):
    in_specs = [
        pl.BlockSpec(memory_space=pltpu.HBM if i in hbm else pl.ANY if i in free else pltpu.VMEM)
        for i in range(len(args))
    ]
    args = [pltpu.with_memory_space_constraint(a, pltpu.HBM) if i in hbm else a for i, a in enumerate(args)]
    single = not isinstance(outs, (list, tuple))
    listed = [outs] if single else list(outs)
    out_specs = [pl.BlockSpec(memory_space=pltpu.VMEM) for _ in listed]
    flops, nbytes = cost or (0, 0)
    result = pl.pallas_call(
        body,
        out_shape=listed,
        in_specs=in_specs,
        out_specs=out_specs,
        scratch_shapes=list(scratch),
        compiler_params=pltpu.CompilerParams(vmem_limit_bytes=vmem or 16 << 20),
        cost_estimate=pl.CostEstimate(flops=flops, bytes_accessed=nbytes, transcendentals=0),
        name=name,
    )(*args)
    return result[0] if single else result


def shape(dims, dtype):
    return jax.ShapeDtypeStruct(tuple(dims), dtype)


def spread(rows, values):
    index = iota((rows, LANES), 0)
    total = jnp.full((rows, LANES), values[0])
    for i in range(1, len(values)):
        total = jnp.where(index == i, values[i], total)
    return total


def is_key():
    return lax.axis_index("tensor") % 2 == 0


def is_first():
    return lax.axis_index("tensor") < 2


def project_body(
    length_hbm, group_hbm, offset_hbm, tok_hbm, gain_hbm, kvw_hbm, qw_hbm, cache_hbm, routes_hbm, weight_hbm,
    slot_hbm, sink_hbm,
    q_ref, own_ref, normed_ref, cosine_ref, sine_ref, cache_ref, token_ref, group_out, length_out, position_out,
    sink_out, routes_ref, weight_ref, slot_ref,
    length_ref, group_ref, offset_ref, sink_ref, tok_ref, gain_ref, kvw_ref, qw_ref, sems,
):
    rows, width = tok_ref.shape
    pairs = [
        (length_hbm, length_ref), (group_hbm, group_ref), (offset_hbm, offset_ref), (tok_hbm, tok_ref),
        (gain_hbm, gain_ref), (kvw_hbm.at[0], kvw_ref), (routes_hbm, routes_ref), (weight_hbm, weight_ref),
        (slot_hbm, slot_ref), (sink_hbm, sink_ref),
    ]
    pairs += [(qw_hbm, qw_ref), (cache_hbm.at[0, 0], cache_ref)]
    loads = [pltpu.make_async_copy(src, dst, sems.at[i]) for i, (src, dst) in enumerate(pairs)]
    for load in loads:
        load.start()
    dim = kvw_ref.shape[1]
    heads = qw_ref.shape[1] // dim
    half = dim // 2
    quarter = width // 4
    for load in loads[:3]:
        load.wait()
    groups = [group_ref[i] for i in range(rows)]
    lengths = [length_ref[0, g] for g in groups]
    group_out[...] = spread(rows, groups)
    length_out[...] = spread(rows, lengths)
    position = spread(rows, [lengths[i] + offset_ref[i] for i in range(rows)])
    position_out[...] = position
    lane = iota((rows, dim), 1)
    step = jnp.where(lane >= half, lane - half, lane).astype(F32)
    angle = position.astype(F32) * jnp.exp(step * (-math.log(10000.0) / half))
    cosine = jnp.cos(angle)
    sine = jnp.sin(angle)
    sine = jnp.where(lane < half, -sine, sine)
    cosine_ref[...] = cosine
    sine_ref[...] = sine
    loads[3].wait()
    loads[4].wait()
    tok = tok_ref[...].astype(F32)
    mean = jnp.sum(tok * tok, axis=1, keepdims=True) / width
    normed = (tok * lax.rsqrt(mean + EPSILON) * gain_ref[...].astype(F32).reshape(1, width)).astype(BF16)
    for i in range(2):
        low, high = (tok[:, (2 * i + k) * quarter : (2 * i + k + 1) * quarter] for k in range(2))
        token_ref[:, i * quarter : (i + 1) * quarter] = jnp.where(
            is_first(), jnp.where(is_key(), low, high), 0.0
        )
    normed_ref[...] = normed
    loads[9].wait()
    sink_out[...] = spread(sink_out.shape[0], [sink_ref[i] for i in range(heads)])
    loads[5].wait()
    own = dot(normed, kvw_ref[...])
    turned = own * cosine + pltpu.roll(own, half, 1) * sine
    own_ref[...] = jnp.where(is_key(), turned, own).astype(BF16)
    loads[10].wait()
    q = dot(normed, qw_ref[...])
    for h in range(heads):
        head = q[:, h * dim : (h + 1) * dim]
        q_ref[h * rows : (h + 1) * rows, :] = (head * cosine + pltpu.roll(head, half, 1) * sine).astype(BF16)
    for load in loads[6:9] + loads[11:]:
        load.wait()


def extra_body(routes_ref, weight_ref, slot_ref, sent_ref, extra_ref):
    rows = routes_ref.shape[1]
    copies = slot_ref.shape[1]
    replicas = copies // EXPERTS
    block = iota((copies, rows), 1) // (rows // replicas)
    place = iota((copies, rows), 0)
    chosen = jnp.zeros((copies, rows), F32)
    for k in range(TOP):
        named = routes_ref[k : k + 1, :] * replicas + block
        chosen = chosen + jnp.where(named == place, weight_ref[k : k + 1, :], 0.0)
    order = (iota((copies, copies), 0) == slot_ref[...]).astype(F32).astype(BF16)
    high = chosen.astype(BF16)
    low = (chosen - high.astype(F32)).astype(BF16)
    extra_ref[...] = jnp.zeros(extra_ref.shape, F32)
    for i, term in enumerate((high, low)):
        moved = lax.dot_general(term, order, (((0,), (1,)), ((), ())), preferred_element_type=F32)
        extra_ref[:, i * copies : (i + 1) * copies] = jnp.where(is_first(), moved, 0.0)


def attend_body(
    q_ref, own_ref, normed_ref, other_ref, cosine_ref, sine_ref, mine_ref, theirs_ref, group_ref, length_ref,
    position_ref, sink_ref, out_ref, token_ref, send_ref, keep_ref,
):
    rows, dim = own_ref.shape
    heads = q_ref.shape[0] // rows
    slots = mine_ref.shape[0]
    quarter = send_ref.shape[1] // 2
    scale = 1.0 / dim**0.5
    mine, theirs = mine_ref[...], theirs_ref[...]
    keys = jnp.where(is_key(), mine, theirs)
    values = jnp.where(is_key(), theirs, mine)
    scores = dot_t(q_ref[...], keys)
    other = dot(normed_ref[...], other_ref[...])
    turned = other * cosine_ref[...] + pltpu.roll(other, dim // 2, 1) * sine_ref[...]
    other = jnp.where(is_key(), other, turned).astype(BF16).astype(F32)
    own = own_ref[...].astype(F32)
    key = jnp.where(is_key(), own, other)
    value = jnp.where(is_key(), other, own)
    group, row_length, position = group_ref[...], length_ref[...], position_ref[...]
    lane = iota((rows, LANES), 1)
    seen = []
    for start in range(0, slots, LANES):
        place = lane + start % PROMPT_CAP
        seen.append((group == start // PROMPT_CAP) & (place < row_length) & (place > position - WINDOW))
    probs, own_probs = [], []
    for h in range(heads):
        span = slice(h * rows, (h + 1) * rows)
        masked = [
            jnp.where(seen[k], scores[span, k * LANES : (k + 1) * LANES] * scale, HIDE) for k in range(len(seen))
        ]
        sink = sink_ref[h : h + 1, :1]
        score = jnp.sum(q_ref[span, :].astype(F32) * key, axis=1, keepdims=True) * scale
        top = jnp.max(functools.reduce(jnp.maximum, masked), axis=1, keepdims=True)
        top = jnp.maximum(jnp.maximum(top, score), sink)
        part = [jnp.exp(m - top) for m in masked]
        fresh = jnp.exp(score - top)
        total = jnp.sum(functools.reduce(jnp.add, part), axis=1, keepdims=True) + fresh + jnp.exp(sink - top)
        inverse = 1.0 / total
        probs.append(jnp.concatenate([(p * inverse).astype(BF16) for p in part], axis=1))
        own_probs.append((fresh * inverse).astype(BF16).astype(F32))
    cached = dot(jnp.concatenate(probs, axis=0), values)
    context = [
        (cached[h * rows : (h + 1) * rows] + own_probs[h] * value).astype(BF16) for h in range(heads)
    ]
    attended = dot(jnp.concatenate(context, axis=1), out_ref[...])
    part = [attended[:, i * quarter : (i + 1) * quarter] for i in range(4)]
    for i in range(2):
        span = slice(i * quarter, (i + 1) * quarter)
        send_ref[:, span] = jnp.where(is_key(), part[2 * i + 1], part[2 * i]).astype(BF16)
        keep_ref[:, span] = jnp.where(is_key(), part[2 * i], part[2 * i + 1]) + token_ref[:, span]


def chip_body(keep_ref, extra_ref, got_ref, out_ref):
    width = got_ref.shape[1]
    out_ref[:, :width] = (keep_ref[...] + got_ref[...].astype(F32)).astype(BF16)
    out_ref[:, width:] = extra_ref[...].astype(BF16)


def relay_body(block_ref, *refs):
    refs[-1][...] = block_ref[...]


def after_all(block, earlier):
    return call(
        relay_body,
        shape(block.shape, block.dtype),
        (block, *earlier),
        free=range(1, 1 + len(earlier)),
        name="relay",
        cost=(block.size, 1 << 17),
    )


def residual_body(copies, gain_ref, own_ref, y_ref, xy_ref, x_ref, loaded_ref, rows_ref, keep_ref):
    rows, total = own_ref.shape
    width = keep_ref.shape[1]
    quarter = width // 2
    gain = [gain_ref[:, i * quarter : (i + 1) * quarter] for i in range(4)]
    gain = [jnp.where(is_key(), gain[2 * i].astype(F32), gain[2 * i + 1].astype(F32)) for i in range(2)]
    lane = iota((rows, total - width), 1)
    for i, (a_ref, b_ref) in enumerate(((own_ref, x_ref), (y_ref, xy_ref))):
        span = slice(i * rows, (i + 1) * rows)
        squares = jnp.zeros((rows, 1), F32)
        for k in range(2):
            cols = slice(k * quarter, (k + 1) * quarter)
            part = (a_ref[:, cols].astype(F32) + b_ref[:, cols].astype(F32)).astype(BF16)
            wide = part.astype(F32)
            squares = squares + jnp.sum(wide * wide, axis=1, keepdims=True)
            rows_ref[span, cols] = (wide * gain[k]).astype(BF16)
            if i == 0:
                keep_ref[:, cols] = part
        extra = a_ref[:, width:].astype(F32) + b_ref[:, width:].astype(F32)
        high = squares.astype(BF16).astype(F32)
        extra = jnp.where(lane == 2 * copies, high, extra)
        extra = jnp.where(lane == 2 * copies + 1, squares - high, extra)
        rows_ref[span, width:] = extra.astype(BF16)


def load_body(*refs):
    sems = refs[-1]
    count = (len(refs) - 2) // 2
    loads = []
    for src, dst in zip(refs[1 : 1 + count], refs[1 + count : -1]):
        tall = src.shape[0] // CHUNKS
        for k in range(CHUNKS):
            part = pl.ds(k * tall, tall)
            loads.append(pltpu.make_async_copy(src.at[part], dst.at[part], sems.at[len(loads)]))
    for load in loads:
        load.start()
    for load in loads:
        load.wait()


def expert_body(copies, hosted, blocks, *refs):
    own_refs, other_refs = refs[:blocks], refs[blocks : 2 * blocks]
    gate_ref, up_ref, down_ref = refs[2 * blocks : 2 * blocks + 3]
    hidden_ref, send_ref = refs[-2:]
    width = gate_ref.shape[1]
    units = gate_ref.shape[0] // hosted
    quarter = width // 4
    own = jnp.concatenate([r[...] for r in own_refs], axis=0)
    other = jnp.concatenate([r[...] for r in other_refs], axis=0)
    parts = []
    for i in range(4):
        span = slice(i // 2 * quarter, (i // 2 + 1) * quarter)
        mine = is_key() if i % 2 == 0 else jnp.logical_not(is_key())
        parts.append(jnp.where(mine, own[:, span], other[:, span]))
    rows = jnp.concatenate(parts, axis=1)
    extra = own[:, 2 * quarter :].astype(F32)
    lane = iota(extra.shape, 1)
    squares = jnp.where((lane == 2 * copies) | (lane == 2 * copies + 1), extra + other[:, 2 * quarter :].astype(F32), 0.0)
    scale = lax.rsqrt(jnp.sum(squares, axis=1, keepdims=True) / width + EPSILON)
    tall = rows.shape[0] // blocks
    parts = []
    for j in range(hosted):
        slot = lax.axis_index("expert") * hosted + j
        one = jnp.where((lane == slot) | (lane == slot + copies), extra, 0.0)
        weight = jnp.sum(one, axis=1, keepdims=True)
        span = slice(j * units, (j + 1) * units)
        gate = dot_t(rows, gate_ref[span, :]) * scale
        up = dot_t(rows, up_ref[span, :]) * scale
        parts.append((jnp.maximum(gate, 0.0) * up * weight).astype(BF16))
    hidden = jnp.concatenate(parts, axis=1)
    for b in range(blocks):
        hidden_ref[b] = hidden[b * tall : (b + 1) * tall]
    for k in range(2):
        start = pl.multiple_of((2 * k + 1 - lax.axis_index("tensor") % 2) * quarter, LANES)
        total = dot(hidden, down_ref[:, pl.ds(start, quarter)]).astype(BF16)
        for b in range(blocks):
            send_ref[b, :, k * quarter : (k + 1) * quarter] = total[b * tall : (b + 1) * tall]


def keep_body(blocks, hidden_ref, down_ref, out_ref):
    quarter = down_ref.shape[1] // 4
    tall = hidden_ref.shape[1]
    hidden = jnp.concatenate([hidden_ref[b] for b in range(blocks)], axis=0)
    for k in range(2):
        start = pl.multiple_of((2 * k + lax.axis_index("tensor") % 2) * quarter, LANES)
        total = dot(hidden, down_ref[:, pl.ds(start, quarter)])
        for b in range(blocks):
            out_ref[b, :, k * quarter : (k + 1) * quarter] = total[b * tall : (b + 1) * tall]


def chips_body(keep_ref, got_ref, *out_refs):
    for b, out_ref in enumerate(out_refs):
        out_ref[...] = (keep_ref[b] + got_ref[b].astype(F32)).astype(out_ref.dtype)


def pass_body(terms, *refs):
    total = refs[0][...]
    for r in refs[1:terms]:
        total = total + r[...].astype(F32)
    outs = refs[terms:]
    tall = total.shape[0] // len(outs)
    for i, r in enumerate(outs):
        r[...] = total[i * tall : (i + 1) * tall].astype(r.dtype)


def pair_body(terms, *refs):
    total = refs[0][...]
    for r in refs[1:terms]:
        total = total + r[...].astype(F32)
    own_ref, x_ref, y_ref = refs[terms:]
    rows = own_ref.shape[0]
    own_ref[...] = total[:rows]
    x_ref[...] = total[:rows].astype(BF16)
    y_ref[...] = total[rows:].astype(BF16)


def combine_body(own_ref, x_ref, y_ref, xy_ref, residual_ref, combined_ref, square_ref):
    quarter = combined_ref.shape[1]
    total = (own_ref[...] + x_ref[...].astype(F32)) + (y_ref[...].astype(F32) + xy_ref[...].astype(F32))
    total = residual_ref[...].astype(F32) + total
    combined_ref[...] = jnp.where(is_first(), total[:, :quarter], total[:, quarter:])
    square_ref[...] = jnp.broadcast_to(jnp.sum(total * total, axis=1, keepdims=True), square_ref.shape)


def finish_body(width, combined_ref, gain_ref, a_ref, b_ref, out_ref):
    mean = (a_ref[...] + b_ref[...])[:, :1] / width
    out_ref[...] = (combined_ref[...] * lax.rsqrt(mean + EPSILON) * gain_ref[...].astype(F32)).astype(BF16)


def run_experts(own, other, gate_weight, up_weight, down_weight, hosted, copies, first):
    blocks = len(own)
    tall, total = own[0].shape
    units, width = gate_weight.shape
    step = min(tall, 64)
    grid = (tall // step,) if tall > step else ()

    def spec(dims, place):
        if not grid:
            return pl.BlockSpec(memory_space=pltpu.VMEM)
        return pl.BlockSpec(dims, place)

    row_spec = spec((step, total), lambda i: (i, 0))
    half_spec = spec((blocks, step, width // 2), lambda i: (0, i, 0))
    hidden_spec = spec((blocks, step, units), lambda i: (0, i, 0))
    whole = pl.BlockSpec(memory_space=pltpu.VMEM)
    params = pltpu.CompilerParams(vmem_limit_bytes=32 << 20)
    hidden, send = pl.pallas_call(
        functools.partial(expert_body, copies, hosted, blocks),
        grid=grid,
        out_shape=[shape((blocks, tall, units), BF16), shape((blocks, tall, width // 2), BF16)],
        in_specs=[row_spec] * (2 * blocks) + [whole] * 3,
        out_specs=[hidden_spec, half_spec],
        compiler_params=params,
        cost_estimate=pl.CostEstimate(flops=1, bytes_accessed=1, transcendentals=0),
        name="experts",
    )(*own, *other, gate_weight, up_weight, down_weight)
    got = swap(send, "tensor", 1)
    keep = pl.pallas_call(
        functools.partial(keep_body, blocks),
        grid=grid,
        out_shape=shape((blocks, tall, width // 2), F32),
        in_specs=[hidden_spec, whole],
        out_specs=half_spec,
        compiler_params=params,
        cost_estimate=pl.CostEstimate(flops=1, bytes_accessed=1, transcendentals=0),
        name="experts_own_half",
    )(hidden, down_weight)
    sums = call(
        chips_body,
        [shape((tall, width // 2), F32 if first and b == 0 else BF16) for b in range(blocks)],
        (keep, got),
        vmem=48 << 20,
        name="chip_sums",
        cost=(1, 1),
    )
    return list(sums), send, got


def on_device(
    tokens, attn_gain, query_weight, key_value_weight, paired_cache, prompt_length, group_index, offsets,
    sink_logit, out_weight, mixer_gain, routes, route_weight, copy_slot, gate_weight, up_weight, down_weight,
    final_gain,
):
    rows, width = tokens.shape
    dim = key_value_weight.shape[2]
    heads = query_weight.shape[1] // dim
    half, quarter = width // 2, width // 4
    slots = paired_cache.shape[2]
    copies = copy_slot.shape[0]
    far = lax.axis_size("expert") // 2
    extra_width = -(-(2 * copies + 2) // LANES) * LANES
    hosted = gate_weight.shape[0]
    gate_weight = jnp.swapaxes(gate_weight, 1, 2).reshape(-1, width)
    up_weight = jnp.swapaxes(up_weight, 1, 2).reshape(-1, width)
    down_weight = down_weight.reshape(-1, width)

    other_cache = swap(paired_cache[0, 0], "tensor", 1)
    other_weight = swap(key_value_weight[0], "tensor", 1)
    place = shape((rows, LANES), I32)
    turn = shape((rows, dim), F32)
    queries, own_new, normed, cosine, sine, own_cache, token_half, *rest, named, named_weight, slot = call(
        project_body,
        [
            shape((heads * rows, dim), BF16), shape((rows, dim), BF16), shape((rows, width), BF16), turn, turn,
            shape((slots, dim), BF16), shape((rows, half), F32), place, place, place, shape((8, LANES), F32),
            shape((TOP, rows), I32), shape((TOP, rows), F32), shape((1, copies), I32),
        ],
        (
            prompt_length, group_index, offsets, tokens, attn_gain, key_value_weight, query_weight,
            paired_cache, routes.T, route_weight.T, copy_slot[None, :], sink_logit,
        ),
        hbm=range(12),
        scratch=[
            pltpu.SMEM(prompt_length.shape, I32),
            pltpu.SMEM(group_index.shape, I32),
            pltpu.SMEM(offsets.shape, I32),
            pltpu.SMEM(sink_logit.shape, F32),
            pltpu.VMEM(tokens.shape, BF16),
            pltpu.VMEM((width,), BF16),
            pltpu.VMEM(key_value_weight.shape[1:], BF16),
            pltpu.VMEM(query_weight.shape, BF16),
            pltpu.SemaphoreType.DMA((12,)),
        ],
        name="project",
        cost=(2 * rows * width * (heads + 1) * dim, 2 << 20),
    )
    send, keep = call(
        attend_body,
        [shape((rows, half), BF16), shape((rows, half), F32)],
        (queries, own_new, normed, other_weight, cosine, sine, own_cache, other_cache, *rest, out_weight, token_half),
        name="attention",
        cost=(4 * heads * rows * dim * slots, 1 << 20),
    )
    extra = call(
        extra_body,
        shape((rows, extra_width), F32),
        (named, named_weight, slot, send),
        free=[3],
        name="route_columns",
    )
    own = call(
        chip_body, shape((rows, half + extra_width), BF16), (keep, extra, swap(send, "tensor", 1)), name="chip_sum",
        cost=(rows * width, 1 << 18),
    )
    far_y, far_xy, near_x = swap(own, "expert", far), swap_both(own, far, 2), swap(own, "tensor", 2)
    weights = (gate_weight, up_weight, down_weight)
    weights = call(
        load_body,
        [shape(w.shape, BF16) for w in weights],
        (own, *weights),
        hbm=range(1, 4),
        scratch=[pltpu.SemaphoreType.DMA((len(weights) * CHUNKS,))],
        name="load_experts",
        cost=(0, 8 << 20),
    )
    block, residual = call(
        functools.partial(residual_body, copies),
        [shape((2 * rows, half + extra_width), BF16), shape((rows, half), BF16)],
        (mixer_gain[None, :], own, far_y, far_xy, near_x, weights[0]),
        free=[5],
        name="residual",
        cost=(rows * width, 1 << 18),
    )

    bit, stages = 1, []
    while bit < far:
        stages.append([bit] if 2 * bit >= far else [bit, 2 * bit, 3 * bit])
        bit *= 4
    blocks = [block]
    for stage in stages:
        whole = blocks[0] if len(blocks) == 1 else jnp.concatenate(blocks, axis=0)
        blocks = [whole] + [swap(whole, "expert", b) for b in stage]
    pieces = []
    for group in (blocks[:1], blocks[1:]):
        if pieces:
            group = [after_all(b, [got if i else send]) for i, b in enumerate(group)]
        others = [swap(b, "tensor", 1) for b in group]
        sums, send, got = run_experts(group, others, *weights, hosted, copies, not pieces)
        pieces += sums
    terms = [pieces[0]] + [swap(p, "expert", b) for p, b in zip(pieces[1:], stages[-1])]
    for stage in stages[-2::-1]:
        tall = terms[0].shape[0] // (len(stage) + 1)
        pieces = call(
            functools.partial(pass_body, len(terms)),
            [shape((tall, half), F32)] + [shape((tall, half), BF16)] * len(stage),
            terms,
            vmem=48 << 20,
            name="pass_on",
            cost=(tall * width, 1 << 20),
        )
        terms = [pieces[0]] + [swap(p, "expert", b) for p, b in zip(pieces[1:], stage)]
    own, x_part, far_part = call(
        functools.partial(pair_body, len(terms)),
        [shape((rows, half), F32), shape((rows, half), BF16), shape((rows, half), BF16)],
        terms,
        name="z_sums",
        cost=(rows * width, 1 << 18),
    )
    far_y, far_xy, near_x = swap(far_part, "expert", far), swap_both(far_part, far, 2), swap(x_part, "tensor", 2)
    combined, squares = call(
        combine_body,
        [shape((rows, quarter), F32), shape((rows, LANES), F32)],
        (own, near_x, far_y, far_xy, residual),
        name="combine",
        cost=(rows * width, 1 << 18),
    )
    return call(
        functools.partial(finish_body, width),
        shape((rows, quarter), BF16),
        (combined, final_gain[None, :], squares, swap(squares, "tensor", 1)),
        name="finish",
        cost=(rows * width, 1 << 18),
    )


def solution(mesh):
    in_specs = (
        P("expert", None),
        P(),
        P(None, "tensor"),
        P("tensor", None, None),
        P("expert", "tensor", None, None),
        P("expert", None),
        P("expert"),
        P("expert"),
        P("tensor"),
        P("tensor", None),
        P(),
        P("expert", None),
        P("expert", None),
        P(),
        P("expert", None, "tensor"),
        P("expert", None, "tensor"),
        P("expert", "tensor", None),
        P("tensor"),
    )
    out_specs = P("expert", "tensor")
    return jax.shard_map(
        on_device, mesh=mesh, in_specs=in_specs, out_specs=out_specs, check_vma=False
    )
```

```python
import functools
import math

import jax
import jax.numpy as jnp
from jax import lax
from jax.experimental import pallas as pl
from jax.experimental.pallas import tpu as pltpu
from jax.sharding import PartitionSpec as P

EXPERTS = 32
TOP = 4
PROMPT_CAP = 256
WINDOW = 192
EPSILON = 1e-06
LANES = 128
CHUNKS = 4
HIDE = -1e30
F32 = jnp.float32
BF16 = jnp.bfloat16
I32 = jnp.int32


def swap(block, axis, bits):
    count = lax.axis_size(axis)
    return lax.ppermute(block, axis, [(i, i ^ bits) for i in range(count)])


def swap_both(block, expert_bits, tensor_bits):
    lanes = lax.axis_size("tensor")
    count = lax.axis_size("expert") * lanes
    bits = expert_bits * lanes + tensor_bits
    return lax.ppermute(block, ("expert", "tensor"), [(i, i ^ bits) for i in range(count)])


def iota(shape, dim):
    return lax.broadcasted_iota(I32, shape, dim)


def dot(a, b):
    return jnp.dot(a, b, preferred_element_type=F32)


def dot_t(a, b):
    return lax.dot_general(a, b, (((1,), (1,)), ((), ())), preferred_element_type=F32)


def call(body, outs, args, hbm=(), free=(), scratch=(), vmem=None, cost=None, name=None):
    in_specs = [
        pl.BlockSpec(memory_space=pltpu.HBM if i in hbm else pl.ANY if i in free else pltpu.VMEM)
        for i in range(len(args))
    ]
    args = [pltpu.with_memory_space_constraint(a, pltpu.HBM) if i in hbm else a for i, a in enumerate(args)]
    single = not isinstance(outs, (list, tuple))
    listed = [outs] if single else list(outs)
    out_specs = [pl.BlockSpec(memory_space=pltpu.VMEM) for _ in listed]
    flops, nbytes = cost or (0, 0)
    result = pl.pallas_call(
        body,
        out_shape=listed,
        in_specs=in_specs,
        out_specs=out_specs,
        scratch_shapes=list(scratch),
        compiler_params=pltpu.CompilerParams(vmem_limit_bytes=vmem or 16 << 20),
        cost_estimate=pl.CostEstimate(flops=flops, bytes_accessed=nbytes, transcendentals=0),
        name=name,
    )(*args)
    return result[0] if single else result


def shape(dims, dtype):
    return jax.ShapeDtypeStruct(tuple(dims), dtype)


def spread(rows, values):
    index = iota((rows, LANES), 0)
    total = jnp.full((rows, LANES), values[0])
    for i in range(1, len(values)):
        total = jnp.where(index == i, values[i], total)
    return total


def is_key():
    return lax.axis_index("tensor") % 2 == 0


def is_first():
    return lax.axis_index("tensor") < 2


def project_body(
    length_hbm, group_hbm, offset_hbm, tok_hbm, gain_hbm, kvw_hbm, qw_hbm, cache_hbm, routes_hbm, weight_hbm,
    slot_hbm, sink_hbm,
    q_ref, own_ref, normed_ref, cosine_ref, sine_ref, cache_ref, token_ref, group_out, length_out, position_out,
    sink_out, routes_ref, weight_ref, slot_ref,
    length_ref, group_ref, offset_ref, sink_ref, tok_ref, gain_ref, kvw_ref, qw_ref, sems,
):
    rows, width = tok_ref.shape
    pairs = [
        (length_hbm, length_ref), (group_hbm, group_ref), (offset_hbm, offset_ref), (tok_hbm, tok_ref),
        (gain_hbm, gain_ref), (kvw_hbm.at[0], kvw_ref), (routes_hbm, routes_ref), (weight_hbm, weight_ref),
        (slot_hbm, slot_ref), (sink_hbm, sink_ref),
    ]
    pairs += [(qw_hbm, qw_ref), (cache_hbm.at[0, 0], cache_ref)]
    loads = [pltpu.make_async_copy(src, dst, sems.at[i]) for i, (src, dst) in enumerate(pairs)]
    for load in loads:
        load.start()
    dim = kvw_ref.shape[1]
    heads = qw_ref.shape[1] // dim
    half = dim // 2
    quarter = width // 4
    for load in loads[:3]:
        load.wait()
    groups = [group_ref[i] for i in range(rows)]
    lengths = [length_ref[0, g] for g in groups]
    group_out[...] = spread(rows, groups)
    length_out[...] = spread(rows, lengths)
    position = spread(rows, [lengths[i] + offset_ref[i] for i in range(rows)])
    position_out[...] = position
    lane = iota((rows, dim), 1)
    step = jnp.where(lane >= half, lane - half, lane).astype(F32)
    angle = position.astype(F32) * jnp.exp(step * (-math.log(10000.0) / half))
    cosine = jnp.cos(angle)
    sine = jnp.sin(angle)
    sine = jnp.where(lane < half, -sine, sine)
    cosine_ref[...] = cosine
    sine_ref[...] = sine
    loads[3].wait()
    loads[4].wait()
    tok = tok_ref[...].astype(F32)
    mean = jnp.sum(tok * tok, axis=1, keepdims=True) / width
    normed = (tok * lax.rsqrt(mean + EPSILON) * gain_ref[...].astype(F32).reshape(1, width)).astype(BF16)
    for i in range(2):
        low, high = (tok[:, (2 * i + k) * quarter : (2 * i + k + 1) * quarter] for k in range(2))
        token_ref[:, i * quarter : (i + 1) * quarter] = jnp.where(
            is_first(), jnp.where(is_key(), low, high), 0.0
        )
    normed_ref[...] = normed
    loads[9].wait()
    sink_out[...] = spread(sink_out.shape[0], [sink_ref[i] for i in range(heads)])
    loads[5].wait()
    own = dot(normed, kvw_ref[...])
    turned = own * cosine + pltpu.roll(own, half, 1) * sine
    own_ref[...] = jnp.where(is_key(), turned, own).astype(BF16)
    loads[10].wait()
    q = dot(normed, qw_ref[...])
    for h in range(heads):
        head = q[:, h * dim : (h + 1) * dim]
        q_ref[h * rows : (h + 1) * rows, :] = (head * cosine + pltpu.roll(head, half, 1) * sine).astype(BF16)
    for load in loads[6:9] + loads[11:]:
        load.wait()


def extra_body(routes_ref, weight_ref, slot_ref, sent_ref, extra_ref):
    rows = routes_ref.shape[1]
    copies = slot_ref.shape[1]
    replicas = copies // EXPERTS
    block = iota((copies, rows), 1) // (rows // replicas)
    place = iota((copies, rows), 0)
    chosen = jnp.zeros((copies, rows), F32)
    for k in range(TOP):
        named = routes_ref[k : k + 1, :] * replicas + block
        chosen = chosen + jnp.where(named == place, weight_ref[k : k + 1, :], 0.0)
    order = (iota((copies, copies), 0) == slot_ref[...]).astype(F32).astype(BF16)
    high = chosen.astype(BF16)
    low = (chosen - high.astype(F32)).astype(BF16)
    extra_ref[...] = jnp.zeros(extra_ref.shape, F32)
    for i, term in enumerate((high, low)):
        moved = lax.dot_general(term, order, (((0,), (1,)), ((), ())), preferred_element_type=F32)
        extra_ref[:, i * copies : (i + 1) * copies] = jnp.where(is_first(), moved, 0.0)


def attend_body(
    q_ref, own_ref, normed_ref, other_ref, cosine_ref, sine_ref, mine_ref, theirs_ref, group_ref, length_ref,
    position_ref, sink_ref, out_ref, token_ref, send_ref, keep_ref,
):
    rows, dim = own_ref.shape
    heads = q_ref.shape[0] // rows
    slots = mine_ref.shape[0]
    quarter = send_ref.shape[1] // 2
    scale = 1.0 / dim**0.5
    mine, theirs = mine_ref[...], theirs_ref[...]
    keys = jnp.where(is_key(), mine, theirs)
    values = jnp.where(is_key(), theirs, mine)
    scores = dot_t(q_ref[...], keys)
    other = dot(normed_ref[...], other_ref[...])
    turned = other * cosine_ref[...] + pltpu.roll(other, dim // 2, 1) * sine_ref[...]
    other = jnp.where(is_key(), other, turned).astype(BF16).astype(F32)
    own = own_ref[...].astype(F32)
    key = jnp.where(is_key(), own, other)
    value = jnp.where(is_key(), other, own)
    group, row_length, position = group_ref[...], length_ref[...], position_ref[...]
    lane = iota((rows, LANES), 1)
    seen = []
    for start in range(0, slots, LANES):
        place = lane + start % PROMPT_CAP
        seen.append((group == start // PROMPT_CAP) & (place < row_length) & (place > position - WINDOW))
    probs, own_probs = [], []
    for h in range(heads):
        span = slice(h * rows, (h + 1) * rows)
        masked = [
            jnp.where(seen[k], scores[span, k * LANES : (k + 1) * LANES] * scale, HIDE) for k in range(len(seen))
        ]
        sink = sink_ref[h : h + 1, :1]
        score = jnp.sum(q_ref[span, :].astype(F32) * key, axis=1, keepdims=True) * scale
        top = jnp.max(functools.reduce(jnp.maximum, masked), axis=1, keepdims=True)
        top = jnp.maximum(jnp.maximum(top, score), sink)
        part = [jnp.exp(m - top) for m in masked]
        fresh = jnp.exp(score - top)
        total = jnp.sum(functools.reduce(jnp.add, part), axis=1, keepdims=True) + fresh + jnp.exp(sink - top)
        inverse = 1.0 / total
        probs.append(jnp.concatenate([(p * inverse).astype(BF16) for p in part], axis=1))
        own_probs.append((fresh * inverse).astype(BF16).astype(F32))
    cached = dot(jnp.concatenate(probs, axis=0), values)
    context = [
        (cached[h * rows : (h + 1) * rows] + own_probs[h] * value).astype(BF16) for h in range(heads)
    ]
    attended = dot(jnp.concatenate(context, axis=1), out_ref[...])
    part = [attended[:, i * quarter : (i + 1) * quarter] for i in range(4)]
    for i in range(2):
        span = slice(i * quarter, (i + 1) * quarter)
        send_ref[:, span] = jnp.where(is_key(), part[2 * i + 1], part[2 * i]).astype(BF16)
        keep_ref[:, span] = jnp.where(is_key(), part[2 * i], part[2 * i + 1]) + token_ref[:, span]


def chip_body(keep_ref, extra_ref, got_ref, out_ref):
    width = got_ref.shape[1]
    out_ref[:, :width] = (keep_ref[...] + got_ref[...].astype(F32)).astype(BF16)
    out_ref[:, width:] = extra_ref[...].astype(BF16)


def relay_body(block_ref, *refs):
    refs[-1][...] = block_ref[...]


def after_all(block, earlier):
    return call(
        relay_body,
        shape(block.shape, block.dtype),
        (block, *earlier),
        free=range(1, 1 + len(earlier)),
        name="relay",
        cost=(block.size, 1 << 17),
    )


def residual_body(copies, gain_ref, own_ref, y_ref, xy_ref, x_ref, loaded_ref, rows_ref, keep_ref):
    rows, total = own_ref.shape
    width = keep_ref.shape[1]
    quarter = width // 2
    gain = [gain_ref[:, i * quarter : (i + 1) * quarter] for i in range(4)]
    gain = [jnp.where(is_key(), gain[2 * i].astype(F32), gain[2 * i + 1].astype(F32)) for i in range(2)]
    lane = iota((rows, total - width), 1)
    for i, (a_ref, b_ref) in enumerate(((own_ref, x_ref), (y_ref, xy_ref))):
        span = slice(i * rows, (i + 1) * rows)
        squares = jnp.zeros((rows, 1), F32)
        for k in range(2):
            cols = slice(k * quarter, (k + 1) * quarter)
            part = (a_ref[:, cols].astype(F32) + b_ref[:, cols].astype(F32)).astype(BF16)
            wide = part.astype(F32)
            squares = squares + jnp.sum(wide * wide, axis=1, keepdims=True)
            rows_ref[span, cols] = (wide * gain[k]).astype(BF16)
            if i == 0:
                keep_ref[:, cols] = part
        extra = a_ref[:, width:].astype(F32) + b_ref[:, width:].astype(F32)
        high = squares.astype(BF16).astype(F32)
        extra = jnp.where(lane == 2 * copies, high, extra)
        extra = jnp.where(lane == 2 * copies + 1, squares - high, extra)
        rows_ref[span, width:] = extra.astype(BF16)


def load_body(*refs):
    sems = refs[-1]
    count = (len(refs) - 2) // 2
    loads = []
    for src, dst in zip(refs[1 : 1 + count], refs[1 + count : -1]):
        tall = src.shape[0] // CHUNKS
        for k in range(CHUNKS):
            part = pl.ds(k * tall, tall)
            loads.append(pltpu.make_async_copy(src.at[part], dst.at[part], sems.at[len(loads)]))
    for load in loads:
        load.start()
    for load in loads:
        load.wait()


def expert_body(copies, hosted, blocks, *refs):
    own_refs, other_refs = refs[:blocks], refs[blocks : 2 * blocks]
    gate_ref, up_ref, down_ref, hidden_ref = refs[2 * blocks : 2 * blocks + 4]
    send_refs = refs[2 * blocks + 4 :]
    width = gate_ref.shape[1]
    units = gate_ref.shape[0] // hosted
    quarter = width // 4
    own = jnp.concatenate([r[...] for r in own_refs], axis=0)
    other = jnp.concatenate([r[...] for r in other_refs], axis=0)
    parts = []
    for i in range(4):
        span = slice(i // 2 * quarter, (i // 2 + 1) * quarter)
        mine = is_key() if i % 2 == 0 else jnp.logical_not(is_key())
        parts.append(jnp.where(mine, own[:, span], other[:, span]))
    rows = jnp.concatenate(parts, axis=1)
    extra = own[:, 2 * quarter :].astype(F32)
    lane = iota(extra.shape, 1)
    squares = jnp.where((lane == 2 * copies) | (lane == 2 * copies + 1), extra + other[:, 2 * quarter :].astype(F32), 0.0)
    scale = lax.rsqrt(jnp.sum(squares, axis=1, keepdims=True) / width + EPSILON)
    tall = rows.shape[0] // blocks
    parts = []
    for j in range(hosted):
        slot = lax.axis_index("expert") * hosted + j
        one = jnp.where((lane == slot) | (lane == slot + copies), extra, 0.0)
        weight = jnp.sum(one, axis=1, keepdims=True)
        span = slice(j * units, (j + 1) * units)
        gate = dot_t(rows, gate_ref[span, :]) * scale
        up = dot_t(rows, up_ref[span, :]) * scale
        parts.append((jnp.maximum(gate, 0.0) * up * weight).astype(BF16))
    hidden = jnp.concatenate(parts, axis=1)
    for b in range(blocks):
        hidden_ref[b] = hidden[b * tall : (b + 1) * tall]
    send_half(hidden, down_ref, send_refs)


def tiles(units):
    step = 256 if units % 256 == 0 else units
    return [slice(i, i + step) for i in range(0, units, step)]


def quarters(blocks, quarter, core):
    rows = jnp.concatenate([r[:, : 2 * quarter] for r in blocks], axis=0)
    for k in range(2):
        start = pl.multiple_of((2 * k + core) * quarter, LANES)
        yield rows[:, k * quarter : (k + 1) * quarter], pl.ds(start, quarter)


def half_body(blocks, *refs):
    own_refs = refs[:blocks]
    gate_ref, up_ref, gate_out, up_out = refs[blocks:]
    quarter = gate_ref.shape[1] // 4
    pairs = list(quarters(own_refs, quarter, lax.axis_index("tensor") % 2))
    for span in tiles(gate_ref.shape[0]):
        for weight_ref, out_ref in ((gate_ref, gate_out), (up_ref, up_out)):
            total = sum(dot_t(part, weight_ref[span, cols]) for part, cols in pairs)
            out_ref[:, :, span] = total.reshape(blocks, -1, total.shape[1])


def rest_body(copies, hosted, blocks, *refs):
    own_refs, other_refs = refs[:blocks], refs[blocks : 2 * blocks]
    gate_ref, up_ref, down_ref, gate_half, up_half, hidden_ref = refs[2 * blocks : 2 * blocks + 6]
    send_refs = refs[2 * blocks + 6 :]
    total, width = gate_ref.shape
    units = total // hosted
    quarter = width // 4
    extra = jnp.concatenate([r[:, 2 * quarter :] for r in own_refs], axis=0).astype(F32)
    far_extra = jnp.concatenate([r[:, 2 * quarter :] for r in other_refs], axis=0).astype(F32)
    lane = iota(extra.shape, 1)
    squares = jnp.where((lane == 2 * copies) | (lane == 2 * copies + 1), extra + far_extra, 0.0)
    scale = lax.rsqrt(jnp.sum(squares, axis=1, keepdims=True) / width + EPSILON)
    weights = []
    for j in range(hosted):
        slot = lax.axis_index("expert") * hosted + j
        one = jnp.where((lane == slot) | (lane == slot + copies), extra, 0.0)
        weights.append(jnp.sum(one, axis=1, keepdims=True))
    pairs = list(quarters(other_refs, quarter, 1 - lax.axis_index("tensor") % 2))
    count = extra.shape[0]
    parts = []
    for span in tiles(total):
        size = span.stop - span.start
        place = iota((count, size), 1) + span.start
        weight = weights[span.start // units]
        for j in range(span.start // units + 1, (span.stop - 1) // units + 1):
            weight = jnp.where(place >= j * units, weights[j], weight)
        gate, up = gate_half[:, :, span].reshape(count, size), up_half[:, :, span].reshape(count, size)
        for part, cols in pairs:
            gate = gate + dot_t(part, gate_ref[span, cols])
            up = up + dot_t(part, up_ref[span, cols])
        parts.append((jnp.maximum(gate * scale, 0.0) * (up * scale) * weight).astype(BF16))
    hidden = jnp.concatenate(parts, axis=1)
    tall = count // blocks
    for b in range(blocks):
        hidden_ref[b] = hidden[b * tall : (b + 1) * tall]
    send_half(hidden, down_ref, send_refs)


def send_half(hidden, down_ref, send_refs):
    quarter = down_ref.shape[1] // 4
    tall = hidden.shape[0] // len(send_refs)
    for k in range(2):
        start = pl.multiple_of((2 * k + 1 - lax.axis_index("tensor") % 2) * quarter, LANES)
        total = dot(hidden, down_ref[:, pl.ds(start, quarter)]).astype(BF16)
        for b, send_ref in enumerate(send_refs):
            send_ref[:, k * quarter : (k + 1) * quarter] = total[b * tall : (b + 1) * tall]


def keep_body(blocks, hidden_ref, down_ref, out_ref):
    quarter = down_ref.shape[1] // 4
    tall = hidden_ref.shape[1]
    hidden = jnp.concatenate([hidden_ref[b] for b in range(blocks)], axis=0)
    for k in range(2):
        start = pl.multiple_of((2 * k + lax.axis_index("tensor") % 2) * quarter, LANES)
        total = dot(hidden, down_ref[:, pl.ds(start, quarter)])
        for b in range(blocks):
            out_ref[b, :, k * quarter : (k + 1) * quarter] = total[b * tall : (b + 1) * tall]


def chips_body(b, keep_ref, got_ref, out_ref):
    out_ref[...] = (keep_ref[b] + got_ref[...].astype(F32)).astype(out_ref.dtype)


def pass_body(terms, *refs):
    total = refs[0][...]
    for r in refs[1:terms]:
        total = total + r[...].astype(F32)
    outs = refs[terms:]
    tall = total.shape[0] // len(outs)
    for i, r in enumerate(outs):
        r[...] = total[i * tall : (i + 1) * tall].astype(r.dtype)


def pair_body(terms, *refs):
    total = refs[0][...]
    for r in refs[1:terms]:
        total = total + r[...].astype(F32)
    own_ref, x_ref, y_ref = refs[terms:]
    rows = own_ref.shape[0]
    own_ref[...] = total[:rows]
    x_ref[...] = total[:rows].astype(BF16)
    y_ref[...] = total[rows:].astype(BF16)


def combine_body(own_ref, x_ref, y_ref, xy_ref, residual_ref, combined_ref, square_ref):
    quarter = combined_ref.shape[1]
    total = (own_ref[...] + x_ref[...].astype(F32)) + (y_ref[...].astype(F32) + xy_ref[...].astype(F32))
    total = residual_ref[...].astype(F32) + total
    combined_ref[...] = jnp.where(is_first(), total[:, :quarter], total[:, quarter:])
    square_ref[...] = jnp.broadcast_to(jnp.sum(total * total, axis=1, keepdims=True), square_ref.shape)


def finish_body(width, combined_ref, gain_ref, a_ref, b_ref, out_ref):
    mean = (a_ref[...] + b_ref[...])[:, :1] / width
    out_ref[...] = (combined_ref[...] * lax.rsqrt(mean + EPSILON) * gain_ref[...].astype(F32)).astype(BF16)


def run_experts(own, other, gate_weight, up_weight, down_weight, hosted, copies, first):
    blocks = len(own)
    tall, total = own[0].shape
    units, width = gate_weight.shape
    step = min(tall, 64)
    grid = (tall // step,) if tall > step else ()

    def spec(dims, place):
        if not grid:
            return pl.BlockSpec(memory_space=pltpu.VMEM)
        return pl.BlockSpec(dims, place)

    row_spec = spec((step, total), lambda i: (i, 0))
    half_spec = spec((step, width // 2), lambda i: (i, 0))
    keep_spec = spec((blocks, step, width // 2), lambda i: (0, i, 0))
    hidden_spec = spec((blocks, step, units), lambda i: (0, i, 0))
    whole = pl.BlockSpec(memory_space=pltpu.VMEM)
    params = pltpu.CompilerParams(vmem_limit_bytes=32 << 20)
    tiny = pl.CostEstimate(flops=1, bytes_accessed=1, transcendentals=0)
    halves = []
    if not first:
        halves = pl.pallas_call(
            functools.partial(half_body, blocks),
            grid=grid,
            out_shape=[shape((blocks, tall, units), F32)] * 2,
            in_specs=[row_spec] * blocks + [whole] * 2,
            out_specs=[hidden_spec] * 2,
            compiler_params=params,
            cost_estimate=tiny,
            name="experts_half_depth",
        )(*own, gate_weight, up_weight)
    hidden, *sends = pl.pallas_call(
        functools.partial(expert_body if first else rest_body, copies, hosted, blocks),
        grid=grid,
        out_shape=[shape((blocks, tall, units), BF16)] + [shape((tall, width // 2), BF16)] * blocks,
        in_specs=[row_spec] * (2 * blocks) + [whole] * 3 + [hidden_spec] * len(halves),
        out_specs=[hidden_spec] + [half_spec] * blocks,
        compiler_params=params,
        cost_estimate=tiny,
        name="experts",
    )(*own, *other, gate_weight, up_weight, down_weight, *halves)
    got = [swap(send, "tensor", 1) for send in sends]
    keep = pl.pallas_call(
        functools.partial(keep_body, blocks),
        grid=grid,
        out_shape=shape((blocks, tall, width // 2), F32),
        in_specs=[hidden_spec, whole],
        out_specs=keep_spec,
        compiler_params=params,
        cost_estimate=tiny,
        name="experts_own_half",
    )(hidden, down_weight)
    sums = [
        call(
            functools.partial(chips_body, b),
            shape((tall, width // 2), F32 if first else BF16),
            (keep, got[b]),
            vmem=48 << 20,
            name="chip_sums",
            cost=(1, 1),
        )
        for b in range(blocks)
    ]
    return sums, sends[0], got[0]


def on_device(
    tokens, attn_gain, query_weight, key_value_weight, paired_cache, prompt_length, group_index, offsets,
    sink_logit, out_weight, mixer_gain, routes, route_weight, copy_slot, gate_weight, up_weight, down_weight,
    final_gain,
):
    rows, width = tokens.shape
    dim = key_value_weight.shape[2]
    heads = query_weight.shape[1] // dim
    half, quarter = width // 2, width // 4
    slots = paired_cache.shape[2]
    copies = copy_slot.shape[0]
    far = lax.axis_size("expert") // 2
    extra_width = -(-(2 * copies + 2) // LANES) * LANES
    hosted = gate_weight.shape[0]
    gate_weight = jnp.swapaxes(gate_weight, 1, 2).reshape(-1, width)
    up_weight = jnp.swapaxes(up_weight, 1, 2).reshape(-1, width)
    down_weight = down_weight.reshape(-1, width)

    other_cache = swap(paired_cache[0, 0], "tensor", 1)
    other_weight = swap(key_value_weight[0], "tensor", 1)
    place = shape((rows, LANES), I32)
    turn = shape((rows, dim), F32)
    queries, own_new, normed, cosine, sine, own_cache, token_half, *rest, named, named_weight, slot = call(
        project_body,
        [
            shape((heads * rows, dim), BF16), shape((rows, dim), BF16), shape((rows, width), BF16), turn, turn,
            shape((slots, dim), BF16), shape((rows, half), F32), place, place, place, shape((8, LANES), F32),
            shape((TOP, rows), I32), shape((TOP, rows), F32), shape((1, copies), I32),
        ],
        (
            prompt_length, group_index, offsets, tokens, attn_gain, key_value_weight, query_weight,
            paired_cache, routes.T, route_weight.T, copy_slot[None, :], sink_logit,
        ),
        hbm=range(12),
        scratch=[
            pltpu.SMEM(prompt_length.shape, I32),
            pltpu.SMEM(group_index.shape, I32),
            pltpu.SMEM(offsets.shape, I32),
            pltpu.SMEM(sink_logit.shape, F32),
            pltpu.VMEM(tokens.shape, BF16),
            pltpu.VMEM((width,), BF16),
            pltpu.VMEM(key_value_weight.shape[1:], BF16),
            pltpu.VMEM(query_weight.shape, BF16),
            pltpu.SemaphoreType.DMA((12,)),
        ],
        name="project",
        cost=(2 * rows * width * (heads + 1) * dim, 2 << 20),
    )
    send, keep = call(
        attend_body,
        [shape((rows, half), BF16), shape((rows, half), F32)],
        (queries, own_new, normed, other_weight, cosine, sine, own_cache, other_cache, *rest, out_weight, token_half),
        name="attention",
        cost=(4 * heads * rows * dim * slots, 1 << 20),
    )
    extra = call(
        extra_body,
        shape((rows, extra_width), F32),
        (named, named_weight, slot, send),
        free=[3],
        name="route_columns",
    )
    own = call(
        chip_body, shape((rows, half + extra_width), BF16), (keep, extra, swap(send, "tensor", 1)), name="chip_sum",
        cost=(rows * width, 1 << 18),
    )
    far_y, far_xy, near_x = swap(own, "expert", far), swap_both(own, far, 2), swap(own, "tensor", 2)
    weights = (gate_weight, up_weight, down_weight)
    weights = call(
        load_body,
        [shape(w.shape, BF16) for w in weights],
        (own, *weights),
        hbm=range(1, 4),
        scratch=[pltpu.SemaphoreType.DMA((len(weights) * CHUNKS,))],
        name="load_experts",
        cost=(0, 8 << 20),
    )
    block, residual = call(
        functools.partial(residual_body, copies),
        [shape((2 * rows, half + extra_width), BF16), shape((rows, half), BF16)],
        (mixer_gain[None, :], own, far_y, far_xy, near_x, weights[0]),
        free=[5],
        name="residual",
        cost=(rows * width, 1 << 18),
    )

    bit, stages = 1, []
    while bit < far:
        stages.append([bit] if 2 * bit >= far else [3 * bit, bit, 2 * bit])
        bit *= 4
    blocks = [block]
    for stage in stages:
        whole = blocks[0] if len(blocks) == 1 else jnp.concatenate(blocks, axis=0)
        blocks = [whole] + [swap(whole, "expert", b) for b in stage]
    pieces = []
    for group in (blocks[:1], blocks[1:]):
        if pieces:
            group = [after_all(b, [got if i else send]) for i, b in enumerate(group)]
        others = [swap(b, "tensor", 1) for b in group]
        sums, send, got = run_experts(group, others, *weights, hosted, copies, not pieces)
        pieces += sums
    terms = [pieces[0]] + [swap(p, "expert", b) for p, b in zip(pieces[1:], stages[-1])]
    for stage in stages[-2::-1]:
        tall = terms[0].shape[0] // (len(stage) + 1)
        pieces = call(
            functools.partial(pass_body, len(terms)),
            [shape((tall, half), F32)] + [shape((tall, half), BF16)] * len(stage),
            terms,
            vmem=48 << 20,
            name="pass_on",
            cost=(tall * width, 1 << 20),
        )
        terms = [pieces[0]] + [swap(p, "expert", b) for p, b in zip(pieces[1:], stage)]
    own, x_part, far_part = call(
        functools.partial(pair_body, len(terms)),
        [shape((rows, half), F32), shape((rows, half), BF16), shape((rows, half), BF16)],
        terms,
        name="z_sums",
        cost=(rows * width, 1 << 18),
    )
    far_y, far_xy, near_x = swap(far_part, "expert", far), swap_both(far_part, far, 2), swap(x_part, "tensor", 2)
    combined, squares = call(
        combine_body,
        [shape((rows, quarter), F32), shape((rows, LANES), F32)],
        (own, near_x, far_y, far_xy, residual),
        name="combine",
        cost=(rows * width, 1 << 18),
    )
    return call(
        functools.partial(finish_body, width),
        shape((rows, quarter), BF16),
        (combined, final_gain[None, :], squares, swap(squares, "tensor", 1)),
        name="finish",
        cost=(rows * width, 1 << 18),
    )


def solution(mesh):
    in_specs = (
        P("expert", None),
        P(),
        P(None, "tensor"),
        P("tensor", None, None),
        P("expert", "tensor", None, None),
        P("expert", None),
        P("expert"),
        P("expert"),
        P("tensor"),
        P("tensor", None),
        P(),
        P("expert", None),
        P("expert", None),
        P(),
        P("expert", None, "tensor"),
        P("expert", None, "tensor"),
        P("expert", "tensor", None),
        P("tensor"),
    )
    out_specs = P("expert", "tensor")
    return jax.shard_map(
        on_device, mesh=mesh, in_specs=in_specs, out_specs=out_specs, check_vma=False
    )
```

```python
import functools
import math

import jax
import jax.numpy as jnp
from jax import lax
from jax.experimental import pallas as pl
from jax.experimental.pallas import tpu as pltpu
from jax.sharding import PartitionSpec as P

EXPERTS = 32
TOP = 4
PROMPT_CAP = 256
WINDOW = 192
EPSILON = 1e-06
LANES = 128
CHUNKS = 4
HIDE = -1e30
F32 = jnp.float32
BF16 = jnp.bfloat16
I32 = jnp.int32


def swap(block, axis, bits):
    count = lax.axis_size(axis)
    return lax.ppermute(block, axis, [(i, i ^ bits) for i in range(count)])


def swap_both(block, expert_bits, tensor_bits):
    lanes = lax.axis_size("tensor")
    count = lax.axis_size("expert") * lanes
    bits = expert_bits * lanes + tensor_bits
    return lax.ppermute(block, ("expert", "tensor"), [(i, i ^ bits) for i in range(count)])


def iota(shape, dim):
    return lax.broadcasted_iota(I32, shape, dim)


def dot(a, b):
    return jnp.dot(a, b, preferred_element_type=F32)


def dot_t(a, b):
    return lax.dot_general(a, b, (((1,), (1,)), ((), ())), preferred_element_type=F32)


def call(body, outs, args, hbm=(), free=(), scratch=(), vmem=None, cost=None, name=None):
    in_specs = [
        pl.BlockSpec(memory_space=pltpu.HBM if i in hbm else pl.ANY if i in free else pltpu.VMEM)
        for i in range(len(args))
    ]
    args = [pltpu.with_memory_space_constraint(a, pltpu.HBM) if i in hbm else a for i, a in enumerate(args)]
    single = not isinstance(outs, (list, tuple))
    listed = [outs] if single else list(outs)
    out_specs = [pl.BlockSpec(memory_space=pltpu.VMEM) for _ in listed]
    flops, nbytes = cost or (0, 0)
    result = pl.pallas_call(
        body,
        out_shape=listed,
        in_specs=in_specs,
        out_specs=out_specs,
        scratch_shapes=list(scratch),
        compiler_params=pltpu.CompilerParams(vmem_limit_bytes=vmem or 16 << 20),
        cost_estimate=pl.CostEstimate(flops=flops, bytes_accessed=nbytes, transcendentals=0),
        name=name,
    )(*args)
    return result[0] if single else result


def shape(dims, dtype):
    return jax.ShapeDtypeStruct(tuple(dims), dtype)


def spread(rows, values):
    index = iota((rows, LANES), 0)
    total = jnp.full((rows, LANES), values[0])
    for i in range(1, len(values)):
        total = jnp.where(index == i, values[i], total)
    return total


def is_key():
    return lax.axis_index("tensor") % 2 == 0


def is_first():
    return lax.axis_index("tensor") < 2


def project_body(
    length_hbm, group_hbm, offset_hbm, tok_hbm, gain_hbm, kvw_hbm, qw_hbm, cache_hbm, routes_hbm, weight_hbm,
    slot_hbm, sink_hbm,
    q_ref, own_ref, normed_ref, cosine_ref, sine_ref, cache_ref, token_ref, group_out, length_out, position_out,
    sink_out, routes_ref, weight_ref, slot_ref,
    length_ref, group_ref, offset_ref, sink_ref, tok_ref, gain_ref, kvw_ref, qw_ref, sems,
):
    rows, width = tok_ref.shape
    pairs = [
        (length_hbm, length_ref), (group_hbm, group_ref), (offset_hbm, offset_ref), (tok_hbm, tok_ref),
        (gain_hbm, gain_ref), (kvw_hbm.at[0], kvw_ref), (routes_hbm, routes_ref), (weight_hbm, weight_ref),
        (slot_hbm, slot_ref), (sink_hbm, sink_ref),
    ]
    pairs += [(qw_hbm, qw_ref), (cache_hbm.at[0, 0], cache_ref)]
    loads = [pltpu.make_async_copy(src, dst, sems.at[i]) for i, (src, dst) in enumerate(pairs)]
    for load in loads:
        load.start()
    dim = kvw_ref.shape[1]
    heads = qw_ref.shape[1] // dim
    half = dim // 2
    quarter = width // 4
    for load in loads[:3]:
        load.wait()
    groups = [group_ref[i] for i in range(rows)]
    lengths = [length_ref[0, g] for g in groups]
    group_out[...] = spread(rows, groups)
    length_out[...] = spread(rows, lengths)
    position = spread(rows, [lengths[i] + offset_ref[i] for i in range(rows)])
    position_out[...] = position
    lane = iota((rows, dim), 1)
    step = jnp.where(lane >= half, lane - half, lane).astype(F32)
    angle = position.astype(F32) * jnp.exp(step * (-math.log(10000.0) / half))
    cosine = jnp.cos(angle)
    sine = jnp.sin(angle)
    sine = jnp.where(lane < half, -sine, sine)
    cosine_ref[...] = cosine
    sine_ref[...] = sine
    loads[3].wait()
    loads[4].wait()
    tok = tok_ref[...].astype(F32)
    mean = jnp.sum(tok * tok, axis=1, keepdims=True) / width
    normed = (tok * lax.rsqrt(mean + EPSILON) * gain_ref[...].astype(F32).reshape(1, width)).astype(BF16)
    for i in range(2):
        low, high = (tok[:, (2 * i + k) * quarter : (2 * i + k + 1) * quarter] for k in range(2))
        token_ref[:, i * quarter : (i + 1) * quarter] = jnp.where(
            is_first(), jnp.where(is_key(), low, high), 0.0
        )
    normed_ref[...] = normed
    loads[9].wait()
    sink_out[...] = spread(sink_out.shape[0], [sink_ref[i] for i in range(heads)])
    loads[5].wait()
    own = dot(normed, kvw_ref[...])
    turned = own * cosine + pltpu.roll(own, half, 1) * sine
    own_ref[...] = jnp.where(is_key(), turned, own).astype(BF16)
    loads[10].wait()
    q = dot(normed, qw_ref[...])
    for h in range(heads):
        head = q[:, h * dim : (h + 1) * dim]
        q_ref[h * rows : (h + 1) * rows, :] = (head * cosine + pltpu.roll(head, half, 1) * sine).astype(BF16)
    for load in loads[6:9] + loads[11:]:
        load.wait()


def extra_body(routes_ref, weight_ref, slot_ref, sent_ref, extra_ref):
    rows = routes_ref.shape[1]
    copies = slot_ref.shape[1]
    replicas = copies // EXPERTS
    block = iota((copies, rows), 1) // (rows // replicas)
    place = iota((copies, rows), 0)
    chosen = jnp.zeros((copies, rows), F32)
    for k in range(TOP):
        named = routes_ref[k : k + 1, :] * replicas + block
        chosen = chosen + jnp.where(named == place, weight_ref[k : k + 1, :], 0.0)
    order = (iota((copies, copies), 0) == slot_ref[...]).astype(F32).astype(BF16)
    high = chosen.astype(BF16)
    low = (chosen - high.astype(F32)).astype(BF16)
    extra_ref[...] = jnp.zeros(extra_ref.shape, F32)
    for i, term in enumerate((high, low)):
        moved = lax.dot_general(term, order, (((0,), (1,)), ((), ())), preferred_element_type=F32)
        extra_ref[:, i * copies : (i + 1) * copies] = jnp.where(is_first(), moved, 0.0)


def attend_body(
    q_ref, own_ref, normed_ref, other_ref, cosine_ref, sine_ref, mine_ref, theirs_ref, group_ref, length_ref,
    position_ref, sink_ref, out_ref, token_ref, send_ref, keep_ref,
):
    rows, dim = own_ref.shape
    heads = q_ref.shape[0] // rows
    slots = mine_ref.shape[0]
    quarter = send_ref.shape[1] // 2
    scale = 1.0 / dim**0.5
    mine, theirs = mine_ref[...], theirs_ref[...]
    keys = jnp.where(is_key(), mine, theirs)
    values = jnp.where(is_key(), theirs, mine)
    scores = dot_t(q_ref[...], keys)
    other = dot(normed_ref[...], other_ref[...])
    turned = other * cosine_ref[...] + pltpu.roll(other, dim // 2, 1) * sine_ref[...]
    other = jnp.where(is_key(), other, turned).astype(BF16).astype(F32)
    own = own_ref[...].astype(F32)
    key = jnp.where(is_key(), own, other)
    value = jnp.where(is_key(), other, own)
    group, row_length, position = group_ref[...], length_ref[...], position_ref[...]
    lane = iota((rows, LANES), 1)
    seen = []
    for start in range(0, slots, LANES):
        place = lane + start % PROMPT_CAP
        seen.append((group == start // PROMPT_CAP) & (place < row_length) & (place > position - WINDOW))
    probs, own_probs = [], []
    for h in range(heads):
        span = slice(h * rows, (h + 1) * rows)
        masked = [
            jnp.where(seen[k], scores[span, k * LANES : (k + 1) * LANES] * scale, HIDE) for k in range(len(seen))
        ]
        sink = sink_ref[h : h + 1, :1]
        score = jnp.sum(q_ref[span, :].astype(F32) * key, axis=1, keepdims=True) * scale
        top = jnp.max(functools.reduce(jnp.maximum, masked), axis=1, keepdims=True)
        top = jnp.maximum(jnp.maximum(top, score), sink)
        part = [jnp.exp(m - top) for m in masked]
        fresh = jnp.exp(score - top)
        total = jnp.sum(functools.reduce(jnp.add, part), axis=1, keepdims=True) + fresh + jnp.exp(sink - top)
        inverse = 1.0 / total
        probs.append(jnp.concatenate([(p * inverse).astype(BF16) for p in part], axis=1))
        own_probs.append((fresh * inverse).astype(BF16).astype(F32))
    cached = dot(jnp.concatenate(probs, axis=0), values)
    context = [
        (cached[h * rows : (h + 1) * rows] + own_probs[h] * value).astype(BF16) for h in range(heads)
    ]
    attended = dot(jnp.concatenate(context, axis=1), out_ref[...])
    part = [attended[:, i * quarter : (i + 1) * quarter] for i in range(4)]
    for i in range(2):
        span = slice(i * quarter, (i + 1) * quarter)
        send_ref[:, span] = jnp.where(is_key(), part[2 * i + 1], part[2 * i]).astype(BF16)
        keep_ref[:, span] = jnp.where(is_key(), part[2 * i], part[2 * i + 1]) + token_ref[:, span]


def chip_body(keep_ref, extra_ref, got_ref, out_ref):
    width = got_ref.shape[1]
    out_ref[:, :width] = (keep_ref[...] + got_ref[...].astype(F32)).astype(BF16)
    out_ref[:, width:] = extra_ref[...].astype(BF16)


def relay_body(block_ref, *refs):
    refs[-1][...] = block_ref[...]


def after_all(block, earlier):
    return call(
        relay_body,
        shape(block.shape, block.dtype),
        (block, *earlier),
        free=range(1, 1 + len(earlier)),
        name="relay",
        cost=(block.size, 1 << 17),
    )


def residual_body(copies, gain_ref, own_ref, y_ref, xy_ref, x_ref, loaded_ref, rows_ref, keep_ref):
    rows, total = own_ref.shape
    width = keep_ref.shape[1]
    quarter = width // 2
    gain = [gain_ref[:, i * quarter : (i + 1) * quarter] for i in range(4)]
    gain = [jnp.where(is_key(), gain[2 * i].astype(F32), gain[2 * i + 1].astype(F32)) for i in range(2)]
    lane = iota((rows, total - width), 1)
    for i, (a_ref, b_ref) in enumerate(((own_ref, x_ref), (y_ref, xy_ref))):
        span = slice(i * rows, (i + 1) * rows)
        part = (a_ref[:, :width].astype(F32) + b_ref[:, :width].astype(F32)).astype(BF16)
        if i == 0:
            keep_ref[...] = part
        wide = part.astype(F32)
        squares = jnp.sum(wide * wide, axis=1, keepdims=True)
        scaled = wide * lax.rsqrt(squares / (2 * width) + EPSILON)
        for k in range(2):
            cols = slice(k * quarter, (k + 1) * quarter)
            rows_ref[span, cols] = (scaled[:, cols] * gain[k]).astype(BF16)
        extra = a_ref[:, width:].astype(F32) + b_ref[:, width:].astype(F32)
        squares = squares * 0.5
        high = squares.astype(BF16).astype(F32)
        extra = jnp.where(lane == 2 * copies, high, extra)
        extra = jnp.where(lane == 2 * copies + 1, squares - high, extra)
        rows_ref[span, width:] = extra.astype(BF16)


def load_body(*refs):
    sems = refs[-1]
    count = (len(refs) - 2) // 2
    loads = []
    for src, dst in zip(refs[1 : 1 + count], refs[1 + count : -1]):
        tall = src.shape[0] // CHUNKS
        for k in range(CHUNKS):
            part = pl.ds(k * tall, tall)
            loads.append(pltpu.make_async_copy(src.at[part], dst.at[part], sems.at[len(loads)]))
    for load in loads:
        load.start()
    for load in loads:
        load.wait()


def tiles(units):
    step = 256 if units % 256 == 0 else units
    return [slice(i, i + step) for i in range(0, units, step)]


def quarters(blocks, quarter, core):
    rows = jnp.concatenate([r[:, : 2 * quarter] for r in blocks], axis=0)
    for k in range(2):
        start = pl.multiple_of((2 * k + core) * quarter, LANES)
        yield rows[:, k * quarter : (k + 1) * quarter], pl.ds(start, quarter)


def half_body(blocks, *refs):
    own_refs = refs[:blocks]
    gate_ref, up_ref, gate_out, up_out = refs[blocks:]
    quarter = gate_ref.shape[1] // 4
    pairs = list(quarters(own_refs, quarter, lax.axis_index("tensor") % 2))
    for span in tiles(gate_ref.shape[0]):
        for weight_ref, out_ref in ((gate_ref, gate_out), (up_ref, up_out)):
            total = sum(dot_t(part, weight_ref[span, cols]) for part, cols in pairs)
            out_ref[:, :, span] = total.reshape(blocks, -1, total.shape[1])


def expert_body(copies, hosted, blocks, *refs):
    own_refs, other_refs = refs[:blocks], refs[blocks : 2 * blocks]
    gate_ref, up_ref, down_ref = refs[2 * blocks : 2 * blocks + 3]
    half_refs = refs[2 * blocks + 3 : -1 - blocks]
    hidden_ref, send_refs = refs[-1 - blocks], refs[-blocks:]
    total, width = gate_ref.shape
    units = total // hosted
    quarter = width // 4
    core = lax.axis_index("tensor") % 2
    extra = jnp.concatenate([r[:, 2 * quarter :] for r in own_refs], axis=0).astype(F32)
    far_extra = jnp.concatenate([r[:, 2 * quarter :] for r in other_refs], axis=0).astype(F32)
    lane = iota(extra.shape, 1)
    squared = (lane == 2 * copies) | (lane == 2 * copies + 1)
    own_mean = jnp.sum(jnp.where(squared, extra, 0.0), axis=1, keepdims=True) * (2.0 / width)
    far_mean = jnp.sum(jnp.where(squared, far_extra, 0.0), axis=1, keepdims=True) * (2.0 / width)
    scale = lax.rsqrt(own_mean + far_mean + EPSILON)
    own_scale = scale * jnp.sqrt(own_mean + EPSILON)
    far_scale = scale * jnp.sqrt(far_mean + EPSILON)
    weights = []
    for j in range(hosted):
        slot = lax.axis_index("expert") * hosted + j
        one = jnp.where((lane == slot) | (lane == slot + copies), extra, 0.0)
        weights.append(jnp.sum(one, axis=1, keepdims=True))
    own_pairs = [] if half_refs else list(quarters(own_refs, quarter, core))
    far_pairs = list(quarters(other_refs, quarter, 1 - core))
    count = extra.shape[0]
    parts = []
    for span in tiles(total):
        size = span.stop - span.start
        place = iota((count, size), 1) + span.start
        weight = weights[span.start // units]
        for j in range(span.start // units + 1, (span.stop - 1) // units + 1):
            weight = jnp.where(place >= j * units, weights[j], weight)
        sums = []
        for i, weight_ref in enumerate((gate_ref, up_ref)):
            if half_refs:
                own = half_refs[i][:, :, span].reshape(count, size)
            else:
                own = sum(dot_t(part, weight_ref[span, cols]) for part, cols in own_pairs)
            far = sum(dot_t(part, weight_ref[span, cols]) for part, cols in far_pairs)
            sums.append(own * own_scale + far * far_scale)
        parts.append((jnp.maximum(sums[0], 0.0) * sums[1] * weight).astype(BF16))
    hidden = jnp.concatenate(parts, axis=1)
    tall = count // blocks
    for b in range(blocks):
        hidden_ref[b] = hidden[b * tall : (b + 1) * tall]
    send_half(hidden, down_ref, send_refs)


def send_half(hidden, down_ref, send_refs):
    quarter = down_ref.shape[1] // 4
    tall = hidden.shape[0] // len(send_refs)
    for k in range(2):
        start = pl.multiple_of((2 * k + 1 - lax.axis_index("tensor") % 2) * quarter, LANES)
        total = dot(hidden, down_ref[:, pl.ds(start, quarter)]).astype(BF16)
        for b, send_ref in enumerate(send_refs):
            send_ref[:, k * quarter : (k + 1) * quarter] = total[b * tall : (b + 1) * tall]


def keep_body(blocks, hidden_ref, down_ref, out_ref):
    quarter = down_ref.shape[1] // 4
    tall = hidden_ref.shape[1]
    hidden = jnp.concatenate([hidden_ref[b] for b in range(blocks)], axis=0)
    for k in range(2):
        start = pl.multiple_of((2 * k + lax.axis_index("tensor") % 2) * quarter, LANES)
        total = dot(hidden, down_ref[:, pl.ds(start, quarter)])
        for b in range(blocks):
            out_ref[b, :, k * quarter : (k + 1) * quarter] = total[b * tall : (b + 1) * tall]


def chips_body(b, keep_ref, got_ref, out_ref):
    out_ref[...] = (keep_ref[b] + got_ref[...].astype(F32)).astype(out_ref.dtype)


def pass_body(terms, *refs):
    total = refs[0][...]
    for r in refs[1:terms]:
        total = total + r[...].astype(F32)
    outs = refs[terms:]
    tall = total.shape[0] // len(outs)
    for i, r in enumerate(outs):
        r[...] = total[i * tall : (i + 1) * tall].astype(r.dtype)


def pair_body(terms, *refs):
    total = refs[0][...]
    for r in refs[1:terms]:
        total = total + r[...].astype(F32)
    own_ref, x_ref, y_ref = refs[terms:]
    rows = own_ref.shape[0]
    own_ref[...] = total[:rows]
    x_ref[...] = total[:rows].astype(BF16)
    y_ref[...] = total[rows:].astype(BF16)


def combine_body(y_ref, xy_ref, x_ref, own_ref, residual_ref, combined_ref, square_ref):
    quarter = combined_ref.shape[1]
    total = (own_ref[...] + x_ref[...].astype(F32)) + (y_ref[...].astype(F32) + xy_ref[...].astype(F32))
    total = residual_ref[...].astype(F32) + total
    combined_ref[...] = jnp.where(is_first(), total[:, :quarter], total[:, quarter:])
    square_ref[...] = jnp.broadcast_to(jnp.sum(total * total, axis=1, keepdims=True), square_ref.shape)


def finish_body(width, combined_ref, gain_ref, a_ref, b_ref, out_ref):
    mean = (a_ref[...] + b_ref[...])[:, :1] / width
    out_ref[...] = (combined_ref[...] * lax.rsqrt(mean + EPSILON) * gain_ref[...].astype(F32)).astype(BF16)


def run_experts(own, other, gate_weight, up_weight, down_weight, hosted, copies, first):
    blocks = len(own)
    tall, total = own[0].shape
    units, width = gate_weight.shape
    step = min(tall, 64)
    grid = (tall // step,) if tall > step else ()

    def spec(dims, place):
        if not grid:
            return pl.BlockSpec(memory_space=pltpu.VMEM)
        return pl.BlockSpec(dims, place)

    row_spec = spec((step, total), lambda i: (i, 0))
    half_spec = spec((step, width // 2), lambda i: (i, 0))
    keep_spec = spec((blocks, step, width // 2), lambda i: (0, i, 0))
    hidden_spec = spec((blocks, step, units), lambda i: (0, i, 0))
    whole = pl.BlockSpec(memory_space=pltpu.VMEM)
    params = pltpu.CompilerParams(vmem_limit_bytes=32 << 20)
    tiny = pl.CostEstimate(flops=1, bytes_accessed=1, transcendentals=0)
    halves = []
    if not first:
        halves = pl.pallas_call(
            functools.partial(half_body, blocks),
            grid=grid,
            out_shape=[shape((blocks, tall, units), F32)] * 2,
            in_specs=[row_spec] * blocks + [whole] * 2,
            out_specs=[hidden_spec] * 2,
            compiler_params=params,
            cost_estimate=tiny,
            name="experts_half_depth",
        )(*own, gate_weight, up_weight)
    hidden, *sends = pl.pallas_call(
        functools.partial(expert_body, copies, hosted, blocks),
        grid=grid,
        out_shape=[shape((blocks, tall, units), BF16)] + [shape((tall, width // 2), BF16)] * blocks,
        in_specs=[row_spec] * (2 * blocks) + [whole] * 3 + [hidden_spec] * len(halves),
        out_specs=[hidden_spec] + [half_spec] * blocks,
        compiler_params=params,
        cost_estimate=tiny,
        name="experts",
    )(*own, *other, gate_weight, up_weight, down_weight, *halves)
    got = [swap(send, "tensor", 1) for send in sends]
    keep = pl.pallas_call(
        functools.partial(keep_body, blocks),
        grid=grid,
        out_shape=shape((blocks, tall, width // 2), F32),
        in_specs=[hidden_spec, whole],
        out_specs=keep_spec,
        compiler_params=params,
        cost_estimate=tiny,
        name="experts_own_half",
    )(hidden, down_weight)
    sums = [
        call(
            functools.partial(chips_body, b),
            shape((tall, width // 2), F32 if first else BF16),
            (keep, got[b]),
            vmem=48 << 20,
            name="chip_sums",
            cost=(1, 1),
        )
        for b in range(blocks)
    ]
    return sums, sends[0], got[0]


def on_device(
    tokens, attn_gain, query_weight, key_value_weight, paired_cache, prompt_length, group_index, offsets,
    sink_logit, out_weight, mixer_gain, routes, route_weight, copy_slot, gate_weight, up_weight, down_weight,
    final_gain,
):
    rows, width = tokens.shape
    dim = key_value_weight.shape[2]
    heads = query_weight.shape[1] // dim
    half, quarter = width // 2, width // 4
    slots = paired_cache.shape[2]
    copies = copy_slot.shape[0]
    far = lax.axis_size("expert") // 2
    extra_width = -(-(2 * copies + 2) // LANES) * LANES
    hosted = gate_weight.shape[0]
    gate_weight = jnp.swapaxes(gate_weight, 1, 2).reshape(-1, width)
    up_weight = jnp.swapaxes(up_weight, 1, 2).reshape(-1, width)
    down_weight = down_weight.reshape(-1, width)

    other_cache = swap(paired_cache[0, 0], "tensor", 1)
    other_weight = swap(key_value_weight[0], "tensor", 1)
    place = shape((rows, LANES), I32)
    turn = shape((rows, dim), F32)
    queries, own_new, normed, cosine, sine, own_cache, token_half, *rest, named, named_weight, slot = call(
        project_body,
        [
            shape((heads * rows, dim), BF16), shape((rows, dim), BF16), shape((rows, width), BF16), turn, turn,
            shape((slots, dim), BF16), shape((rows, half), F32), place, place, place, shape((8, LANES), F32),
            shape((TOP, rows), I32), shape((TOP, rows), F32), shape((1, copies), I32),
        ],
        (
            prompt_length, group_index, offsets, tokens, attn_gain, key_value_weight, query_weight,
            paired_cache, routes.T, route_weight.T, copy_slot[None, :], sink_logit,
        ),
        hbm=range(12),
        scratch=[
            pltpu.SMEM(prompt_length.shape, I32),
            pltpu.SMEM(group_index.shape, I32),
            pltpu.SMEM(offsets.shape, I32),
            pltpu.SMEM(sink_logit.shape, F32),
            pltpu.VMEM(tokens.shape, BF16),
            pltpu.VMEM((width,), BF16),
            pltpu.VMEM(key_value_weight.shape[1:], BF16),
            pltpu.VMEM(query_weight.shape, BF16),
            pltpu.SemaphoreType.DMA((12,)),
        ],
        name="project",
        cost=(2 * rows * width * (heads + 1) * dim, 2 << 20),
    )
    send, keep = call(
        attend_body,
        [shape((rows, half), BF16), shape((rows, half), F32)],
        (queries, own_new, normed, other_weight, cosine, sine, own_cache, other_cache, *rest, out_weight, token_half),
        name="attention",
        cost=(4 * heads * rows * dim * slots, 1 << 20),
    )
    extra = call(
        extra_body,
        shape((rows, extra_width), F32),
        (named, named_weight, slot, send),
        free=[3],
        name="route_columns",
    )
    own = call(
        chip_body, shape((rows, half + extra_width), BF16), (keep, extra, swap(send, "tensor", 1)), name="chip_sum",
        cost=(rows * width, 1 << 18),
    )
    far_y, far_xy, near_x = swap(own, "expert", far), swap_both(own, far, 2), swap(own, "tensor", 2)
    weights = (gate_weight, up_weight, down_weight)
    weights = call(
        load_body,
        [shape(w.shape, BF16) for w in weights],
        (own, *weights),
        hbm=range(1, 4),
        scratch=[pltpu.SemaphoreType.DMA((len(weights) * CHUNKS,))],
        name="load_experts",
        cost=(0, 8 << 20),
    )
    block, residual = call(
        functools.partial(residual_body, copies),
        [shape((2 * rows, half + extra_width), BF16), shape((rows, half), BF16)],
        (mixer_gain[None, :], own, far_y, far_xy, near_x, weights[0]),
        free=[5],
        name="residual",
        cost=(rows * width, 1 << 18),
    )

    bit, stages = 1, []
    while bit < far:
        stages.append([bit] if 2 * bit >= far else [3 * bit, bit, 2 * bit])
        bit *= 4
    blocks = [block]
    for stage in stages:
        whole = blocks[0] if len(blocks) == 1 else jnp.concatenate(blocks, axis=0)
        blocks = [whole] + [swap(whole, "expert", b) for b in stage]
    pieces = []
    for group in (blocks[:1], blocks[1:]):
        if pieces:
            group = [after_all(b, [got if i else send]) for i, b in enumerate(group)]
        others = [swap(b, "tensor", 1) for b in group]
        sums, send, got = run_experts(group, others, *weights, hosted, copies, not pieces)
        pieces += sums
    terms = [pieces[0]] + [swap(p, "expert", b) for p, b in zip(pieces[1:], stages[-1])]
    for stage in stages[-2::-1]:
        tall = terms[0].shape[0] // (len(stage) + 1)
        pieces = call(
            functools.partial(pass_body, len(terms)),
            [shape((tall, half), F32)] + [shape((tall, half), BF16)] * len(stage),
            terms,
            vmem=48 << 20,
            name="pass_on",
            cost=(tall * width, 1 << 20),
        )
        terms = [pieces[0]] + [swap(p, "expert", b) for p, b in zip(pieces[1:], stage)]
    own, x_part, far_part = call(
        functools.partial(pair_body, len(terms)),
        [shape((rows, half), F32), shape((rows, half), BF16), shape((rows, half), BF16)],
        terms,
        name="z_sums",
        cost=(rows * width, 1 << 18),
    )
    far_y, far_xy, near_x = swap(far_part, "expert", far), swap_both(far_part, far, 2), swap(x_part, "tensor", 2)
    combined, squares = call(
        combine_body,
        [shape((rows, quarter), F32), shape((rows, LANES), F32)],
        (far_y, far_xy, near_x, own, residual),
        name="combine",
        cost=(rows * width, 1 << 18),
    )
    return call(
        functools.partial(finish_body, width),
        shape((rows, quarter), BF16),
        (combined, final_gain[None, :], squares, swap(squares, "tensor", 1)),
        name="finish",
        cost=(rows * width, 1 << 18),
    )


def solution(mesh):
    in_specs = (
        P("expert", None),
        P(),
        P(None, "tensor"),
        P("tensor", None, None),
        P("expert", "tensor", None, None),
        P("expert", None),
        P("expert"),
        P("expert"),
        P("tensor"),
        P("tensor", None),
        P(),
        P("expert", None),
        P("expert", None),
        P(),
        P("expert", None, "tensor"),
        P("expert", None, "tensor"),
        P("expert", "tensor", None),
        P("tensor"),
    )
    out_specs = P("expert", "tensor")
    return jax.shard_map(
        on_device, mesh=mesh, in_specs=in_specs, out_specs=out_specs, check_vma=False
    )
```

```python
import functools
import math

import jax
import jax.numpy as jnp
from jax import lax
from jax.experimental import pallas as pl
from jax.experimental.pallas import tpu as pltpu
from jax.sharding import PartitionSpec as P

EXPERTS = 32
TOP = 4
PROMPT_CAP = 256
WINDOW = 192
EPSILON = 1e-06
LANES = 128
CHUNKS = 4
HIDE = -1e30
F32 = jnp.float32
BF16 = jnp.bfloat16
I32 = jnp.int32


def swap(block, axis, bits):
    count = lax.axis_size(axis)
    return lax.ppermute(block, axis, [(i, i ^ bits) for i in range(count)])


def swap_both(block, expert_bits, tensor_bits):
    lanes = lax.axis_size("tensor")
    count = lax.axis_size("expert") * lanes
    bits = expert_bits * lanes + tensor_bits
    return lax.ppermute(block, ("expert", "tensor"), [(i, i ^ bits) for i in range(count)])


def iota(shape, dim):
    return lax.broadcasted_iota(I32, shape, dim)


def dot(a, b):
    return jnp.dot(a, b, preferred_element_type=F32)


def dot_t(a, b):
    return lax.dot_general(a, b, (((1,), (1,)), ((), ())), preferred_element_type=F32)


def call(body, outs, args, hbm=(), free=(), scratch=(), vmem=None, cost=None, name=None):
    in_specs = [
        pl.BlockSpec(memory_space=pltpu.HBM if i in hbm else pl.ANY if i in free else pltpu.VMEM)
        for i in range(len(args))
    ]
    args = [pltpu.with_memory_space_constraint(a, pltpu.HBM) if i in hbm else a for i, a in enumerate(args)]
    single = not isinstance(outs, (list, tuple))
    listed = [outs] if single else list(outs)
    out_specs = [pl.BlockSpec(memory_space=pltpu.VMEM) for _ in listed]
    flops, nbytes = cost or (0, 0)
    result = pl.pallas_call(
        body,
        out_shape=listed,
        in_specs=in_specs,
        out_specs=out_specs,
        scratch_shapes=list(scratch),
        compiler_params=pltpu.CompilerParams(vmem_limit_bytes=vmem or 16 << 20),
        cost_estimate=pl.CostEstimate(flops=flops, bytes_accessed=nbytes, transcendentals=0),
        name=name,
    )(*args)
    return result[0] if single else result


def shape(dims, dtype):
    return jax.ShapeDtypeStruct(tuple(dims), dtype)


def spread(rows, values):
    index = iota((rows, LANES), 0)
    total = jnp.full((rows, LANES), values[0])
    for i in range(1, len(values)):
        total = jnp.where(index == i, values[i], total)
    return total


def is_key():
    return lax.axis_index("tensor") % 2 == 0


def is_first():
    return lax.axis_index("tensor") < 2


def project_body(
    length_hbm, group_hbm, offset_hbm, tok_hbm, gain_hbm, kvw_hbm, qw_hbm, cache_hbm, routes_hbm, weight_hbm,
    slot_hbm, sink_hbm,
    q_ref, own_ref, normed_ref, cosine_ref, sine_ref, cache_ref, token_ref, group_out, length_out, position_out,
    sink_out, routes_ref, weight_ref, slot_ref,
    length_ref, group_ref, offset_ref, sink_ref, tok_ref, gain_ref, kvw_ref, qw_ref, sems,
):
    rows, width = tok_ref.shape
    pairs = [
        (length_hbm, length_ref), (group_hbm, group_ref), (offset_hbm, offset_ref), (tok_hbm, tok_ref),
        (gain_hbm, gain_ref), (kvw_hbm.at[0], kvw_ref), (routes_hbm, routes_ref), (weight_hbm, weight_ref),
        (slot_hbm, slot_ref), (sink_hbm, sink_ref),
    ]
    pairs += [(qw_hbm, qw_ref), (cache_hbm.at[0, 0], cache_ref)]
    loads = [pltpu.make_async_copy(src, dst, sems.at[i]) for i, (src, dst) in enumerate(pairs)]
    for load in loads:
        load.start()
    dim = kvw_ref.shape[1]
    heads = qw_ref.shape[1] // dim
    half = dim // 2
    quarter = width // 4
    for load in loads[:3]:
        load.wait()
    groups = [group_ref[i] for i in range(rows)]
    lengths = [length_ref[0, g] for g in groups]
    group_out[...] = spread(rows, groups)
    length_out[...] = spread(rows, lengths)
    position = spread(rows, [lengths[i] + offset_ref[i] for i in range(rows)])
    position_out[...] = position
    lane = iota((rows, dim), 1)
    step = jnp.where(lane >= half, lane - half, lane).astype(F32)
    angle = position.astype(F32) * jnp.exp(step * (-math.log(10000.0) / half))
    cosine = jnp.cos(angle)
    sine = jnp.sin(angle)
    sine = jnp.where(lane < half, -sine, sine)
    cosine_ref[...] = cosine
    sine_ref[...] = sine
    loads[3].wait()
    loads[4].wait()
    tok = tok_ref[...].astype(F32)
    mean = jnp.sum(tok * tok, axis=1, keepdims=True) / width
    normed = (tok * lax.rsqrt(mean + EPSILON) * gain_ref[...].astype(F32).reshape(1, width)).astype(BF16)
    for i in range(2):
        low, high = (tok[:, (2 * i + k) * quarter : (2 * i + k + 1) * quarter] for k in range(2))
        token_ref[:, i * quarter : (i + 1) * quarter] = jnp.where(
            is_first(), jnp.where(is_key(), low, high), 0.0
        )
    normed_ref[...] = normed
    loads[9].wait()
    sink_out[...] = spread(sink_out.shape[0], [sink_ref[i] for i in range(heads)])
    loads[5].wait()
    own = dot(normed, kvw_ref[...])
    turned = own * cosine + pltpu.roll(own, half, 1) * sine
    own_ref[...] = jnp.where(is_key(), turned, own).astype(BF16)
    loads[10].wait()
    q = dot(normed, qw_ref[...])
    for h in range(heads):
        head = q[:, h * dim : (h + 1) * dim]
        q_ref[h * rows : (h + 1) * rows, :] = (head * cosine + pltpu.roll(head, half, 1) * sine).astype(BF16)
    for load in loads[6:9] + loads[11:]:
        load.wait()


def extra_body(routes_ref, weight_ref, slot_ref, sent_ref, extra_ref):
    rows = routes_ref.shape[1]
    copies = slot_ref.shape[1]
    replicas = copies // EXPERTS
    block = iota((copies, rows), 1) // (rows // replicas)
    place = iota((copies, rows), 0)
    chosen = jnp.zeros((copies, rows), F32)
    for k in range(TOP):
        named = routes_ref[k : k + 1, :] * replicas + block
        chosen = chosen + jnp.where(named == place, weight_ref[k : k + 1, :], 0.0)
    order = (iota((copies, copies), 0) == slot_ref[...]).astype(F32).astype(BF16)
    high = chosen.astype(BF16)
    low = (chosen - high.astype(F32)).astype(BF16)
    extra_ref[...] = jnp.zeros(extra_ref.shape, F32)
    for i, term in enumerate((high, low)):
        moved = lax.dot_general(term, order, (((0,), (1,)), ((), ())), preferred_element_type=F32)
        extra_ref[:, i * copies : (i + 1) * copies] = jnp.where(is_first(), moved, 0.0)


def attend_body(
    q_ref, own_ref, normed_ref, other_ref, cosine_ref, sine_ref, mine_ref, theirs_ref, group_ref, length_ref,
    position_ref, sink_ref, out_ref, token_ref, send_ref, keep_ref,
):
    rows, dim = own_ref.shape
    heads = q_ref.shape[0] // rows
    slots = mine_ref.shape[0]
    quarter = send_ref.shape[1] // 2
    scale = 1.0 / dim**0.5
    mine, theirs = mine_ref[...], theirs_ref[...]
    keys = jnp.where(is_key(), mine, theirs)
    values = jnp.where(is_key(), theirs, mine)
    scores = dot_t(q_ref[...], keys)
    other = dot(normed_ref[...], other_ref[...])
    turned = other * cosine_ref[...] + pltpu.roll(other, dim // 2, 1) * sine_ref[...]
    other = jnp.where(is_key(), other, turned).astype(BF16).astype(F32)
    own = own_ref[...].astype(F32)
    key = jnp.where(is_key(), own, other)
    value = jnp.where(is_key(), other, own)
    group, row_length, position = group_ref[...], length_ref[...], position_ref[...]
    lane = iota((rows, LANES), 1)
    seen = []
    for start in range(0, slots, LANES):
        place = lane + start % PROMPT_CAP
        seen.append((group == start // PROMPT_CAP) & (place < row_length) & (place > position - WINDOW))
    probs, own_probs = [], []
    for h in range(heads):
        span = slice(h * rows, (h + 1) * rows)
        masked = [
            jnp.where(seen[k], scores[span, k * LANES : (k + 1) * LANES] * scale, HIDE) for k in range(len(seen))
        ]
        sink = sink_ref[h : h + 1, :1]
        score = jnp.sum(q_ref[span, :].astype(F32) * key, axis=1, keepdims=True) * scale
        top = jnp.max(functools.reduce(jnp.maximum, masked), axis=1, keepdims=True)
        top = jnp.maximum(jnp.maximum(top, score), sink)
        part = [jnp.exp(m - top) for m in masked]
        fresh = jnp.exp(score - top)
        total = jnp.sum(functools.reduce(jnp.add, part), axis=1, keepdims=True) + fresh + jnp.exp(sink - top)
        inverse = 1.0 / total
        probs.append(jnp.concatenate([(p * inverse).astype(BF16) for p in part], axis=1))
        own_probs.append((fresh * inverse).astype(BF16).astype(F32))
    cached = dot(jnp.concatenate(probs, axis=0), values)
    context = [
        (cached[h * rows : (h + 1) * rows] + own_probs[h] * value).astype(BF16) for h in range(heads)
    ]
    attended = dot(jnp.concatenate(context, axis=1), out_ref[...])
    part = [attended[:, i * quarter : (i + 1) * quarter] for i in range(4)]
    for i in range(2):
        span = slice(i * quarter, (i + 1) * quarter)
        send_ref[:, span] = jnp.where(is_key(), part[2 * i + 1], part[2 * i]).astype(BF16)
        keep_ref[:, span] = jnp.where(is_key(), part[2 * i], part[2 * i + 1]) + token_ref[:, span]


def chip_body(keep_ref, extra_ref, got_ref, out_ref):
    width = got_ref.shape[1]
    out_ref[:, :width] = (keep_ref[...] + got_ref[...].astype(F32)).astype(BF16)
    out_ref[:, width:] = extra_ref[...].astype(BF16)


def relay_body(block_ref, *refs):
    refs[-1][...] = block_ref[...]


def after_all(block, earlier):
    return call(
        relay_body,
        shape(block.shape, block.dtype),
        (block, *earlier),
        free=range(1, 1 + len(earlier)),
        name="relay",
        cost=(block.size, 1 << 17),
    )


def residual_body(copies, gain_ref, own_ref, y_ref, xy_ref, x_ref, loaded_ref, rows_ref, keep_ref):
    rows, total = own_ref.shape
    width = keep_ref.shape[1]
    quarter = width // 2
    gain = [gain_ref[:, i * quarter : (i + 1) * quarter] for i in range(4)]
    gain = [jnp.where(is_key(), gain[2 * i].astype(F32), gain[2 * i + 1].astype(F32)) for i in range(2)]
    lane = iota((rows, total - width), 1)
    for i, (a_ref, b_ref) in enumerate(((own_ref, x_ref), (y_ref, xy_ref))):
        span = slice(i * rows, (i + 1) * rows)
        part = (a_ref[:, :width].astype(F32) + b_ref[:, :width].astype(F32)).astype(BF16)
        if i == 0:
            keep_ref[...] = part
        wide = part.astype(F32)
        squares = jnp.sum(wide * wide, axis=1, keepdims=True)
        scaled = wide * lax.rsqrt(squares / (2 * width) + EPSILON)
        for k in range(2):
            cols = slice(k * quarter, (k + 1) * quarter)
            rows_ref[span, cols] = (scaled[:, cols] * gain[k]).astype(BF16)
        extra = a_ref[:, width:].astype(F32) + b_ref[:, width:].astype(F32)
        squares = squares * 0.5
        high = squares.astype(BF16).astype(F32)
        extra = jnp.where(lane == 2 * copies, high, extra)
        extra = jnp.where(lane == 2 * copies + 1, squares - high, extra)
        rows_ref[span, width:] = extra.astype(BF16)


def load_body(*refs):
    sems = refs[-1]
    count = (len(refs) - 2) // 2
    loads = []
    for src, dst in zip(refs[1 : 1 + count], refs[1 + count : -1]):
        tall = src.shape[0] // CHUNKS
        for k in range(CHUNKS):
            part = pl.ds(k * tall, tall)
            loads.append(pltpu.make_async_copy(src.at[part], dst.at[part], sems.at[len(loads)]))
    for load in loads:
        load.start()
    for load in loads:
        load.wait()


def tiles(units):
    step = 256 if units % 256 == 0 else units
    return [slice(i, i + step) for i in range(0, units, step)]


def quarters(blocks, quarter, core):
    rows = jnp.concatenate([r[:, : 2 * quarter] for r in blocks], axis=0)
    for k in range(2):
        start = pl.multiple_of((2 * k + core) * quarter, LANES)
        yield rows[:, k * quarter : (k + 1) * quarter], pl.ds(start, quarter)


def half_body(blocks, *refs):
    own_refs = refs[:blocks]
    gate_ref, up_ref, gate_out, up_out = refs[blocks:]
    quarter = gate_ref.shape[1] // 4
    pairs = list(quarters(own_refs, quarter, lax.axis_index("tensor") % 2))
    for span in tiles(gate_ref.shape[0]):
        for weight_ref, out_ref in ((gate_ref, gate_out), (up_ref, up_out)):
            total = sum(dot_t(part, weight_ref[span, cols]) for part, cols in pairs)
            out_ref[:, :, span] = total.reshape(blocks, -1, total.shape[1])


def expert_body(copies, hosted, blocks, *refs):
    own_refs, other_refs = refs[:blocks], refs[blocks : 2 * blocks]
    gate_ref, up_ref, down_ref = refs[2 * blocks : 2 * blocks + 3]
    half_refs = refs[2 * blocks + 3 : -1 - blocks]
    hidden_ref, send_refs = refs[-1 - blocks], refs[-blocks:]
    total, width = gate_ref.shape
    units = total // hosted
    quarter = width // 4
    core = lax.axis_index("tensor") % 2
    extra = jnp.concatenate([r[:, 2 * quarter :] for r in own_refs], axis=0).astype(F32)
    far_extra = jnp.concatenate([r[:, 2 * quarter :] for r in other_refs], axis=0).astype(F32)
    lane = iota(extra.shape, 1)
    squared = (lane == 2 * copies) | (lane == 2 * copies + 1)
    own_mean = jnp.sum(jnp.where(squared, extra, 0.0), axis=1, keepdims=True) * (2.0 / width)
    far_mean = jnp.sum(jnp.where(squared, far_extra, 0.0), axis=1, keepdims=True) * (2.0 / width)
    scale = lax.rsqrt(own_mean + far_mean + EPSILON)
    own_scale = scale * jnp.sqrt(own_mean + EPSILON)
    far_scale = scale * jnp.sqrt(far_mean + EPSILON)
    weights = []
    for j in range(hosted):
        slot = lax.axis_index("expert") * hosted + j
        one = jnp.where((lane == slot) | (lane == slot + copies), extra, 0.0)
        weights.append(jnp.sum(one, axis=1, keepdims=True))
    own_pairs = [] if half_refs else list(quarters(own_refs, quarter, core))
    far_pairs = list(quarters(other_refs, quarter, 1 - core))
    count = extra.shape[0]
    parts = []
    for span in tiles(total):
        size = span.stop - span.start
        place = iota((count, size), 1) + span.start
        weight = weights[span.start // units]
        for j in range(span.start // units + 1, (span.stop - 1) // units + 1):
            weight = jnp.where(place >= j * units, weights[j], weight)
        sums = []
        for i, weight_ref in enumerate((gate_ref, up_ref)):
            if half_refs:
                own = half_refs[i][:, :, span].reshape(count, size)
            else:
                own = sum(dot_t(part, weight_ref[span, cols]) for part, cols in own_pairs)
            far = sum(dot_t(part, weight_ref[span, cols]) for part, cols in far_pairs)
            sums.append(own * own_scale + far * far_scale)
        parts.append((jnp.maximum(sums[0], 0.0) * sums[1] * weight).astype(BF16))
    hidden = jnp.concatenate(parts, axis=1)
    tall = count // blocks
    for b in range(blocks):
        hidden_ref[b] = hidden[b * tall : (b + 1) * tall]
    send_half(hidden, down_ref, send_refs)


def send_half(hidden, down_ref, send_refs):
    quarter = down_ref.shape[1] // 4
    tall = hidden.shape[0] // len(send_refs)
    for k in range(2):
        start = pl.multiple_of((2 * k + 1 - lax.axis_index("tensor") % 2) * quarter, LANES)
        total = dot(hidden, down_ref[:, pl.ds(start, quarter)]).astype(BF16)
        for b, send_ref in enumerate(send_refs):
            send_ref[:, k * quarter : (k + 1) * quarter] = total[b * tall : (b + 1) * tall]


def keep_body(blocks, hidden_ref, down_ref, out_ref):
    quarter = down_ref.shape[1] // 4
    tall = hidden_ref.shape[1]
    hidden = jnp.concatenate([hidden_ref[b] for b in range(blocks)], axis=0)
    for k in range(2):
        start = pl.multiple_of((2 * k + lax.axis_index("tensor") % 2) * quarter, LANES)
        total = dot(hidden, down_ref[:, pl.ds(start, quarter)])
        for b in range(blocks):
            out_ref[b, :, k * quarter : (k + 1) * quarter] = total[b * tall : (b + 1) * tall]


def chips_body(b, keep_ref, got_ref, far_ref, own_ref):
    total = keep_ref[b] + got_ref[...].astype(F32)
    groups, rows, width = far_ref.shape
    total = total.reshape(groups, 2, rows, width)
    far_ref[...] = total[:, 1].astype(far_ref.dtype)
    own_ref[...] = total[:, 0].astype(own_ref.dtype)


def pass_body(terms, *refs):
    total = refs[0][...]
    for r in refs[1:terms]:
        total = total + r[...].astype(F32)
    outs = refs[terms:]
    tall = total.shape[0] // len(outs)
    for i, r in enumerate(outs):
        r[...] = total[i * tall : (i + 1) * tall].astype(r.dtype)


def sum_body(terms, *refs):
    total = refs[0][...]
    for r in refs[1:terms]:
        total = total + r[...].astype(F32)
    for r in refs[terms:]:
        r[...] = total.reshape(r.shape).astype(r.dtype)


def combine_body(own_ref, x_ref, y_ref, xy_ref, residual_ref, combined_ref, square_ref):
    quarter = combined_ref.shape[1]
    total = (own_ref[...] + x_ref[...].astype(F32)) + (y_ref[...].astype(F32) + xy_ref[...].astype(F32))
    total = residual_ref[...].astype(F32) + total
    combined_ref[...] = jnp.where(is_first(), total[:, :quarter], total[:, quarter:])
    square_ref[...] = jnp.broadcast_to(jnp.sum(total * total, axis=1, keepdims=True), square_ref.shape)


def finish_body(width, combined_ref, gain_ref, a_ref, b_ref, out_ref):
    mean = (a_ref[...] + b_ref[...])[:, :1] / width
    out_ref[...] = (combined_ref[...] * lax.rsqrt(mean + EPSILON) * gain_ref[...].astype(F32)).astype(BF16)


def run_experts(own, other, gate_weight, up_weight, down_weight, hosted, copies, rows, first):
    blocks = len(own)
    tall, total = own[0].shape
    units, width = gate_weight.shape
    step = min(tall, 64)
    grid = (tall // step,) if tall > step else ()

    def spec(dims, place):
        if not grid:
            return pl.BlockSpec(memory_space=pltpu.VMEM)
        return pl.BlockSpec(dims, place)

    row_spec = spec((step, total), lambda i: (i, 0))
    half_spec = spec((step, width // 2), lambda i: (i, 0))
    keep_spec = spec((blocks, step, width // 2), lambda i: (0, i, 0))
    hidden_spec = spec((blocks, step, units), lambda i: (0, i, 0))
    whole = pl.BlockSpec(memory_space=pltpu.VMEM)
    params = pltpu.CompilerParams(vmem_limit_bytes=32 << 20)
    tiny = pl.CostEstimate(flops=1, bytes_accessed=1, transcendentals=0)
    halves = []
    if not first:
        halves = pl.pallas_call(
            functools.partial(half_body, blocks),
            grid=grid,
            out_shape=[shape((blocks, tall, units), F32)] * 2,
            in_specs=[row_spec] * blocks + [whole] * 2,
            out_specs=[hidden_spec] * 2,
            compiler_params=params,
            cost_estimate=tiny,
            name="experts_half_depth",
        )(*own, gate_weight, up_weight)
    hidden, *sends = pl.pallas_call(
        functools.partial(expert_body, copies, hosted, blocks),
        grid=grid,
        out_shape=[shape((blocks, tall, units), BF16)] + [shape((tall, width // 2), BF16)] * blocks,
        in_specs=[row_spec] * (2 * blocks) + [whole] * 3 + [hidden_spec] * len(halves),
        out_specs=[hidden_spec] + [half_spec] * blocks,
        compiler_params=params,
        cost_estimate=tiny,
        name="experts",
    )(*own, *other, gate_weight, up_weight, down_weight, *halves)
    got = [swap(send, "tensor", 1) for send in sends]
    keep = pl.pallas_call(
        functools.partial(keep_body, blocks),
        grid=grid,
        out_shape=shape((blocks, tall, width // 2), F32),
        in_specs=[hidden_spec, whole],
        out_specs=keep_spec,
        compiler_params=params,
        cost_estimate=tiny,
        name="experts_own_half",
    )(hidden, down_weight)
    sums = [
        call(
            functools.partial(chips_body, b),
            [shape((tall // (2 * rows), rows, width // 2), F32 if first else BF16)] * 2,
            (keep, got[b]),
            vmem=48 << 20,
            name="chip_sums",
            cost=(1, 1),
        )
        for b in range(blocks)
    ]
    return sums, sends[0], got[0]


def on_device(
    tokens, attn_gain, query_weight, key_value_weight, paired_cache, prompt_length, group_index, offsets,
    sink_logit, out_weight, mixer_gain, routes, route_weight, copy_slot, gate_weight, up_weight, down_weight,
    final_gain,
):
    rows, width = tokens.shape
    dim = key_value_weight.shape[2]
    heads = query_weight.shape[1] // dim
    half, quarter = width // 2, width // 4
    slots = paired_cache.shape[2]
    copies = copy_slot.shape[0]
    far = lax.axis_size("expert") // 2
    extra_width = -(-(2 * copies + 2) // LANES) * LANES
    hosted = gate_weight.shape[0]
    gate_weight = jnp.swapaxes(gate_weight, 1, 2).reshape(-1, width)
    up_weight = jnp.swapaxes(up_weight, 1, 2).reshape(-1, width)
    down_weight = down_weight.reshape(-1, width)

    other_cache = swap(paired_cache[0, 0], "tensor", 1)
    other_weight = swap(key_value_weight[0], "tensor", 1)
    place = shape((rows, LANES), I32)
    turn = shape((rows, dim), F32)
    queries, own_new, normed, cosine, sine, own_cache, token_half, *rest, named, named_weight, slot = call(
        project_body,
        [
            shape((heads * rows, dim), BF16), shape((rows, dim), BF16), shape((rows, width), BF16), turn, turn,
            shape((slots, dim), BF16), shape((rows, half), F32), place, place, place, shape((8, LANES), F32),
            shape((TOP, rows), I32), shape((TOP, rows), F32), shape((1, copies), I32),
        ],
        (
            prompt_length, group_index, offsets, tokens, attn_gain, key_value_weight, query_weight,
            paired_cache, routes.T, route_weight.T, copy_slot[None, :], sink_logit,
        ),
        hbm=range(12),
        scratch=[
            pltpu.SMEM(prompt_length.shape, I32),
            pltpu.SMEM(group_index.shape, I32),
            pltpu.SMEM(offsets.shape, I32),
            pltpu.SMEM(sink_logit.shape, F32),
            pltpu.VMEM(tokens.shape, BF16),
            pltpu.VMEM((width,), BF16),
            pltpu.VMEM(key_value_weight.shape[1:], BF16),
            pltpu.VMEM(query_weight.shape, BF16),
            pltpu.SemaphoreType.DMA((12,)),
        ],
        name="project",
        cost=(2 * rows * width * (heads + 1) * dim, 2 << 20),
    )
    send, keep = call(
        attend_body,
        [shape((rows, half), BF16), shape((rows, half), F32)],
        (queries, own_new, normed, other_weight, cosine, sine, own_cache, other_cache, *rest, out_weight, token_half),
        name="attention",
        cost=(4 * heads * rows * dim * slots, 1 << 20),
    )
    extra = call(
        extra_body,
        shape((rows, extra_width), F32),
        (named, named_weight, slot, send),
        free=[3],
        name="route_columns",
    )
    own = call(
        chip_body, shape((rows, half + extra_width), BF16), (keep, extra, swap(send, "tensor", 1)), name="chip_sum",
        cost=(rows * width, 1 << 18),
    )
    far_y, far_xy, near_x = swap(own, "expert", far), swap_both(own, far, 2), swap(own, "tensor", 2)
    weights = (gate_weight, up_weight, down_weight)
    weights = call(
        load_body,
        [shape(w.shape, BF16) for w in weights],
        (own, *weights),
        hbm=range(1, 4),
        scratch=[pltpu.SemaphoreType.DMA((len(weights) * CHUNKS,))],
        name="load_experts",
        cost=(0, 8 << 20),
    )
    block, residual = call(
        functools.partial(residual_body, copies),
        [shape((2 * rows, half + extra_width), BF16), shape((rows, half), BF16)],
        (mixer_gain[None, :], own, far_y, far_xy, near_x, weights[0]),
        free=[5],
        name="residual",
        cost=(rows * width, 1 << 18),
    )

    bit, stages = 1, []
    while bit < far:
        stages.append([bit] if 2 * bit >= far else [bit, 2 * bit, 3 * bit])
        bit *= 4
    blocks = [block]
    for stage in stages:
        whole = blocks[0] if len(blocks) == 1 else jnp.concatenate(blocks, axis=0)
        blocks = [whole] + [swap(whole, "expert", b) for b in stage]
    pieces = []
    for group in (blocks[:1], blocks[1:]):
        if pieces:
            group = [after_all(b, [got if i else send]) for i, b in enumerate(group)]
        others = [swap(b, "tensor", 1) for b in group]
        sums, send, got = run_experts(group, others, *weights, hosted, copies, rows, not pieces)
        pieces += sums
    def scatter(pieces):
        terms = [pieces[0]] + [swap(p, "expert", b) for p, b in zip(pieces[1:], stages[-1])]
        for stage in stages[-2::-1]:
            part = (terms[0].shape[0] // (len(stage) + 1), rows, half)
            pieces = call(
                functools.partial(pass_body, len(terms)),
                [shape(part, F32)] + [shape(part, BF16)] * len(stage),
                terms,
                vmem=48 << 20,
                name="pass_on",
            )
            terms = [pieces[0]] + [swap(p, "expert", b) for p, b in zip(pieces[1:], stage)]
        return terms

    def sum_of(terms, kinds):
        return call(
            functools.partial(sum_body, len(terms)),
            [shape((rows, half), k) for k in kinds],
            terms,
            name="sums",
            cost=(rows * width, 1 << 18),
        )

    far_terms, own_terms = scatter([p[0] for p in pieces]), scatter([p[1] for p in pieces])
    (far_part,) = sum_of(far_terms, (BF16,))
    far_y, far_xy = swap(far_part, "expert", far), swap_both(far_part, far, 2)
    own, x_part = sum_of(own_terms, (F32, BF16))
    near_x = swap(x_part, "tensor", 2)
    combined, squares = call(
        combine_body,
        [shape((rows, quarter), F32), shape((rows, LANES), F32)],
        (own, near_x, far_y, far_xy, residual),
        name="combine",
        cost=(rows * width, 1 << 18),
    )
    return call(
        functools.partial(finish_body, width),
        shape((rows, quarter), BF16),
        (combined, final_gain[None, :], squares, swap(squares, "tensor", 1)),
        name="finish",
        cost=(rows * width, 1 << 18),
    )


def solution(mesh):
    in_specs = (
        P("expert", None),
        P(),
        P(None, "tensor"),
        P("tensor", None, None),
        P("expert", "tensor", None, None),
        P("expert", None),
        P("expert"),
        P("expert"),
        P("tensor"),
        P("tensor", None),
        P(),
        P("expert", None),
        P("expert", None),
        P(),
        P("expert", None, "tensor"),
        P("expert", None, "tensor"),
        P("expert", "tensor", None),
        P("tensor"),
    )
    out_specs = P("expert", "tensor")
    return jax.shard_map(
        on_device, mesh=mesh, in_specs=in_specs, out_specs=out_specs, check_vma=False
    )
```

```python
import functools
import math

import jax
import jax.numpy as jnp
from jax import lax
from jax.experimental import pallas as pl
from jax.experimental.pallas import tpu as pltpu
from jax.sharding import PartitionSpec as P

EXPERTS = 32
TOP = 4
PROMPT_CAP = 256
WINDOW = 192
EPSILON = 1e-06
LANES = 128
CHUNKS = 4
HIDE = -1e30
F32 = jnp.float32
BF16 = jnp.bfloat16
I32 = jnp.int32


def swap(block, axis, bits):
    count = lax.axis_size(axis)
    return lax.ppermute(block, axis, [(i, i ^ bits) for i in range(count)])


def swap_both(block, expert_bits, tensor_bits):
    lanes = lax.axis_size("tensor")
    count = lax.axis_size("expert") * lanes
    bits = expert_bits * lanes + tensor_bits
    return lax.ppermute(block, ("expert", "tensor"), [(i, i ^ bits) for i in range(count)])


def iota(shape, dim):
    return lax.broadcasted_iota(I32, shape, dim)


def dot(a, b):
    return jnp.dot(a, b, preferred_element_type=F32)


def dot_t(a, b):
    return lax.dot_general(a, b, (((1,), (1,)), ((), ())), preferred_element_type=F32)


def call(body, outs, args, hbm=(), free=(), scratch=(), vmem=None, cost=None, name=None):
    in_specs = [
        pl.BlockSpec(memory_space=pltpu.HBM if i in hbm else pl.ANY if i in free else pltpu.VMEM)
        for i in range(len(args))
    ]
    args = [pltpu.with_memory_space_constraint(a, pltpu.HBM) if i in hbm else a for i, a in enumerate(args)]
    single = not isinstance(outs, (list, tuple))
    listed = [outs] if single else list(outs)
    out_specs = [pl.BlockSpec(memory_space=pltpu.VMEM) for _ in listed]
    flops, nbytes = cost or (0, 0)
    result = pl.pallas_call(
        body,
        out_shape=listed,
        in_specs=in_specs,
        out_specs=out_specs,
        scratch_shapes=list(scratch),
        compiler_params=pltpu.CompilerParams(vmem_limit_bytes=vmem or 16 << 20),
        cost_estimate=pl.CostEstimate(flops=flops, bytes_accessed=nbytes, transcendentals=0),
        name=name,
    )(*args)
    return result[0] if single else result


def shape(dims, dtype):
    return jax.ShapeDtypeStruct(tuple(dims), dtype)


def spread(rows, values):
    index = iota((rows, LANES), 0)
    total = jnp.full((rows, LANES), values[0])
    for i in range(1, len(values)):
        total = jnp.where(index == i, values[i], total)
    return total


def is_key():
    return lax.axis_index("tensor") % 2 == 0


def is_first():
    return lax.axis_index("tensor") < 2


def project_body(
    length_hbm, group_hbm, offset_hbm, tok_hbm, gain_hbm, kvw_hbm, qw_hbm, cache_hbm, routes_hbm, weight_hbm,
    slot_hbm, sink_hbm,
    q_ref, own_ref, normed_ref, cosine_ref, sine_ref, cache_ref, token_ref, group_out, length_out, position_out,
    sink_out, routes_ref, weight_ref, slot_ref,
    length_ref, group_ref, offset_ref, sink_ref, tok_ref, gain_ref, kvw_ref, qw_ref, sems,
):
    rows, width = tok_ref.shape
    pairs = [
        (length_hbm, length_ref), (group_hbm, group_ref), (offset_hbm, offset_ref), (tok_hbm, tok_ref),
        (gain_hbm, gain_ref), (kvw_hbm.at[0], kvw_ref), (routes_hbm, routes_ref), (weight_hbm, weight_ref),
        (slot_hbm, slot_ref), (sink_hbm, sink_ref),
    ]
    pairs += [(qw_hbm, qw_ref), (cache_hbm.at[0, 0], cache_ref)]
    loads = [pltpu.make_async_copy(src, dst, sems.at[i]) for i, (src, dst) in enumerate(pairs)]
    for load in loads:
        load.start()
    dim = kvw_ref.shape[1]
    heads = qw_ref.shape[1] // dim
    half = dim // 2
    quarter = width // 4
    for load in loads[:3]:
        load.wait()
    groups = [group_ref[i] for i in range(rows)]
    lengths = [length_ref[0, g] for g in groups]
    group_out[...] = spread(rows, groups)
    length_out[...] = spread(rows, lengths)
    position = spread(rows, [lengths[i] + offset_ref[i] for i in range(rows)])
    position_out[...] = position
    lane = iota((rows, dim), 1)
    step = jnp.where(lane >= half, lane - half, lane).astype(F32)
    angle = position.astype(F32) * jnp.exp(step * (-math.log(10000.0) / half))
    cosine = jnp.cos(angle)
    sine = jnp.sin(angle)
    sine = jnp.where(lane < half, -sine, sine)
    cosine_ref[...] = cosine
    sine_ref[...] = sine
    loads[3].wait()
    loads[4].wait()
    tok = tok_ref[...].astype(F32)
    mean = jnp.sum(tok * tok, axis=1, keepdims=True) / width
    normed = (tok * lax.rsqrt(mean + EPSILON) * gain_ref[...].astype(F32).reshape(1, width)).astype(BF16)
    for i in range(2):
        low, high = (tok[:, (2 * i + k) * quarter : (2 * i + k + 1) * quarter] for k in range(2))
        token_ref[:, i * quarter : (i + 1) * quarter] = jnp.where(
            is_first(), jnp.where(is_key(), low, high), 0.0
        )
    normed_ref[...] = normed
    loads[9].wait()
    sink_out[...] = spread(sink_out.shape[0], [sink_ref[i] for i in range(heads)])
    loads[5].wait()
    own = dot(normed, kvw_ref[...])
    turned = own * cosine + pltpu.roll(own, half, 1) * sine
    own_ref[...] = jnp.where(is_key(), turned, own).astype(BF16)
    loads[10].wait()
    q = dot(normed, qw_ref[...])
    for h in range(heads):
        head = q[:, h * dim : (h + 1) * dim]
        q_ref[h * rows : (h + 1) * rows, :] = (head * cosine + pltpu.roll(head, half, 1) * sine).astype(BF16)
    for load in loads[6:9] + loads[11:]:
        load.wait()


def extra_body(routes_ref, weight_ref, slot_ref, sent_ref, extra_ref):
    rows = routes_ref.shape[1]
    copies = slot_ref.shape[1]
    replicas = copies // EXPERTS
    block = iota((copies, rows), 1) // (rows // replicas)
    place = iota((copies, rows), 0)
    chosen = jnp.zeros((copies, rows), F32)
    for k in range(TOP):
        named = routes_ref[k : k + 1, :] * replicas + block
        chosen = chosen + jnp.where(named == place, weight_ref[k : k + 1, :], 0.0)
    order = (iota((copies, copies), 0) == slot_ref[...]).astype(F32).astype(BF16)
    high = chosen.astype(BF16)
    low = (chosen - high.astype(F32)).astype(BF16)
    extra_ref[...] = jnp.zeros(extra_ref.shape, F32)
    for i, term in enumerate((high, low)):
        moved = lax.dot_general(term, order, (((0,), (1,)), ((), ())), preferred_element_type=F32)
        extra_ref[:, i * copies : (i + 1) * copies] = jnp.where(is_first(), moved, 0.0)


def attend_body(
    q_ref, own_ref, normed_ref, other_ref, cosine_ref, sine_ref, mine_ref, theirs_ref, group_ref, length_ref,
    position_ref, sink_ref, out_ref, token_ref, send_ref, keep_ref,
):
    rows, dim = own_ref.shape
    heads = q_ref.shape[0] // rows
    slots = mine_ref.shape[0]
    quarter = send_ref.shape[1] // 2
    scale = 1.0 / dim**0.5
    mine, theirs = mine_ref[...], theirs_ref[...]
    keys = jnp.where(is_key(), mine, theirs)
    values = jnp.where(is_key(), theirs, mine)
    scores = dot_t(q_ref[...], keys)
    other = dot(normed_ref[...], other_ref[...])
    turned = other * cosine_ref[...] + pltpu.roll(other, dim // 2, 1) * sine_ref[...]
    other = jnp.where(is_key(), other, turned).astype(BF16).astype(F32)
    own = own_ref[...].astype(F32)
    key = jnp.where(is_key(), own, other)
    value = jnp.where(is_key(), other, own)
    group, row_length, position = group_ref[...], length_ref[...], position_ref[...]
    lane = iota((rows, LANES), 1)
    seen = []
    for start in range(0, slots, LANES):
        place = lane + start % PROMPT_CAP
        seen.append((group == start // PROMPT_CAP) & (place < row_length) & (place > position - WINDOW))
    probs, own_probs = [], []
    for h in range(heads):
        span = slice(h * rows, (h + 1) * rows)
        masked = [
            jnp.where(seen[k], scores[span, k * LANES : (k + 1) * LANES] * scale, HIDE) for k in range(len(seen))
        ]
        sink = sink_ref[h : h + 1, :1]
        score = jnp.sum(q_ref[span, :].astype(F32) * key, axis=1, keepdims=True) * scale
        top = jnp.max(functools.reduce(jnp.maximum, masked), axis=1, keepdims=True)
        top = jnp.maximum(jnp.maximum(top, score), sink)
        part = [jnp.exp(m - top) for m in masked]
        fresh = jnp.exp(score - top)
        total = jnp.sum(functools.reduce(jnp.add, part), axis=1, keepdims=True) + fresh + jnp.exp(sink - top)
        inverse = 1.0 / total
        probs.append(jnp.concatenate([(p * inverse).astype(BF16) for p in part], axis=1))
        own_probs.append((fresh * inverse).astype(BF16).astype(F32))
    cached = dot(jnp.concatenate(probs, axis=0), values)
    context = [
        (cached[h * rows : (h + 1) * rows] + own_probs[h] * value).astype(BF16) for h in range(heads)
    ]
    attended = dot(jnp.concatenate(context, axis=1), out_ref[...])
    part = [attended[:, i * quarter : (i + 1) * quarter] for i in range(4)]
    for i in range(2):
        span = slice(i * quarter, (i + 1) * quarter)
        send_ref[:, span] = jnp.where(is_key(), part[2 * i + 1], part[2 * i]).astype(BF16)
        keep_ref[:, span] = jnp.where(is_key(), part[2 * i], part[2 * i + 1]) + token_ref[:, span]


def chip_body(keep_ref, extra_ref, got_ref, out_ref):
    width = got_ref.shape[1]
    out_ref[:, :width] = (keep_ref[...] + got_ref[...].astype(F32)).astype(BF16)
    out_ref[:, width:] = extra_ref[...].astype(BF16)


def relay_body(block_ref, *refs):
    refs[-1][...] = block_ref[...]


def after_all(block, earlier):
    return call(
        relay_body,
        shape(block.shape, block.dtype),
        (block, *earlier),
        free=range(1, 1 + len(earlier)),
        name="relay",
        cost=(block.size, 1 << 17),
    )


def residual_body(copies, gain_ref, own_ref, xy_ref, y_ref, x_ref, loaded_ref, rows_ref, keep_ref):
    rows, total = own_ref.shape
    width = keep_ref.shape[1]
    quarter = width // 2
    gain = [gain_ref[:, i * quarter : (i + 1) * quarter] for i in range(4)]
    gain = [jnp.where(is_key(), gain[2 * i].astype(F32), gain[2 * i + 1].astype(F32)) for i in range(2)]
    lane = iota((rows, total - width), 1)
    for i, (a_ref, b_ref) in enumerate(((own_ref, x_ref), (y_ref, xy_ref))):
        span = slice(i * rows, (i + 1) * rows)
        part = (a_ref[:, :width].astype(F32) + b_ref[:, :width].astype(F32)).astype(BF16)
        if i == 0:
            keep_ref[...] = part
        wide = part.astype(F32)
        squares = jnp.sum(wide * wide, axis=1, keepdims=True)
        scaled = wide * lax.rsqrt(squares / (2 * width) + EPSILON)
        for k in range(2):
            cols = slice(k * quarter, (k + 1) * quarter)
            rows_ref[span, cols] = (scaled[:, cols] * gain[k]).astype(BF16)
        extra = a_ref[:, width:].astype(F32) + b_ref[:, width:].astype(F32)
        squares = squares * 0.5
        high = squares.astype(BF16).astype(F32)
        extra = jnp.where(lane == 2 * copies, high, extra)
        extra = jnp.where(lane == 2 * copies + 1, squares - high, extra)
        rows_ref[span, width:] = extra.astype(BF16)


def load_body(*refs):
    sems = refs[-1]
    count = (len(refs) - 2) // 2
    loads = []
    for src, dst in zip(refs[1 : 1 + count], refs[1 + count : -1]):
        tall = src.shape[0] // CHUNKS
        for k in range(CHUNKS):
            part = pl.ds(k * tall, tall)
            loads.append(pltpu.make_async_copy(src.at[part], dst.at[part], sems.at[len(loads)]))
    for load in loads:
        load.start()
    for load in loads:
        load.wait()


def tiles(units):
    step = 256 if units % 256 == 0 else units
    return [slice(i, i + step) for i in range(0, units, step)]


def quarters(blocks, quarter, core):
    rows = jnp.concatenate([r[:, : 2 * quarter] for r in blocks], axis=0)
    for k in range(2):
        start = pl.multiple_of((2 * k + core) * quarter, LANES)
        yield rows[:, k * quarter : (k + 1) * quarter], pl.ds(start, quarter)


def half_body(blocks, *refs):
    own_refs = refs[:blocks]
    gate_ref, up_ref, gate_out, up_out = refs[blocks:]
    quarter = gate_ref.shape[1] // 4
    pairs = list(quarters(own_refs, quarter, lax.axis_index("tensor") % 2))
    for span in tiles(gate_ref.shape[0]):
        for weight_ref, out_ref in ((gate_ref, gate_out), (up_ref, up_out)):
            total = sum(dot_t(part, weight_ref[span, cols]) for part, cols in pairs)
            out_ref[:, :, span] = total.reshape(blocks, -1, total.shape[1])


def expert_body(copies, hosted, blocks, *refs):
    own_refs, other_refs = refs[:blocks], refs[blocks : 2 * blocks]
    gate_ref, up_ref, down_ref = refs[2 * blocks : 2 * blocks + 3]
    half_refs = refs[2 * blocks + 3 : -1 - blocks]
    hidden_ref, send_refs = refs[-1 - blocks], refs[-blocks:]
    total, width = gate_ref.shape
    units = total // hosted
    quarter = width // 4
    core = lax.axis_index("tensor") % 2
    extra = jnp.concatenate([r[:, 2 * quarter :] for r in own_refs], axis=0).astype(F32)
    far_extra = jnp.concatenate([r[:, 2 * quarter :] for r in other_refs], axis=0).astype(F32)
    lane = iota(extra.shape, 1)
    squared = (lane == 2 * copies) | (lane == 2 * copies + 1)
    own_mean = jnp.sum(jnp.where(squared, extra, 0.0), axis=1, keepdims=True) * (2.0 / width)
    far_mean = jnp.sum(jnp.where(squared, far_extra, 0.0), axis=1, keepdims=True) * (2.0 / width)
    scale = lax.rsqrt(own_mean + far_mean + EPSILON)
    own_scale = scale * jnp.sqrt(own_mean + EPSILON)
    far_scale = scale * jnp.sqrt(far_mean + EPSILON)
    weights = []
    for j in range(hosted):
        slot = lax.axis_index("expert") * hosted + j
        one = jnp.where((lane == slot) | (lane == slot + copies), extra, 0.0)
        weights.append(jnp.sum(one, axis=1, keepdims=True))
    own_pairs = [] if half_refs else list(quarters(own_refs, quarter, core))
    far_pairs = list(quarters(other_refs, quarter, 1 - core))
    count = extra.shape[0]
    parts = []
    for span in tiles(total):
        size = span.stop - span.start
        place = iota((count, size), 1) + span.start
        weight = weights[span.start // units]
        for j in range(span.start // units + 1, (span.stop - 1) // units + 1):
            weight = jnp.where(place >= j * units, weights[j], weight)
        sums = []
        for i, weight_ref in enumerate((gate_ref, up_ref)):
            if half_refs:
                own = half_refs[i][:, :, span].reshape(count, size)
            else:
                own = sum(dot_t(part, weight_ref[span, cols]) for part, cols in own_pairs)
            far = sum(dot_t(part, weight_ref[span, cols]) for part, cols in far_pairs)
            sums.append(own * own_scale + far * far_scale)
        parts.append((jnp.maximum(sums[0], 0.0) * sums[1] * weight).astype(BF16))
    hidden = jnp.concatenate(parts, axis=1)
    tall = count // blocks
    for b in range(blocks):
        hidden_ref[b] = hidden[b * tall : (b + 1) * tall]
    send_half(hidden, down_ref, send_refs)


def send_half(hidden, down_ref, send_refs):
    quarter = down_ref.shape[1] // 4
    tall = hidden.shape[0] // len(send_refs)
    for k in range(2):
        start = pl.multiple_of((2 * k + 1 - lax.axis_index("tensor") % 2) * quarter, LANES)
        total = dot(hidden, down_ref[:, pl.ds(start, quarter)]).astype(BF16)
        for b, send_ref in enumerate(send_refs):
            send_ref[:, k * quarter : (k + 1) * quarter] = total[b * tall : (b + 1) * tall]


def keep_body(blocks, hidden_ref, down_ref, out_ref):
    quarter = down_ref.shape[1] // 4
    tall = hidden_ref.shape[1]
    hidden = jnp.concatenate([hidden_ref[b] for b in range(blocks)], axis=0)
    for k in range(2):
        start = pl.multiple_of((2 * k + lax.axis_index("tensor") % 2) * quarter, LANES)
        total = dot(hidden, down_ref[:, pl.ds(start, quarter)])
        for b in range(blocks):
            out_ref[b, :, k * quarter : (k + 1) * quarter] = total[b * tall : (b + 1) * tall]


def chips_body(b, keep_ref, got_ref, far_ref, own_ref):
    total = keep_ref[b] + got_ref[...].astype(F32)
    groups, rows, width = far_ref.shape
    total = total.reshape(groups, 2, rows, width)
    far_ref[...] = total[:, 1].astype(far_ref.dtype)
    own_ref[...] = total[:, 0].astype(own_ref.dtype)


def pass_body(terms, *refs):
    total = refs[0][...]
    for r in refs[1:terms]:
        total = total + r[...].astype(F32)
    outs = refs[terms:]
    tall = total.shape[0] // len(outs)
    for i, r in enumerate(outs):
        r[...] = total[i * tall : (i + 1) * tall].astype(r.dtype)


def sum_body(terms, *refs):
    total = refs[0][...]
    for r in refs[1:terms]:
        total = total + r[...].astype(F32)
    for r in refs[terms:]:
        r[...] = total.reshape(r.shape).astype(r.dtype)


def combine_body(own_ref, x_ref, y_ref, xy_ref, residual_ref, combined_ref, square_ref):
    quarter = combined_ref.shape[1]
    total = (own_ref[...] + x_ref[...].astype(F32)) + (y_ref[...].astype(F32) + xy_ref[...].astype(F32))
    total = residual_ref[...].astype(F32) + total
    combined_ref[...] = jnp.where(is_first(), total[:, :quarter], total[:, quarter:])
    square_ref[...] = jnp.broadcast_to(jnp.sum(total * total, axis=1, keepdims=True), square_ref.shape)


def finish_body(width, combined_ref, gain_ref, a_ref, b_ref, out_ref):
    mean = (a_ref[...] + b_ref[...])[:, :1] / width
    out_ref[...] = (combined_ref[...] * lax.rsqrt(mean + EPSILON) * gain_ref[...].astype(F32)).astype(BF16)


def run_experts(own, other, gate_weight, up_weight, down_weight, hosted, copies, rows, first):
    blocks = len(own)
    tall, total = own[0].shape
    units, width = gate_weight.shape
    step = min(tall, 64)
    grid = (tall // step,) if tall > step else ()

    def spec(dims, place):
        if not grid:
            return pl.BlockSpec(memory_space=pltpu.VMEM)
        return pl.BlockSpec(dims, place)

    row_spec = spec((step, total), lambda i: (i, 0))
    half_spec = spec((step, width // 2), lambda i: (i, 0))
    keep_spec = spec((blocks, step, width // 2), lambda i: (0, i, 0))
    hidden_spec = spec((blocks, step, units), lambda i: (0, i, 0))
    whole = pl.BlockSpec(memory_space=pltpu.VMEM)
    params = pltpu.CompilerParams(vmem_limit_bytes=32 << 20)
    tiny = pl.CostEstimate(flops=1, bytes_accessed=1, transcendentals=0)
    halves = []
    if not first:
        halves = pl.pallas_call(
            functools.partial(half_body, blocks),
            grid=grid,
            out_shape=[shape((blocks, tall, units), F32)] * 2,
            in_specs=[row_spec] * blocks + [whole] * 2,
            out_specs=[hidden_spec] * 2,
            compiler_params=params,
            cost_estimate=tiny,
            name="experts_half_depth",
        )(*own, gate_weight, up_weight)
    hidden, *sends = pl.pallas_call(
        functools.partial(expert_body, copies, hosted, blocks),
        grid=grid,
        out_shape=[shape((blocks, tall, units), BF16)] + [shape((tall, width // 2), BF16)] * blocks,
        in_specs=[row_spec] * (2 * blocks) + [whole] * 3 + [hidden_spec] * len(halves),
        out_specs=[hidden_spec] + [half_spec] * blocks,
        compiler_params=params,
        cost_estimate=tiny,
        name="experts",
    )(*own, *other, gate_weight, up_weight, down_weight, *halves)
    got = [swap(send, "tensor", 1) for send in sends]
    keep = pl.pallas_call(
        functools.partial(keep_body, blocks),
        grid=grid,
        out_shape=shape((blocks, tall, width // 2), F32),
        in_specs=[hidden_spec, whole],
        out_specs=keep_spec,
        compiler_params=params,
        cost_estimate=tiny,
        name="experts_own_half",
    )(hidden, down_weight)
    sums = [
        call(
            functools.partial(chips_body, b),
            [shape((tall // (2 * rows), rows, width // 2), F32 if first else BF16)] * 2,
            (keep, got[b]),
            vmem=48 << 20,
            name="chip_sums",
            cost=(1, 1),
        )
        for b in range(blocks)
    ]
    return sums, sends[0], got[0]


def on_device(
    tokens, attn_gain, query_weight, key_value_weight, paired_cache, prompt_length, group_index, offsets,
    sink_logit, out_weight, mixer_gain, routes, route_weight, copy_slot, gate_weight, up_weight, down_weight,
    final_gain,
):
    rows, width = tokens.shape
    dim = key_value_weight.shape[2]
    heads = query_weight.shape[1] // dim
    half, quarter = width // 2, width // 4
    slots = paired_cache.shape[2]
    copies = copy_slot.shape[0]
    far = lax.axis_size("expert") // 2
    extra_width = -(-(2 * copies + 2) // LANES) * LANES
    hosted = gate_weight.shape[0]
    gate_weight = jnp.swapaxes(gate_weight, 1, 2).reshape(-1, width)
    up_weight = jnp.swapaxes(up_weight, 1, 2).reshape(-1, width)
    down_weight = down_weight.reshape(-1, width)

    other_cache = swap(paired_cache[0, 0], "tensor", 1)
    other_weight = swap(key_value_weight[0], "tensor", 1)
    place = shape((rows, LANES), I32)
    turn = shape((rows, dim), F32)
    queries, own_new, normed, cosine, sine, own_cache, token_half, *rest, named, named_weight, slot = call(
        project_body,
        [
            shape((heads * rows, dim), BF16), shape((rows, dim), BF16), shape((rows, width), BF16), turn, turn,
            shape((slots, dim), BF16), shape((rows, half), F32), place, place, place, shape((8, LANES), F32),
            shape((TOP, rows), I32), shape((TOP, rows), F32), shape((1, copies), I32),
        ],
        (
            prompt_length, group_index, offsets, tokens, attn_gain, key_value_weight, query_weight,
            paired_cache, routes.T, route_weight.T, copy_slot[None, :], sink_logit,
        ),
        hbm=range(12),
        scratch=[
            pltpu.SMEM(prompt_length.shape, I32),
            pltpu.SMEM(group_index.shape, I32),
            pltpu.SMEM(offsets.shape, I32),
            pltpu.SMEM(sink_logit.shape, F32),
            pltpu.VMEM(tokens.shape, BF16),
            pltpu.VMEM((width,), BF16),
            pltpu.VMEM(key_value_weight.shape[1:], BF16),
            pltpu.VMEM(query_weight.shape, BF16),
            pltpu.SemaphoreType.DMA((12,)),
        ],
        name="project",
        cost=(2 * rows * width * (heads + 1) * dim, 2 << 20),
    )
    send, keep = call(
        attend_body,
        [shape((rows, half), BF16), shape((rows, half), F32)],
        (queries, own_new, normed, other_weight, cosine, sine, own_cache, other_cache, *rest, out_weight, token_half),
        name="attention",
        cost=(4 * heads * rows * dim * slots, 1 << 20),
    )
    extra = call(
        extra_body,
        shape((rows, extra_width), F32),
        (named, named_weight, slot, send),
        free=[3],
        name="route_columns",
    )
    own = call(
        chip_body, shape((rows, half + extra_width), BF16), (keep, extra, swap(send, "tensor", 1)), name="chip_sum",
        cost=(rows * width, 1 << 18),
    )
    far_y, far_xy, near_x = swap(own, "expert", far), swap_both(own, far, 2), swap(own, "tensor", 2)
    weights = (gate_weight, up_weight, down_weight)
    weights = call(
        load_body,
        [shape(w.shape, BF16) for w in weights],
        (own, *weights),
        hbm=range(1, 4),
        scratch=[pltpu.SemaphoreType.DMA((len(weights) * CHUNKS,))],
        name="load_experts",
        cost=(0, 8 << 20),
    )
    block, residual = call(
        functools.partial(residual_body, copies),
        [shape((2 * rows, half + extra_width), BF16), shape((rows, half), BF16)],
        (mixer_gain[None, :], own, far_xy, far_y, near_x, weights[0]),
        free=[5],
        name="residual",
        cost=(rows * width, 1 << 18),
    )

    bit, stages = 1, []
    while bit < far:
        stages.append([bit] if 2 * bit >= far else [3 * bit, bit, 2 * bit])
        bit *= 4
    blocks = [block]
    for stage in stages:
        whole = blocks[0] if len(blocks) == 1 else jnp.concatenate(blocks, axis=0)
        blocks = [whole] + [swap(whole, "expert", b) for b in stage]
    pieces = []
    for group in (blocks[:1], blocks[1:]):
        if pieces:
            group = [after_all(b, [got if i else send]) for i, b in enumerate(group)]
        others = [swap(b, "tensor", 1) for b in group]
        sums, send, got = run_experts(group, others, *weights, hosted, copies, rows, not pieces)
        pieces += sums
    def scatter(pieces):
        terms = [pieces[0]] + [swap(p, "expert", b) for p, b in zip(pieces[1:], stages[-1])][::-1]
        for stage in stages[-2::-1]:
            part = (terms[0].shape[0] // (len(stage) + 1), rows, half)
            pieces = call(
                functools.partial(pass_body, len(terms)),
                [shape(part, F32)] + [shape(part, BF16)] * len(stage),
                terms,
                vmem=48 << 20,
                name="pass_on",
            )
            terms = [pieces[0]] + [swap(p, "expert", b) for p, b in zip(pieces[1:], stage)]
        return terms

    def sum_of(terms, kinds):
        return call(
            functools.partial(sum_body, len(terms)),
            [shape((rows, half), k) for k in kinds],
            terms,
            name="sums",
            cost=(rows * width, 1 << 18),
        )

    far_terms, own_terms = scatter([p[0] for p in pieces]), scatter([p[1] for p in pieces])
    (far_part,) = sum_of(far_terms, (BF16,))
    far_y, far_xy = swap(far_part, "expert", far), swap_both(far_part, far, 2)
    own, x_part = sum_of(own_terms, (F32, BF16))
    near_x = swap(x_part, "tensor", 2)
    combined, squares = call(
        combine_body,
        [shape((rows, quarter), F32), shape((rows, LANES), F32)],
        (own, near_x, far_y, far_xy, residual),
        name="combine",
        cost=(rows * width, 1 << 18),
    )
    return call(
        functools.partial(finish_body, width),
        shape((rows, quarter), BF16),
        (combined, final_gain[None, :], squares, swap(squares, "tensor", 1)),
        name="finish",
        cost=(rows * width, 1 << 18),
    )


def solution(mesh):
    in_specs = (
        P("expert", None),
        P(),
        P(None, "tensor"),
        P("tensor", None, None),
        P("expert", "tensor", None, None),
        P("expert", None),
        P("expert"),
        P("expert"),
        P("tensor"),
        P("tensor", None),
        P(),
        P("expert", None),
        P("expert", None),
        P(),
        P("expert", None, "tensor"),
        P("expert", None, "tensor"),
        P("expert", "tensor", None),
        P("tensor"),
    )
    out_specs = P("expert", "tensor")
    return jax.shard_map(
        on_device, mesh=mesh, in_specs=in_specs, out_specs=out_specs, check_vma=False
    )
```
